32 devices in a mesh: pipe: 4 (over y, x), dp: 8 (over z, core).
Axes of the slice: x: 2, y: 2, z: 4, core: 2. Of those that a mesh axis runs over, the one named last changes fastest.
Arguments:
- activations: bfloat16 [4, 8, 134, 384], P('pipe', 'dp'), may hold values from -8 to 8
- cotangent: bfloat16 [4, 8, 134, 384], P('pipe', 'dp'), may hold values from -6 to 6
- att_qkv: bfloat16 [2, 384, 1152], replicated, may hold values from -0.3125 to 0.3125
- att_dw: bfloat16 [2, 25, 1152], replicated, may hold values from -1.25 to 1.25
- att_group: bfloat16 [2, 36, 32, 32], replicated, may hold values from -1 to 1
- att_proj: bfloat16 [2, 768, 384], replicated, may hold values from -0.21875 to 0.21875
- mb_inv: bfloat16 [2, 384, 1536], replicated, may hold values from -0.3125 to 0.3125
- mb_inv_bias: bfloat16 [2, 1536], replicated, may hold values from -2 to 2
- mb_dw: bfloat16 [2, 9, 1536], replicated, may hold values from -2 to 2
- mb_dw_bias: bfloat16 [2, 1536], replicated, may hold values from -2 to 2
- mb_point: bfloat16 [2, 1536, 384], replicated, may hold values from -0.15625 to 0.15625
- bn_gain: bfloat16 [4, 384], replicated, may hold values from 0.5 to 1.5
- bn_bias: bfloat16 [4, 384], replicated, may hold values from -2 to 2
Outputs:
- outputs: bfloat16 [4, 8, 134, 384], P('pipe', 'dp')
- input_grad: bfloat16 [4, 8, 134, 384], P('pipe', 'dp')
- grad_att_qkv: float32 [2, 384, 1152], P(None, 'pipe', 'dp')
- grad_att_dw: float32 [2, 25, 1152], replicated
- grad_att_group: float32 [2, 36, 32, 32], replicated
- grad_att_proj: float32 [2, 768, 384], P(None, 'dp', 'pipe')
- grad_mb_inv: float32 [2, 384, 1536], P(None, 'pipe', 'dp')
- grad_mb_inv_bias: float32 [2, 1536], replicated
- grad_mb_dw: float32 [2, 9, 1536], replicated
- grad_mb_dw_bias: float32 [2, 1536], replicated
- grad_mb_point: float32 [2, 1536, 384], P(None, 'dp', 'pipe')
- grad_bn_gain: float32 [4, 384], replicated
- grad_bn_bias: float32 [4, 384], replicated
The draws below stay inside these ranges and needn't reach their ends.
All inputs are finite; a program needn't handle non-finite values.
Results may differ from the reference program's by a relative error of at most 0.02.
Values may be sent and summed in bfloat16 or wider, within the bound.
A program may use at most 320 MiB of HBM per device.

```python
import jax
import jax.numpy as jnp
from jax import lax

D = 384
FF = 1536
HDIM = 32
IMAGES = 8
MICRO = 4


def draw_activations(key, part):
    key = jax.random.fold_in(key, 11)
    base_key, chan_key = jax.random.split(key)
    base_draw = jax.random.normal(base_key, (MICRO, IMAGES, 134, D), jnp.float32)
    image_scale = 0.6 + 1.2 * jnp.arange(IMAGES, dtype=jnp.float32) / max(IMAGES - 1, 1)
    channel_scale = jnp.exp(jax.random.uniform(chan_key, (D,), jnp.float32, -0.7, 0.7))
    return jnp.clip(base_draw * image_scale[None, :, None, None] * channel_scale, -8.0, 8.0).astype(jnp.bfloat16)


def shard_levels(stream_key, shape, cuts, least, largest):
    factor_of, own = 1.0, jax.random.fold_in(stream_key, 6)
    for position, shards_of in cuts:
        draws = jnp.exp(jax.random.uniform(jax.random.fold_in(own, position), (shards_of,), jnp.float32, least / len(cuts), largest / len(cuts)))
        factor_of = factor_of * jnp.repeat(draws, shape[position] // shards_of).reshape([-1 if axis == position else 1 for axis in range(len(shape))])
    return factor_of


def bell_draw(stream_key, shape, scale, limit, cuts=(), kind=jnp.bfloat16):
    result = scale * jax.random.normal(stream_key, shape, jnp.float32)
    if cuts:
        result = result * shard_levels(stream_key, shape, cuts, -0.22, 0.18)
    return jnp.clip(result, -limit, limit).astype(kind)


def setup_inputs(seed: int = 0) -> dict:
    seeds = jax.random.split(jax.random.key(seed), 14)
    activations = draw_activations(jax.random.fold_in(seeds[13], 71), 0)
    cotangent = bell_draw(seeds[1], (MICRO, IMAGES, 134, D), 1.0, 6.0, ((0, 4), (1, 8)))
    att_qkv = bell_draw(seeds[2], (2, D, 3 * D), D ** -0.5, 0.3125)
    att_dw = bell_draw(seeds[3], (2, 25, 3 * D), 25 ** -0.5, 1.25)
    att_group = bell_draw(seeds[4], (2, 3 * D // HDIM, HDIM, HDIM), HDIM ** -0.5, 1.0)
    att_proj = bell_draw(seeds[5], (2, 2 * D, D), (2 * D) ** -0.5, 0.21875)
    mb_inv = bell_draw(seeds[6], (2, D, FF), D ** -0.5, 0.3125)
    mb_inv_bias = bell_draw(seeds[7], (2, FF), 0.3, 2.0)
    mb_dw = bell_draw(seeds[8], (2, 9, FF), 9 ** -0.5, 2.0)
    mb_dw_bias = bell_draw(seeds[9], (2, FF), 0.3, 2.0)
    mb_point = bell_draw(seeds[10], (2, FF, D), FF ** -0.5, 0.15625)
    bn_gain = jnp.clip(1.0 + 0.1 * jax.random.normal(seeds[11], (4, D), jnp.float32), 0.5, 1.5).astype(jnp.bfloat16)
    bn_bias = bell_draw(seeds[12], (4, D), 0.3, 2.0)
    return {"activations": activations, "cotangent": cotangent, "att_qkv": att_qkv, "att_dw": att_dw, "att_group": att_group, "att_proj": att_proj, "mb_inv": mb_inv, "mb_inv_bias": mb_inv_bias, "mb_dw": mb_dw, "mb_dw_bias": mb_dw_bias, "mb_point": mb_point, "bn_gain": bn_gain, "bn_bias": bn_bias}


HIGH = lax.Precision.HIGHEST
EPS = 1e-05

@jax.custom_vjp
def low(v):
    return lax.optimization_barrier(v.astype(jnp.bfloat16)).astype(jnp.float32)

@jax.custom_vjp
def low_back(v):
    return v

def low_keep(v):
    return (low(v), None)

def low_pass(kept, grad):
    return (grad,)

def back_keep(v):
    return (v, None)

def back_low(kept, grad):
    return (low(grad),)
low.defvjp(low_keep, low_pass)
low_back.defvjp(back_keep, back_low)

def depthwise(tokens, kernel, reach):
    images = tokens.shape[0]
    channels = tokens.shape[-1]
    margin = reach // 2
    results = []
    for crop_count, crop_side, offset in ((2, 7, 0), (4, 3, 98)):
        crop_tokens = crop_count * crop_side * crop_side
        crop_cells = tokens[:, offset:offset + crop_tokens].reshape(images, crop_count, crop_side, crop_side, channels)
        padded = jnp.pad(crop_cells, ((0, 0), (0, 0), (margin, margin), (margin, margin), (0, 0)))
        summed = jnp.zeros(crop_cells.shape, jnp.float32)
        for row_step in range(reach):
            for col_step in range(reach):
                summed = summed + padded[:, :, row_step:row_step + crop_side, col_step:col_step + crop_side, :] * kernel[row_step * reach + col_step]
        results.append(summed.reshape(images, crop_tokens, channels))
    return jnp.concatenate(results, axis=1)

def crop_attention(queries, keys, values):
    kv_state = jnp.einsum('...lhi,...lhj->...hij', keys, values, precision=HIGH)
    key_total = lax.optimization_barrier(jnp.sum(keys, axis=-3))
    numerator = jnp.einsum('...lhi,...hij->...lhj', queries, kv_state, precision=HIGH)
    denominator = jnp.einsum('...lhi,...hi->...lh', queries, key_total, precision=HIGH)
    return numerator / denominator[..., None]

def attention_mix(joined, conv_kernel, group_weight):
    images = joined.shape[0]
    tokens_img = joined.shape[1]
    triple = joined.shape[2]
    head_size = group_weight.shape[-1]
    groups = group_weight.shape[0]
    spread = depthwise(joined, conv_kernel, 5)
    spread = jnp.einsum('abgi,gio->abgo', spread.reshape(images, tokens_img, groups, head_size), group_weight, precision=HIGH)
    heads = triple // (3 * head_size)
    scales = jnp.concatenate([joined.reshape(images, tokens_img, heads, 3 * head_size), spread.reshape(images, tokens_img, heads, 3 * head_size)], axis=2)
    queries = jax.nn.softplus(scales[..., :head_size])
    keys = jax.nn.softplus(scales[..., head_size:2 * head_size])
    values = scales[..., 2 * head_size:]
    outputs_crop = []
    for crop_count, crop_side, offset in ((2, 7, 0), (4, 3, 98)):
        crop_tokens = crop_count * crop_side * crop_side

        def by_crop(array_in):
            return array_in[:, offset:offset + crop_tokens].reshape(images, crop_count, crop_side * crop_side, 2 * heads, head_size)
        attended = crop_attention(by_crop(queries), by_crop(keys), by_crop(values))
        outputs_crop.append(attended.reshape(images, crop_tokens, 2 * heads * head_size))
    return jnp.concatenate(outputs_crop, axis=1)

def mb_mix(pre_act, conv_kernel, conv_bias):
    spread = depthwise(jax.nn.silu(pre_act), conv_kernel, 3) + conv_bias
    return jax.nn.silu(spread)

def attention_block(image_block, w_qkv, conv_kernel, group_weight, w_proj):
    flat_rows = image_block.reshape(-1, image_block.shape[-1])
    joined = low(low_back(jnp.dot(flat_rows, w_qkv, precision=HIGH, preferred_element_type=jnp.float32)))
    mixed = attention_mix(joined.reshape(image_block.shape[0], image_block.shape[1], -1), conv_kernel, group_weight)
    mixed = low(low_back(mixed.reshape(flat_rows.shape[0], -1)))
    return low_back(jnp.dot(mixed, w_proj, precision=HIGH, preferred_element_type=jnp.float32)).reshape(image_block.shape)

def expand_block(image_block, w_inv, bias_inv, conv_kernel, conv_bias, w_point):
    flat_rows = image_block.reshape(-1, image_block.shape[-1])
    pre_act = low_back(jnp.dot(flat_rows, w_inv, precision=HIGH, preferred_element_type=jnp.float32) + bias_inv)
    mixed = mb_mix(pre_act.reshape(image_block.shape[0], image_block.shape[1], -1), conv_kernel, conv_bias)
    mixed = low(low_back(mixed.reshape(flat_rows.shape[0], -1)))
    return low_back(jnp.dot(mixed, w_point, precision=HIGH, preferred_element_type=jnp.float32)).reshape(image_block.shape)

def run_segments(state, att_qkv, att_dw, att_group, att_proj, mb_inv, mb_inv_bias, mb_dw, mb_dw_bias, mb_point, bn_gain, bn_bias):
    images = state.shape[0]
    for segment_num in range(4):
        state = low_back(state)
        layer_num = segment_num // 2
        blocks = state.reshape(images // 8, 8, state.shape[1], state.shape[2])
        if segment_num % 2 == 0:
            branch = lax.map(lambda image_block: jax.checkpoint(attention_block)(image_block, att_qkv[layer_num], att_dw[layer_num], att_group[layer_num], att_proj[layer_num]), blocks)
        else:
            branch = lax.map(lambda image_block: jax.checkpoint(expand_block)(image_block, mb_inv[layer_num], mb_inv_bias[layer_num], mb_dw[layer_num], mb_dw_bias[layer_num], mb_point[layer_num]), blocks)
        branch = branch.reshape(-1, state.shape[2])
        col_mean = lax.optimization_barrier(jnp.mean(branch, axis=0))
        variance = lax.optimization_barrier(jnp.mean(branch * branch, axis=0)) - col_mean * col_mean
        normed = (branch - col_mean) * lax.rsqrt(variance + EPS)
        flat_rows = state.reshape(-1, state.shape[2])
        state = low((flat_rows + bn_gain[segment_num] * normed + bn_bias[segment_num]).reshape(state.shape))
    return state

def reference(activations, cotangent, att_qkv, att_dw, att_group, att_proj, mb_inv, mb_inv_bias, mb_dw, mb_dw_bias, mb_point, bn_gain, bn_bias):
    weights = tuple((weight.astype(jnp.float32) for weight in (att_qkv, att_dw, att_group, att_proj, mb_inv, mb_inv_bias, mb_dw, mb_dw_bias, mb_point, bn_gain, bn_bias)))

    def forward(inputs, *params):

        def one_batch(carry, batch_in):
            return (carry, run_segments(batch_in, *params))
        return lax.scan(one_batch, jnp.float32(0.0), inputs)[1]
    results, pullback = jax.vjp(forward, activations.astype(jnp.float32), *weights)
    grads = pullback(cotangent.astype(jnp.float32))
    return (results.astype(jnp.bfloat16), grads[0].astype(jnp.bfloat16), grads[1], grads[2], grads[3], grads[4], grads[5], grads[6], grads[7], grads[8], grads[9], grads[10], grads[11])
```

```python
import functools

import jax
import jax.numpy as jnp
from jax import lax
from jax.experimental import pallas as pl
from jax.experimental.pallas import tpu as pltpu
from jax.sharding import PartitionSpec as P

F32 = jnp.float32
BF = jnp.bfloat16
EPS = 1e-05
LANE = 128
SUB = 8
ROWS = 160
SMALL = 112
BLOCKS = ((0, 56), (56, 56), (112, 48))
HEADS = 4
UNITS = 6
NN = (((1,), (0,)), ((), ()))
NT = (((1,), (1,)), ((), ()))
TN = (((0,), (0,)), ((), ()))


def mm(a, b, dims=NN):
    return lax.dot_general(a, b, dims, preferred_element_type=F32)


def iota(shape, dim):
    return lax.broadcasted_iota(jnp.int32, shape, dim)


def lanes(j):
    if isinstance(j, int):
        return slice(j * LANE, (j + 1) * LANE)
    return pl.ds(pl.multiple_of(j * LANE, LANE), LANE)


def spread_matrix(tokens):
    row, col = iota((ROWS, tokens), 0), iota((ROWS, tokens), 1)
    crop = (row >= 56).astype(jnp.int32)
    inner = row - 56 * crop
    big = crop * 49 + (inner >> 3) * 7 + (inner & 7)
    small_row = row - SMALL
    pair = (small_row >= 24).astype(jnp.int32)
    inner = small_row - 24 * pair
    small = 98 + (pair * 2 + ((inner & 7) >> 2)) * 9 + (inner >> 3) * 3 + (inner & 3)
    is_big = row < SMALL
    valid = jnp.where(is_big, row & 7, (row & 3) + 4) < 7
    hit = (jnp.where(is_big, big, small) == col) & valid
    return jnp.where(hit, 1.0, 0.0).astype(BF)


def split_matrix(width):
    row, col = iota((width, width), 0), iota((width, width), 1)
    head = (row >= 96).astype(jnp.int32) + (row >= 192).astype(jnp.int32) + (row >= 288).astype(jnp.int32)
    rest = row - 96 * head
    part = (rest >= 32).astype(jnp.int32) + (rest >= 64).astype(jnp.int32)
    target = part * 128 + head * 32 + (rest - 32 * part)
    return jnp.where(target == col, 1.0, 0.0).astype(BF)


def row_mask(width=LANE):
    row = iota((ROWS, width), 0)
    valid = jnp.where(row < SMALL, row & 7, (row & 3) + 4) < 7
    return jnp.where(valid, 1.0, 0.0)


def crop_mask(rows, columns):
    row, col = iota((rows, columns), 0), iota((rows, columns), 1)
    for step in (3, 2, 1):
        col = jnp.where(col >= rows * step, col - rows * step, col)
    row_crop = (row >= 24).astype(jnp.int32) * 2 + ((row & 7) >> 2)
    col_crop = (col >= 24).astype(jnp.int32) * 2 + ((col & 7) >> 2)
    return jnp.where(row_crop == col_crop, 1.0, 0.0)


def head_masks():
    lane = iota((1, LANE), 1)
    return [jnp.where((lane >= 32 * h) & (lane < 32 * h + 32), 1.0, 0.0) for h in range(HEADS)]


def stacked(value, masks):
    return jnp.concatenate([value * mask for mask in masks], axis=0).astype(BF)


def shifted(tokens, step):
    if step == 0:
        return tokens
    moved = pltpu.roll(tokens, (-step) % SUB, 1)
    if abs(step) == 1:
        return moved
    at = iota((1, SUB, LANE), 1)
    if tokens.shape[0] > 6:
        wrong = (at == 0) if step < 0 else (at == 6)
    else:
        wrong = ((at & 3) == 0) if step < 0 else ((at & 3) == 2)
    return jnp.where(wrong, 0.0, moved)


def tap_pairs(side, step):
    return range(max(0, -step), min(side, side - step))


def crops(tokens):
    return ((tokens[:14], 7), (tokens[14:], 3))


def depthwise(tokens, taps, reach, flip=False):
    margin = reach // 2
    parts = []
    for cells, side in crops(tokens):
        sums = [None] * side
        for dj in range(-margin, margin + 1):
            moved = shifted(cells, dj).reshape(2, side, SUB, LANE)
            for di in range(-margin, margin + 1):
                tap = (margin - di) * reach + margin - dj if flip else (margin + di) * reach + margin + dj
                weight = taps[tap : tap + 1, :].reshape(1, 1, LANE)
                for a in tap_pairs(side, di):
                    term = moved[:, a + di] * weight
                    sums[a] = term if sums[a] is None else sums[a] + term
        parts.append(jnp.stack(sums, axis=1).reshape(2 * side, SUB, LANE))
    return jnp.concatenate(parts, axis=0)


def depthwise_taps(tokens, grads, reach):
    margin = reach // 2
    totals = {}
    for (cells, side), (grad_cells, _) in zip(crops(tokens), crops(grads)):
        grad_cells = grad_cells.reshape(2, side, SUB, LANE)
        for dj in range(-margin, margin + 1):
            moved = shifted(cells, dj).reshape(2, side, SUB, LANE)
            for di in range(-margin, margin + 1):
                tap = (margin + di) * reach + margin + dj
                total = totals.get(tap)
                for a in tap_pairs(side, di):
                    term = moved[:, a + di] * grad_cells[:, a]
                    total = term if total is None else total + term
                if total is not None:
                    totals[tap] = total
    return [jnp.sum(jnp.sum(totals[tap], axis=0), axis=0, keepdims=True) for tap in range(reach * reach)]


def softplus(x):
    small = jnp.exp(-jnp.abs(x))
    return jnp.maximum(x, 0.0) + jnp.where(small < 1e-3, small * (1.0 - 0.5 * small), jnp.log(1.0 + small))


def silu_parts(x):
    gate = 0.5 * jnp.tanh(0.5 * x) + 0.5
    value = x * gate
    return value, gate + value * (1.0 - gate)


def column_sum(value):
    return jnp.sum(value, axis=0, keepdims=True)


def kernel(
    n_dp,
    x_ref, ct_ref, qkv_ref, dw_ref, group_ref, proj_ref, inv_ref, ibias_ref, mdw_ref, mbias_ref, point_ref,
    gain_ref, shift_ref,
    out_ref, xgrad_ref, gqkv_ref, gproj_ref, ginv_ref, gpoint_ref, sga_ref, sgm_ref,
    perm, wp, blocks_bd, dwp, rmask, smask, hid, hidf, normed, mixo, rden, tvals, joined, s0, dvals, gmix,
    pre_u, pre_d, act, act_d, mid, gact, branch, gnow, stats, exbuf, send_sem, recv_sem,
):
    me = lax.axis_index("dp")
    layers = qkv_ref.shape[0]
    width = x_ref.shape[1]
    expanded = inv_ref.shape[2]
    total_rows = float(x_ref.shape[0] * n_dp)
    wide = width // LANE
    stages = 2 * layers

    barrier = pltpu.get_barrier_semaphore()

    def greet(k, carry):
        pl.semaphore_signal(barrier, inc=1, device_id={"dp": lax.rem(me + k, n_dp)})
        return carry

    lax.fori_loop(1, n_dp, greet, 0)

    masks = head_masks()
    perm[...] = split_matrix(width)
    rmask[...] = row_mask()
    smask[...] = crop_mask(48, 192)

    block_lane, block_row = iota((LANE, LANE), 1), iota((LANE, LANE), 0)
    on_diag = (block_lane >> 5) == (block_row >> 5)
    tile = jnp.where((iota((32, LANE), 1) & 31) == iota((32, LANE), 0), 1.0, 0.0).astype(BF)
    for l in range(layers):
        for c in range(wide):
            cut = slice(c * width, (c + 1) * width)
            w_split = mm(qkv_ref[l, :, cut], perm[...]).astype(BF)
            k_split = mm(dw_ref[l, :, cut], perm[...])
            for part in range(3):
                target = lanes(part * wide + c)
                wp[l, :, target] = w_split[:, lanes(part)]
                dwp[l, 0:25, target] = k_split[:, lanes(part)]
                rows = jnp.concatenate([group_ref[l, 3 * (4 * c + i) + part] for i in range(HEADS)], axis=0)
                full = jnp.where(on_diag, mm(rows, tile), 0.0)
                blocks_bd[l, part * wide + c] = full.astype(BF)

    spread = spread_matrix(x_ref.shape[0])
    hid[0] = mm(spread, x_ref[...]).astype(BF)
    gnow[...] = mm(spread, ct_ref[...])
    pl.semaphore_wait(barrier, n_dp - 1)

    def exchange(e, vectors):
        count = len(vectors) * wide
        rows = -(-count // SUB) * SUB
        for i, vector in enumerate(vectors):
            for j in range(wide):
                at = i * wide + j
                exbuf[e, me, at : at + 1, :] = vector[:, lanes(j)]

        def send(k, carry):
            pltpu.make_async_remote_copy(
                src_ref=exbuf.at[e, me, 0:rows],
                dst_ref=exbuf.at[e, me, 0:rows],
                send_sem=send_sem.at[e],
                recv_sem=recv_sem.at[e],
                device_id={"dp": lax.rem(me + k, n_dp)},
            ).start()
            return carry

        lax.fori_loop(1, n_dp, send, 0)
        whole = exbuf.at[e, 0 : n_dp - 1, 0:rows]
        pltpu.make_async_copy(whole, whole, recv_sem.at[e]).wait()
        total = exbuf[e, 0, 0:rows]
        for d in range(1, n_dp):
            total = total + exbuf[e, d, 0:rows]
        pltpu.make_async_copy(whole, whole, send_sem.at[e]).wait()
        return [
            jnp.concatenate([total[i * wide + j : i * wide + j + 1] for j in range(wide)], axis=1)
            for i in range(len(vectors))
        ]

    def attention_forward(l, s):
        joined[l] = mm(hid[s], wp[l]).astype(BF).astype(F32)

        def chunk(j, carry):
            at = lanes(j)
            cells = joined[l, :, at]
            conv = depthwise(cells.reshape(20, SUB, LANE), dwp[l, :, at], 5).reshape(ROWS, LANE)
            conv = (conv * rmask[...]).astype(BF)
            s0[l, :, at] = conv
            linear = mm(conv, blocks_bd[l, j])
            part = j // wide
            keep = rmask[...]
            for source, value in ((0, cells), (1, linear)):
                soft = softplus(value)
                soft = jnp.where(part == 1, soft * keep, soft)
                tvals[l, :, lanes(part * UNITS + source * wide + j % wide)] = jnp.where(part == 2, value, soft)
            return carry

        lax.fori_loop(0, 3 * wide, chunk, 0)

        def unit(u, carry):
            for start, size in BLOCKS:
                rows = slice(start, start + size)
                query = tvals[l, rows, lanes(u)]
                key = tvals[l, rows, lanes(u + UNITS)]
                value = tvals[l, rows, lanes(u + 2 * UNITS)]
                scores = mm(query.astype(BF), stacked(key, masks), NT)
                if start == SMALL:
                    scores = scores * smask[...]
                both = jnp.concatenate(
                    [stacked(value, masks), stacked(jnp.ones_like(value), masks)], axis=1
                )
                sums = mm(scores.astype(BF), both)
                inverse = 1.0 / sums[:, LANE:]
                rden[l, rows, lanes(u)] = inverse
                mixo[l, rows, lanes(u)] = sums[:, :LANE] * inverse
            return carry

        lax.fori_loop(0, UNITS, unit, 0)
        branch[...] = mm(mixo[l].astype(BF), proj_ref[l])

    def expand_forward(l, s):
        pre_u[l] = mm(hid[s], inv_ref[l])

        def chunk(j, carry):
            at = lanes(j)
            pre = pre_u[l, :, at] + ibias_ref[l, :, at].astype(F32)
            value, slope = silu_parts(pre)
            value = value * rmask[...]
            pre_u[l, :, at] = value
            pre_d[l, :, at] = slope * rmask[...]
            taps = mdw_ref[l, :, at].astype(F32)
            conv = depthwise(value.reshape(20, SUB, LANE), taps, 3).reshape(ROWS, LANE)
            out, out_slope = silu_parts(conv + mbias_ref[l, :, at].astype(F32))
            act[l, :, at] = (out * rmask[...]).astype(BF)
            act_d[l, :, at] = out_slope
            return carry

        lax.fori_loop(0, expanded // LANE, chunk, 0)
        branch[...] = mm(act[l], point_ref[l])

    for s in range(stages):
        l = s // 2
        if s % 2 == 0:
            attention_forward(l, s)
        else:
            expand_forward(l, s)
        keep = rmask[...]
        for j in range(wide):
            branch[:, lanes(j)] = branch[:, lanes(j)] * keep
        value = branch[...]
        vectors = [column_sum(value), column_sum(value * value)]
        mean, square = exchange(s, vectors)
        mean = mean * (1.0 / total_rows)
        square = square * (1.0 / total_rows)
        scale = lax.rsqrt(square - mean * mean + EPS)
        stats[s : s + 1, :] = scale
        norm = (branch[...] - mean) * scale
        gain = gain_ref[s].astype(F32)
        shift = shift_ref[s].astype(F32)
        after = hid[s].astype(F32) + gain * norm + shift
        for j in range(wide):
            normed[s, :, lanes(j)] = norm[:, lanes(j)] * keep
            hid[s + 1, :, lanes(j)] = (after[:, lanes(j)] * keep).astype(BF)

    out_ref[...] = mm(spread, hid[stages], TN).astype(BF)

    def attention_backward(l, s, grad_branch):
        gmix[...] = mm(grad_branch, proj_ref[l], NT).astype(BF).astype(F32)

        def unit(u, carry):
            for start, size in BLOCKS:
                rows = slice(start, start + size)
                query = tvals[l, rows, lanes(u)]
                key = tvals[l, rows, lanes(u + UNITS)]
                value = tvals[l, rows, lanes(u + 2 * UNITS)]
                down = gmix[rows, lanes(u)] * rden[l, rows, lanes(u)]
                level = -down * mixo[l, rows, lanes(u)]
                ones = jnp.ones_like(value)
                key_stack, query_stack, down_stack = (
                    stacked(key, masks),
                    stacked(query, masks),
                    stacked(down, masks),
                )
                grad_scores = mm(
                    jnp.concatenate([down, level], axis=1).astype(BF),
                    jnp.concatenate([stacked(value, masks), stacked(ones, masks)], axis=1),
                    NT,
                )
                grad_scores_t = mm(
                    jnp.concatenate([value, ones], axis=1).astype(BF),
                    jnp.concatenate([down_stack, stacked(level, masks)], axis=1),
                    NT,
                )
                scores_t = mm(key.astype(BF), query_stack, NT)
                if start == SMALL:
                    inside = smask[...]
                    grad_scores = grad_scores * inside
                    grad_scores_t = grad_scores_t * inside
                    scores_t = scores_t * inside
                grad_query = mm(grad_scores.astype(BF), key_stack)
                grad_key = mm(grad_scores_t.astype(BF), query_stack)
                grad_value = mm(scores_t.astype(BF), down_stack)
                dvals[rows, lanes(u)] = grad_query * (1.0 - jnp.exp(-query))
                dvals[rows, lanes(u + UNITS)] = grad_key * (1.0 - jnp.exp(-key))
                dvals[rows, lanes(u + 2 * UNITS)] = grad_value
            return carry

        lax.fori_loop(0, UNITS, unit, 0)

        def chunk(j, carry):
            at = lanes(j)
            part = j // wide
            slot = part * UNITS + j % wide
            grad_spread = dvals[:, lanes(slot + wide)].astype(BF)
            block = jnp.where(on_diag, mm(s0[l, :, at], grad_spread, TN), 0.0)
            sga_ref[l, 32:64, at] = block[0:32] + block[32:64] + block[64:96] + block[96:128]
            grad_conv = mm(grad_spread, blocks_bd[l, j], NT).reshape(20, SUB, LANE)
            cells = joined[l, :, at].reshape(20, SUB, LANE)
            for tap, row in enumerate(depthwise_taps(cells, grad_conv, 5)):
                sga_ref[l, tap : tap + 1, at] = row
            back = depthwise(grad_conv, dwp[l, :, at], 5, flip=True).reshape(ROWS, LANE)
            mid[:, at] = (dvals[:, lanes(slot)] + back * rmask[...]).astype(BF)
            return carry

        lax.fori_loop(0, 3 * wide, chunk, 0)
        grad_hidden = mm(mid[:, : 3 * width], wp[l], NT)
        for c in range(wide):
            piece = jnp.concatenate([mid[:, lanes(part * wide + c)] for part in range(3)], axis=1)
            natural = mm(piece, perm[...], NT).astype(BF)
            gqkv_ref[l, :, c * width : (c + 1) * width] = mm(hid[s], natural, TN).astype(BF)
        gproj_ref[l] = mm(grad_branch, mixo[l].astype(BF), TN).astype(BF)
        return grad_hidden

    def expand_backward(l, s, grad_branch):
        gact[...] = mm(grad_branch, point_ref[l], NT).astype(BF).astype(F32)

        def chunk(j, carry):
            at = lanes(j)
            grad_conv = gact[:, at] * act_d[l, :, at]
            sgm_ref[l, 9:10, at] = column_sum(grad_conv)
            cells = pre_u[l, :, at].reshape(20, SUB, LANE)
            grad_conv = grad_conv.reshape(20, SUB, LANE)
            for tap, row in enumerate(depthwise_taps(cells, grad_conv, 3)):
                sgm_ref[l, tap : tap + 1, at] = row
            taps = mdw_ref[l, :, at].astype(F32)
            back = depthwise(grad_conv, taps, 3, flip=True).reshape(ROWS, LANE)
            grad_pre = (back * pre_d[l, :, at]).astype(BF)
            mid[:, at] = grad_pre
            sgm_ref[l, 10:11, at] = column_sum(grad_pre.astype(F32))
            return carry

        lax.fori_loop(0, expanded // LANE, chunk, 0)
        grad_hidden = mm(mid[...], inv_ref[l], NT)
        ginv_ref[l] = mm(hid[s], mid[...], TN).astype(BF)
        gpoint_ref[l] = mm(grad_branch, act[l], TN).astype(BF)
        return grad_hidden

    for s in range(stages - 1, -1, -1):
        l = s // 2
        keep = rmask[...]
        upstream = gnow[...]
        norm = normed[s]
        local_cross, local_sum = column_sum(upstream * norm), column_sum(upstream)
        if s % 2 == 0:
            sga_ref[l, 25:26, 0:width] = local_cross
            sga_ref[l, 25:26, width : 2 * width] = local_sum
        else:
            sgm_ref[l, 11:12, 0:width] = local_cross
            sgm_ref[l, 11:12, width : 2 * width] = local_sum
        cross, total = exchange(stages + s, [local_cross, local_sum])
        gain = gain_ref[s].astype(F32)
        scale = stats[s : s + 1, :]
        cross = cross * (1.0 / total_rows)
        total = total * (1.0 / total_rows)
        grad_branch = (scale * gain) * (gnow[...] - total - normed[s] * cross)
        grad_branch = jnp.concatenate(
            [grad_branch[:, lanes(j)] * keep for j in range(wide)], axis=1
        ).astype(BF)
        back = attention_backward if s % 2 == 0 else expand_backward
        grad_hidden = back(l, s, grad_branch)
        gnow[...] = (gnow[...] + grad_hidden).astype(BF).astype(F32)

    xgrad_ref[...] = mm(spread, gnow[...].astype(BF), TN).astype(BF)


def body(
    activations, cotangent, att_qkv, att_dw, att_group, att_proj, mb_inv, mb_inv_bias, mb_dw, mb_dw_bias, mb_point,
    bn_gain, bn_bias,
):
    n_dp = lax.axis_size("dp")
    layers, width, joined_width = att_qkv.shape
    mixed_width = att_proj.shape[1]
    expanded = mb_inv.shape[2]
    tokens = activations.shape[2]
    stages = 2 * layers
    vmem = pl.BlockSpec(memory_space=pltpu.VMEM)
    results = pl.pallas_call(
        functools.partial(kernel, n_dp),
        out_shape=(
            jax.ShapeDtypeStruct((tokens, width), BF),
            jax.ShapeDtypeStruct((tokens, width), BF),
            jax.ShapeDtypeStruct((layers, width, joined_width), BF),
            jax.ShapeDtypeStruct((layers, width, mixed_width), BF),
            jax.ShapeDtypeStruct((layers, width, expanded), BF),
            jax.ShapeDtypeStruct((layers, width, expanded), BF),
            jax.ShapeDtypeStruct((layers, 64, joined_width), F32),
            jax.ShapeDtypeStruct((layers, 16, expanded), F32),
        ),
        in_specs=[vmem] * 13,
        out_specs=(vmem,) * 8,
        scratch_shapes=[
            pltpu.VMEM((width, width), BF),
            pltpu.VMEM((layers, width, joined_width), BF),
            pltpu.VMEM((layers, joined_width // LANE, LANE, LANE), BF),
            pltpu.VMEM((layers, 32, joined_width), F32),
            pltpu.VMEM((ROWS, LANE), F32),
            pltpu.VMEM((48, 192), F32),
            pltpu.VMEM((stages + 1, ROWS, width), BF),
            pltpu.VMEM((8, LANE), F32),
            pltpu.VMEM((stages, ROWS, width), F32),
            pltpu.VMEM((layers, ROWS, mixed_width), F32),
            pltpu.VMEM((layers, ROWS, mixed_width), F32),
            pltpu.VMEM((layers, ROWS, 3 * mixed_width), F32),
            pltpu.VMEM((layers, ROWS, joined_width), F32),
            pltpu.VMEM((layers, ROWS, joined_width), BF),
            pltpu.VMEM((ROWS, 3 * mixed_width), F32),
            pltpu.VMEM((ROWS, mixed_width), F32),
            pltpu.VMEM((layers, ROWS, expanded), F32),
            pltpu.VMEM((layers, ROWS, expanded), F32),
            pltpu.VMEM((layers, ROWS, expanded), BF),
            pltpu.VMEM((layers, ROWS, expanded), F32),
            pltpu.VMEM((ROWS, expanded), BF),
            pltpu.VMEM((ROWS, expanded), F32),
            pltpu.VMEM((ROWS, width), F32),
            pltpu.VMEM((ROWS, width), F32),
            pltpu.VMEM((8, width), F32),
            pltpu.VMEM((2 * stages, n_dp, SUB, LANE), F32),
            pltpu.SemaphoreType.DMA((2 * stages,)),
            pltpu.SemaphoreType.DMA((2 * stages,)),
        ],
        compiler_params=pltpu.CompilerParams(
            collective_id=0, has_side_effects=True, vmem_limit_bytes=60 * 1024 * 1024
        ),
    )(
        activations.reshape(tokens, width),
        cotangent.reshape(tokens, width),
        att_qkv,
        att_dw,
        att_group,
        att_proj,
        mb_inv,
        mb_inv_bias.reshape(layers, 1, expanded),
        mb_dw,
        mb_dw_bias.reshape(layers, 1, expanded),
        mb_point,
        bn_gain.reshape(stages, 1, width),
        bn_bias.reshape(stages, 1, width),
    )
    out, xgrad, gqkv, gproj, ginv, gpoint, sga, sgm = results

    def owned(grad):
        summed = lax.psum_scatter(grad.astype(F32), "dp", scatter_dimension=2, tiled=True)
        return lax.psum_scatter(summed.astype(BF), "pipe", scatter_dimension=1, tiled=True).astype(F32)

    sga, sgm = lax.psum((sga, sgm), ("pipe", "dp"))
    heads = width // 32
    natural = sga.reshape(layers, 64, 3, heads, 32).transpose(0, 1, 3, 2, 4)
    grad_dw = natural[:, :25].reshape(layers, 25, joined_width)
    grad_group = natural[:, 32:].transpose(0, 2, 3, 1, 4).reshape(layers, 3 * heads, 32, 32)
    gains = jnp.stack([sga[:, 25, : 2 * width], sgm[:, 11, : 2 * width]], axis=1).reshape(stages, 2 * width)
    return (
        out.reshape(activations.shape),
        xgrad.reshape(activations.shape),
        owned(gqkv),
        grad_dw,
        grad_group,
        owned(gproj).transpose(0, 2, 1),
        owned(ginv),
        sgm[:, 10],
        sgm[:, :9],
        sgm[:, 9],
        owned(gpoint).transpose(0, 2, 1),
        gains[:, :width],
        gains[:, width:],
    )


def solution(mesh):
    placed = (P("pipe", "dp", None, None), P("pipe", "dp", None, None)) + (P(),) * 11
    return jax.shard_map(
        body,
        mesh=mesh,
        in_specs=placed,
        out_specs=(
            P("pipe", "dp", None, None),
            P("pipe", "dp", None, None),
            P(None, "pipe", "dp"),
            P(),
            P(),
            P(None, "dp", "pipe"),
            P(None, "pipe", "dp"),
            P(),
            P(),
            P(),
            P(None, "dp", "pipe"),
            P(),
            P(),
        ),
        check_vma=False,
    )
```

```python
import functools

import jax
import jax.numpy as jnp
from jax import lax
from jax.experimental import pallas as pl
from jax.experimental.pallas import tpu as pltpu
from jax.sharding import PartitionSpec as P

F32 = jnp.float32
BF = jnp.bfloat16
EPS = 1e-05
LANE = 128
SUB = 8
ROWS = 160
SMALL = 112
BLOCKS = ((0, 56), (56, 56), (112, 48))
HEADS = 4
UNITS = 6
NN = (((1,), (0,)), ((), ()))
NT = (((1,), (1,)), ((), ()))
TN = (((0,), (0,)), ((), ()))


def mm(a, b, dims=NN):
    return lax.dot_general(a, b, dims, preferred_element_type=F32)


def iota(shape, dim):
    return lax.broadcasted_iota(jnp.int32, shape, dim)


def lanes(j):
    if isinstance(j, int):
        return slice(j * LANE, (j + 1) * LANE)
    return pl.ds(pl.multiple_of(j * LANE, LANE), LANE)


def spread_matrix(tokens):
    row, col = iota((ROWS, tokens), 0), iota((ROWS, tokens), 1)
    crop = (row >= 56).astype(jnp.int32)
    inner = row - 56 * crop
    big = crop * 49 + (inner >> 3) * 7 + (inner & 7)
    small_row = row - SMALL
    pair = (small_row >= 24).astype(jnp.int32)
    inner = small_row - 24 * pair
    small = 98 + (pair * 2 + ((inner & 7) >> 2)) * 9 + (inner >> 3) * 3 + (inner & 3)
    is_big = row < SMALL
    valid = jnp.where(is_big, row & 7, (row & 3) + 4) < 7
    hit = (jnp.where(is_big, big, small) == col) & valid
    return jnp.where(hit, 1.0, 0.0).astype(BF)


def split_matrix(width):
    row, col = iota((width, width), 0), iota((width, width), 1)
    head = (row >= 96).astype(jnp.int32) + (row >= 192).astype(jnp.int32) + (row >= 288).astype(jnp.int32)
    rest = row - 96 * head
    part = (rest >= 32).astype(jnp.int32) + (rest >= 64).astype(jnp.int32)
    target = part * 128 + head * 32 + (rest - 32 * part)
    return jnp.where(target == col, 1.0, 0.0).astype(BF)


def row_mask(width=LANE):
    row = iota((ROWS, width), 0)
    valid = jnp.where(row < SMALL, row & 7, (row & 3) + 4) < 7
    return jnp.where(valid, 1.0, 0.0)


def crop_mask(rows, columns):
    row, col = iota((rows, columns), 0), iota((rows, columns), 1)
    for step in (3, 2, 1):
        col = jnp.where(col >= rows * step, col - rows * step, col)
    row_crop = (row >= 24).astype(jnp.int32) * 2 + ((row & 7) >> 2)
    col_crop = (col >= 24).astype(jnp.int32) * 2 + ((col & 7) >> 2)
    return jnp.where(row_crop == col_crop, 1.0, 0.0)


def head_masks():
    lane = iota((1, LANE), 1)
    return [jnp.where((lane >= 32 * h) & (lane < 32 * h + 32), 1.0, 0.0) for h in range(HEADS)]


def stacked(value, masks):
    return jnp.concatenate([value * mask for mask in masks], axis=0).astype(BF)


def shifted(tokens, step):
    if step == 0:
        return tokens
    moved = pltpu.roll(tokens, (-step) % SUB, 1)
    if abs(step) == 1:
        return moved
    at = iota((1, SUB, LANE), 1)
    if tokens.shape[0] > 6:
        wrong = (at == 0) if step < 0 else (at == 6)
    else:
        wrong = ((at & 3) == 0) if step < 0 else ((at & 3) == 2)
    return jnp.where(wrong, 0.0, moved)


def tap_pairs(side, step):
    return range(max(0, -step), min(side, side - step))


def crops(tokens):
    return ((tokens[:14], 7), (tokens[14:], 3))


def depthwise(tokens, taps, reach, flip=False):
    margin = reach // 2
    parts = []
    for cells, side in crops(tokens):
        sums = [None] * side
        for dj in range(-margin, margin + 1):
            moved = shifted(cells, dj).reshape(2, side, SUB, LANE)
            for di in range(-margin, margin + 1):
                tap = (margin - di) * reach + margin - dj if flip else (margin + di) * reach + margin + dj
                weight = taps[tap : tap + 1, :].reshape(1, 1, LANE)
                for a in tap_pairs(side, di):
                    term = moved[:, a + di] * weight
                    sums[a] = term if sums[a] is None else sums[a] + term
        parts.append(jnp.stack(sums, axis=1).reshape(2 * side, SUB, LANE))
    return jnp.concatenate(parts, axis=0)


def depthwise_taps(tokens, grads, reach):
    margin = reach // 2
    totals = {}
    for (cells, side), (grad_cells, _) in zip(crops(tokens), crops(grads)):
        grad_cells = grad_cells.reshape(2, side, SUB, LANE)
        for dj in range(-margin, margin + 1):
            moved = shifted(cells, dj).reshape(2, side, SUB, LANE)
            for di in range(-margin, margin + 1):
                tap = (margin + di) * reach + margin + dj
                total = totals.get(tap)
                for a in tap_pairs(side, di):
                    term = moved[:, a + di] * grad_cells[:, a]
                    total = term if total is None else total + term
                if total is not None:
                    totals[tap] = total
    return [jnp.sum(jnp.sum(totals[tap], axis=0), axis=0, keepdims=True) for tap in range(reach * reach)]


def softplus(x):
    small = jnp.exp(-jnp.abs(x))
    return jnp.maximum(x, 0.0) + jnp.where(small < 1e-3, small * (1.0 - 0.5 * small), jnp.log(1.0 + small))


def silu_parts(x):
    gate = 0.5 * jnp.tanh(0.5 * x) + 0.5
    value = x * gate
    return value, gate + value * (1.0 - gate)


def column_sum(value):
    return jnp.sum(value, axis=0, keepdims=True)


def wait_bytes(ref, sem):
    pltpu.make_async_copy(ref, ref, sem).wait()


class Reduction:
    def __init__(self, place, own, pair, first, second, send_sem, recv_sem, base):
        self.place, self.own, self.pair, self.first, self.second = place, own, pair, first, second
        self.send_sem, self.recv_sem, self.base = send_sem, recv_sem, base
        self.copies = []

    def copy(self, source, target, kind, pipe, dp):
        made = pltpu.make_async_remote_copy(
            src_ref=source,
            dst_ref=target,
            send_sem=self.send_sem.at[self.base + kind],
            recv_sem=self.recv_sem.at[self.base + kind],
            device_id={"pipe": pipe, "dp": dp},
        )
        made.start()
        self.copies.append(made)
        return made

    def start(self):
        at = self.place
        self.arriving = [self.copy(self.own.at[1 - at.core], self.pair, 0, at.pipe, at.dp + 1 - 2 * at.core)]

    def step1(self):
        at = self.place
        self.arriving[0].wait_recv()

        def add(q, carry):
            self.own[at.core, q] = self.own[at.core, q] + self.pair[q]
            return carry

        lax.fori_loop(0, self.pair.shape[0], add, 0)
        peer = at.pipe + (1 + at.core) * (1 - 2 * at.bit1)
        self.arriving = [
            self.copy(self.own.at[at.core, at.slab(1 - at.bit1, bit)], self.first.at[bit], 1 + bit, peer, at.dp)
            for bit in range(2)
        ]

    def step2(self):
        at = self.place
        for bit, arrived in enumerate(self.arriving):
            arrived.wait_recv()
            slab = at.slab(at.bit1, bit)
            self.own[at.core, slab] = self.own[at.core, slab] + self.first[bit]
        peer = at.pipe + (2 - at.core) * (1 - 2 * at.bit2)
        self.arriving = [
            self.copy(self.own.at[at.core, at.slab(at.bit1, 1 - at.bit2)], self.second, 3, peer, at.dp)
        ]

    def part(self):
        self.arriving[0].wait_recv()
        return self.own[self.place.core, self.place.pipe].astype(F32) + self.second[...].astype(F32)

    def drain(self):
        for made in self.copies:
            made.wait_send()


class Place:
    def __init__(self):
        self.pipe, self.dp = lax.axis_index("pipe"), lax.axis_index("dp")
        self.core = lax.rem(self.dp, 2)
        low, high = lax.rem(self.pipe, 2), self.pipe // 2
        self.bit1 = low * (1 - self.core) + high * self.core
        self.bit2 = high * (1 - self.core) + low * self.core

    def slab(self, bit1, bit2):
        return bit1 * (1 + self.core) + bit2 * (2 - self.core)


class Projection(Reduction):
    def __init__(self, *args):
        *rest, self.outgoing, self.landed, self.whole, self.result = args
        super().__init__(*rest)

    def step3(self):
        at = self.place
        n_dp, rows, padded = self.outgoing.shape
        columns = self.own.shape[3]
        share = columns // n_dp
        cover = min(padded + LANE, columns)
        self.whole[:, 0:columns] = self.part()

        def cut(d, carry):
            offset = d * share
            base = jnp.minimum(offset // LANE, (columns - cover) // LANE) * LANE
            piece = self.whole[:, pl.ds(pl.multiple_of(base, LANE), cover)]
            piece = pltpu.roll(piece, lax.rem(cover - (offset - base), cover), 1)
            self.outgoing[d] = piece[:, 0:padded].astype(BF)
            return carry

        lax.fori_loop(0, n_dp, cut, 0)

        def send(k, carry):
            peer = lax.rem(at.dp + k, n_dp)
            pltpu.make_async_remote_copy(
                src_ref=self.outgoing.at[peer],
                dst_ref=self.landed.at[at.dp],
                send_sem=self.send_sem.at[self.base + 4],
                recv_sem=self.recv_sem.at[self.base + 4],
                device_id={"dp": peer},
            ).start()
            return carry

        lax.fori_loop(1, n_dp, send, 0)
        self.landed[at.dp] = self.outgoing[at.dp]

    def finish(self):
        n_dp, rows, _ = self.outgoing.shape
        wait_bytes(self.landed.at[0 : n_dp - 1], self.recv_sem.at[self.base + 4])
        for core in range(2):
            total = self.landed[core].astype(F32)
            for d in range(core + 2, n_dp, 2):
                total = total + self.landed[d].astype(F32)
            self.result[core * rows : (core + 1) * rows, :] = total
        wait_bytes(self.outgoing.at[0 : n_dp - 1], self.send_sem.at[self.base + 4])


class Small(Reduction):
    def __init__(self, *args):
        *rest, self.along, self.everywhere, self.result = args
        super().__init__(*rest)

    def step3(self):
        at = self.place
        pairs = self.along.shape[0]
        mine = at.dp // 2
        self.along[mine] = self.part()

        def send(k, carry):
            peer = lax.rem(mine + k, pairs)
            pltpu.make_async_remote_copy(
                src_ref=self.along.at[mine],
                dst_ref=self.along.at[mine],
                send_sem=self.send_sem.at[self.base + 4],
                recv_sem=self.recv_sem.at[self.base + 4],
                device_id={"dp": peer * 2 + at.core},
            ).start()
            return carry

        lax.fori_loop(1, pairs, send, 0)

    def step4(self):
        at = self.place
        pairs = self.along.shape[0]
        wait_bytes(self.along.at[0 : pairs - 1], self.recv_sem.at[self.base + 4])
        total = self.along[0]
        for d in range(1, pairs):
            total = total + self.along[d]
        parts = self.everywhere.shape[0]
        segments = parts // 2
        mine = at.core * segments + at.pipe
        self.everywhere[mine] = total

        def send(k, carry):
            peer = lax.rem(mine + k, parts)
            pltpu.make_async_remote_copy(
                src_ref=self.everywhere.at[mine],
                dst_ref=self.everywhere.at[mine],
                send_sem=self.send_sem.at[self.base + 5],
                recv_sem=self.recv_sem.at[self.base + 5],
                device_id={"pipe": lax.rem(peer, segments), "dp": at.dp - at.core + peer // segments},
            ).start()
            return carry

        lax.fori_loop(1, parts, send, 0)

    def finish(self):
        parts = self.everywhere.shape[0]
        wait_bytes(self.everywhere.at[0 : parts - 1], self.recv_sem.at[self.base + 5])
        for q in range(parts):
            self.result[q * SUB : (q + 1) * SUB, :] = self.everywhere[q]

    def drain(self):
        super().drain()
        pairs, parts = self.along.shape[0], self.everywhere.shape[0]
        wait_bytes(self.along.at[0 : pairs - 1], self.send_sem.at[self.base + 4])
        wait_bytes(self.everywhere.at[0 : parts - 1], self.send_sem.at[self.base + 5])


KINDS = 6
MATRICES = ("qkv", "proj", "inv", "point")
SMALLS = ("att", "mb")


def kernel(n_dp, n_pipe, count_in, names, *refs):
    (
        x_ref, ct_ref, qkv_hbm, dw_ref, group_ref, proj_hbm, inv_hbm, ibias_ref, mdw_ref, mbias_ref, point_hbm,
        gain_ref, shift_ref,
    ) = refs[:count_in]
    at = dict(zip(names, refs[count_in:]))
    (
        qkv_own, proj_ref, inv_ref, point_ref, perm, rowperm, wp, blocks_bd, dwp, mdwp, rmask, smask, hid, hid_t,
        grad_t, normed, mixo, rden, tvals, joined, s0, dvals, gmix, pre_u, pre_d, act, act_d, mid, gact, branch,
        gnow, stats, exbuf, send_sem, recv_sem, load_sem, red_send, red_recv, whole,
    ) = (at[name] for name in (
        "qkv_own", "proj", "inv", "point", "perm", "rowperm", "wp", "blocks_bd", "dwp", "mdwp", "rmask", "smask", "hid",
        "hid_t", "grad_t", "normed", "mixo", "rden", "tvals", "joined", "s0", "dvals", "gmix", "pre_u", "pre_d",
        "act", "act_d", "mid", "dvals", "branch", "gnow", "stats", "exbuf", "send_sem", "recv_sem", "load_sem",
        "red_send", "red_recv", "whole",
    ))
    place = Place()
    me = place.dp
    layers = proj_ref.shape[0]
    width = x_ref.shape[1]
    expanded = inv_ref.shape[2]
    total_rows = float(x_ref.shape[0] * n_dp)
    wide = width // LANE
    stages = 2 * layers

    loads = {}
    for i, (source, target) in enumerate(
        ((proj_hbm, proj_ref), (inv_hbm, inv_ref), (point_hbm, point_ref)), 1
    ):
        for l in range(layers):
            loads[i, l] = pltpu.make_async_copy(source.at[l], target.at[l], load_sem.at[i, l])
    piece_rows = width // 2 // n_pipe
    for l in range(layers):
        for q in range(2 * n_pipe):
            pltpu.make_async_copy(
                qkv_hbm.at[l, q * piece_rows : (q + 1) * piece_rows],
                qkv_own.at[l, q // n_pipe, q % n_pipe],
                load_sem.at[0, l],
            ).start()
        for i in range(1, 4):
            loads[i, l].start()

    barrier = pltpu.get_barrier_semaphore()

    def greet(k, carry):
        pl.semaphore_signal(barrier, inc=1, device_id={"dp": lax.rem(me + k, n_dp)})
        return carry

    lax.fori_loop(1, n_dp, greet, 0)

    def greet_segment(k, carry):
        there = lax.rem(place.pipe + k, n_pipe)
        for other in (me, me + 1 - 2 * place.core):
            pl.semaphore_signal(barrier, inc=1, device_id={"pipe": there, "dp": other})
        return carry

    lax.fori_loop(1, n_pipe, greet_segment, 0)

    jobs = {}
    for l in range(layers):
        for i, name in enumerate(MATRICES):
            jobs[name, l] = Projection(
                place, *(at[f"{name}_{kind}"].at[l] for kind in ("own", "pair", "first", "second")), red_send, red_recv,
                KINDS * (6 * l + i), at[f"{name}_outgoing"], at[f"{name}_landed"].at[l], whole,
                at[f"out_{name}"].at[l],
            )
        for i, name in enumerate(SMALLS):
            jobs[name, l] = Small(
                place, *(at[f"{name}_{kind}"].at[l] for kind in ("own", "pair", "first", "second")), red_send, red_recv,
                KINDS * (6 * l + 4 + i), *(at[f"{name}_{kind}"].at[l] for kind in ("along", "everywhere")),
                at[f"out_{name}"].at[l],
            )

    masks = head_masks()
    perm[...] = split_matrix(width)
    row, col = iota((width, width), 0), iota((width, width), 1)
    half = width // 2
    core_of = (row >= half).astype(jnp.int32)
    inner = row - half * core_of
    for q in range(1, n_pipe):
        inner = jnp.where(row - half * core_of >= q * piece_rows, inner + piece_rows, inner)
    rowperm[...] = jnp.where(inner + core_of * piece_rows == col, 1.0, 0.0).astype(BF)
    rmask[...] = row_mask()
    smask[...] = crop_mask(48, 192)

    block_lane, block_row = iota((LANE, LANE), 1), iota((LANE, LANE), 0)
    on_diag = (block_lane >> 5) == (block_row >> 5)
    tile = jnp.where((iota((32, LANE), 1) & 31) == iota((32, LANE), 0), 1.0, 0.0).astype(BF)

    for t in range(dw_ref.shape[0]):
        taps = dw_ref[t].astype(F32)
        for l in range(layers):
            dwp[l, t : t + 1, :] = taps[l : l + 1]
    for t in range(mdw_ref.shape[0]):
        taps = mdw_ref[t].astype(F32)
        for l in range(layers):
            mdwp[l, t : t + 1, :] = taps[l : l + 1]

    def prepare(l):
        wait_bytes(qkv_own.at[l], load_sem.at[0, l])
        for c in range(wide):
            cut = slice(c * width, (c + 1) * width)
            w_split = mm(qkv_own[l, :, :, :, cut].reshape(width, width), perm[...]).astype(BF)
            for part in range(3):
                wp[l, :, lanes(part * wide + c)] = w_split[:, lanes(part)]
        taps = [mm(dwp[l, :, c * width : (c + 1) * width].astype(BF), perm[...]) for c in range(wide)]
        for c in range(wide):
            for part in range(3):
                dwp[l, :, lanes(part * wide + c)] = taps[c][:, lanes(part)]
                rows = jnp.concatenate([group_ref[l, 3 * (4 * c + i) + part] for i in range(HEADS)], axis=0)
                full = jnp.where(on_diag, mm(rows, tile), 0.0)
                blocks_bd[l, part * wide + c] = full.astype(BF)

    spread = spread_matrix(x_ref.shape[0])
    hid[0] = mm(spread, x_ref[...]).astype(BF)
    gnow[...] = mm(spread, ct_ref[...])
    prepare(0)
    pl.semaphore_wait(barrier, n_dp - 1 + 2 * (n_pipe - 1))

    def slot_rows(count):
        return -(-count * wide // SUB) * SUB

    def exchange_start(e, vectors):
        rows = slot_rows(len(vectors))
        for i, vector in enumerate(vectors):
            for j in range(wide):
                row = i * wide + j
                exbuf[e, me, row : row + 1, :] = vector[:, lanes(j)]

        def send(k, carry):
            pltpu.make_async_remote_copy(
                src_ref=exbuf.at[e, me, 0:rows],
                dst_ref=exbuf.at[e, me, 0:rows],
                send_sem=send_sem.at[e],
                recv_sem=recv_sem.at[e],
                device_id={"dp": lax.rem(me + k, n_dp)},
            ).start()
            return carry

        lax.fori_loop(1, n_dp, send, 0)

    def exchange_finish(e, count):
        rows = slot_rows(count)
        wait_bytes(exbuf.at[e, 0 : n_dp - 1, 0:rows], recv_sem.at[e])
        total = exbuf[e, 0, 0:rows]
        for d in range(1, n_dp):
            total = total + exbuf[e, d, 0:rows]
        total = total * (1.0 / total_rows)
        return [
            jnp.concatenate([total[i * wide + j : i * wide + j + 1] for j in range(wide)], axis=1)
            for i in range(count)
        ]

    def attention_forward(l, s):
        joined[l] = mm(hid[s], wp[l]).astype(BF).astype(F32)

        def chunk(j, carry):
            at = lanes(j)
            cells = joined[l, :, at]
            conv = depthwise(cells.reshape(20, SUB, LANE), dwp[l, :, at], 5).reshape(ROWS, LANE)
            conv = (conv * rmask[...]).astype(BF)
            s0[l, :, at] = conv
            linear = mm(conv, blocks_bd[l, j])
            part = j // wide
            keep = rmask[...]
            for source, value in ((0, cells), (1, linear)):
                soft = softplus(value)
                soft = jnp.where(part == 1, soft * keep, soft)
                tvals[l, :, lanes(part * UNITS + source * wide + j % wide)] = jnp.where(part == 2, value, soft)
            return carry

        lax.fori_loop(0, 3 * wide, chunk, 0)

        def unit(u, carry):
            for start, size in BLOCKS:
                rows = slice(start, start + size)
                query = tvals[l, rows, lanes(u)]
                key = tvals[l, rows, lanes(u + UNITS)]
                value = tvals[l, rows, lanes(u + 2 * UNITS)]
                scores = mm(query.astype(BF), stacked(key, masks), NT)
                if start == SMALL:
                    scores = scores * smask[...]
                both = jnp.concatenate(
                    [stacked(value, masks), stacked(jnp.ones_like(value), masks)], axis=1
                )
                sums = mm(scores.astype(BF), both)
                inverse = 1.0 / sums[:, LANE:]
                rden[l, rows, lanes(u)] = inverse
                mixo[l, rows, lanes(u)] = sums[:, :LANE] * inverse
            return carry

        lax.fori_loop(0, UNITS, unit, 0)
        loads[1, l].wait()
        branch[...] = mm(mixo[l].astype(BF), proj_ref[l])

    def expand_forward(l, s):
        loads[2, l].wait()
        pre_u[l] = mm(hid[s], inv_ref[l])

        def chunk(j, carry):
            at = lanes(j)
            pre = pre_u[l, :, at] + ibias_ref[:, at].astype(F32)[l : l + 1]
            value, slope = silu_parts(pre)
            value = value * rmask[...]
            pre_u[l, :, at] = value
            pre_d[l, :, at] = (slope * rmask[...]).astype(BF)
            conv = depthwise(value.reshape(20, SUB, LANE), mdwp[l, :, at], 3).reshape(ROWS, LANE)
            out, out_slope = silu_parts(conv + mbias_ref[:, at].astype(F32)[l : l + 1])
            act[l, :, at] = (out * rmask[...]).astype(BF)
            act_d[l, :, at] = out_slope.astype(BF)
            return carry

        lax.fori_loop(0, expanded // LANE, chunk, 0)
        loads[3, l].wait()
        branch[...] = mm(act[l], point_ref[l])

    gains = gain_ref[...].astype(F32)
    shifts = shift_ref[...].astype(F32)
    last = stages - 1
    for s in range(stages):
        l = s // 2
        if s % 2 == 0:
            attention_forward(l, s)
        else:
            expand_forward(l, s)
        keep = rmask[...]
        for j in range(wide):
            branch[:, lanes(j)] = branch[:, lanes(j)] * keep
        value = branch[...]
        vectors = [column_sum(value), column_sum(value * value)]
        if s == last:
            upstream = gnow[...]
            vectors += [column_sum(upstream * value), column_sum(upstream)]
        exchange_start(s, vectors)
        if s == 0:
            for l in range(1, layers):
                prepare(l)
        hid_t[s] = mm(rowperm[...], hid[s], NT).astype(BF)
        mean, square, *backward = exchange_finish(s, len(vectors))
        scale = lax.rsqrt(square - mean * mean + EPS)
        stats[s : s + 1, :] = scale
        norm = (branch[...] - mean) * scale
        after = hid[s].astype(F32) + gains[s : s + 1] * norm + shifts[s : s + 1]
        for j in range(wide):
            normed[s, :, lanes(j)] = norm[:, lanes(j)] * keep
            hid[s + 1, :, lanes(j)] = (after[:, lanes(j)] * keep).astype(BF)
        if s == last:
            first_cross = scale * (backward[0] - mean * backward[1])
            first_total = backward[1]
            local_cross = scale * (vectors[2] - mean * vectors[3])
            local_sum = vectors[3]

    def small_row(name, l, row, value, at):
        jobs[name, l].own[row // 32, row // SUB % 4, row % SUB : row % SUB + 1, at] = value

    def expand_row(l, j, tap, value):
        block = j // wide
        jobs["mb", l].own[block // 2, block % 2 * 2 + tap // SUB, tap % SUB : tap % SUB + 1, lanes(j % wide)] = value

    def matrix(name, l, left, right, columns):
        own = jobs[name, l].own
        step = width
        for c in range(columns // step):
            cut = slice(c * step, (c + 1) * step)
            own[:, :, :, cut] = mm(left, right(cut)).astype(BF).reshape(2, n_pipe, piece_rows, step)
        jobs[name, l].start()

    def attention_backward(l, s, grad_branch, pause):
        gmix[...] = mm(grad_branch, proj_ref[l], NT).astype(BF).astype(F32)
        matrix("proj", l, grad_t[...], lambda cut: mixo[l, :, cut].astype(BF), mixo.shape[2])
        pause(0)

        def unit(u, carry):
            for start, size in BLOCKS:
                rows = slice(start, start + size)
                query = tvals[l, rows, lanes(u)]
                key = tvals[l, rows, lanes(u + UNITS)]
                value = tvals[l, rows, lanes(u + 2 * UNITS)]
                down = gmix[rows, lanes(u)] * rden[l, rows, lanes(u)]
                level = -down * mixo[l, rows, lanes(u)]
                ones = jnp.ones_like(value)
                key_stack, query_stack, down_stack = (
                    stacked(key, masks),
                    stacked(query, masks),
                    stacked(down, masks),
                )
                grad_scores = mm(
                    jnp.concatenate([down, level], axis=1).astype(BF),
                    jnp.concatenate([stacked(value, masks), stacked(ones, masks)], axis=1),
                    NT,
                )
                grad_scores_t = mm(
                    jnp.concatenate([value, ones], axis=1).astype(BF),
                    jnp.concatenate([down_stack, stacked(level, masks)], axis=1),
                    NT,
                )
                scores_t = mm(key.astype(BF), query_stack, NT)
                if start == SMALL:
                    inside = smask[...]
                    grad_scores = grad_scores * inside
                    grad_scores_t = grad_scores_t * inside
                    scores_t = scores_t * inside
                grad_query = mm(grad_scores.astype(BF), key_stack)
                grad_key = mm(grad_scores_t.astype(BF), query_stack)
                grad_value = mm(scores_t.astype(BF), down_stack)
                dvals[rows, lanes(u)] = grad_query * (1.0 - jnp.exp(-query))
                dvals[rows, lanes(u + UNITS)] = grad_key * (1.0 - jnp.exp(-key))
                dvals[rows, lanes(u + 2 * UNITS)] = grad_value
            return carry

        lax.fori_loop(0, UNITS, unit, 0)
        pause(1)

        def chunk(j, carry):
            at = lanes(j)
            part = j // wide
            slot = part * UNITS + j % wide
            grad_spread = dvals[:, lanes(slot + wide)].astype(BF)
            block = jnp.where(on_diag, mm(s0[l, :, at], grad_spread, TN), 0.0)
            block = block[0:32] + block[32:64] + block[64:96] + block[96:128]
            jobs["att", l].own[1, :, :, at] = block.reshape(4, SUB, LANE)
            grad_conv = mm(grad_spread, blocks_bd[l, j], NT).reshape(20, SUB, LANE)
            cells = joined[l, :, at].reshape(20, SUB, LANE)
            for tap, row in enumerate(depthwise_taps(cells, grad_conv, 5)):
                small_row("att", l, tap, row, at)
            back = depthwise(grad_conv, dwp[l, :, at], 5, flip=True).reshape(ROWS, LANE)
            mid[:, at] = (dvals[:, lanes(slot)] + back * rmask[...]).astype(BF)
            return carry

        lax.fori_loop(0, 3 * wide, chunk, 0)
        jobs["att", l].start()
        grad_hidden = mm(mid[:, : 3 * width], wp[l], NT)

        def gradients():
            def natural(cut):
                c = cut.start // width
                piece = jnp.concatenate([mid[:, lanes(part * wide + c)] for part in range(3)], axis=1)
                return mm(piece, perm[...], NT).astype(BF)

            matrix("qkv", l, hid_t[s], natural, 3 * width)

        return grad_hidden, gradients

    def expand_backward(l, s, grad_branch, pause):
        gact[:, 0:expanded] = mm(grad_branch, point_ref[l], NT).astype(BF).astype(F32)
        matrix("point", l, grad_t[...], lambda cut: act[l, :, cut], expanded)
        pause(0)

        def chunk(j, carry):
            at = lanes(j)
            grad_conv = gact[:, at] * act_d[l, :, at].astype(F32)
            expand_row(l, j, 9, column_sum(grad_conv))
            cells = pre_u[l, :, at].reshape(20, SUB, LANE)
            grad_conv = grad_conv.reshape(20, SUB, LANE)
            for tap, row in enumerate(depthwise_taps(cells, grad_conv, 3)):
                expand_row(l, j, tap, row)
            back = depthwise(grad_conv, mdwp[l, :, at], 3, flip=True).reshape(ROWS, LANE)
            grad_pre = (back * pre_d[l, :, at].astype(F32)).astype(BF)
            mid[:, at] = grad_pre
            expand_row(l, j, 10, column_sum(grad_pre.astype(F32)))
            return carry

        lax.fori_loop(0, expanded // LANE, chunk, 0)
        jobs["mb", l].start()
        pause(1)
        grad_hidden = mm(mid[...], inv_ref[l], NT)

        def gradients():
            matrix("inv", l, hid_t[s], lambda cut: mid[:, cut], expanded)

        return grad_hidden, gradients

    queue = []

    def advance():
        for entry in queue:
            if entry[1]:
                entry[1].pop(0)()

    def enter(job):
        steps = [job.step1, job.step2, job.step3]
        if isinstance(job, Small):
            steps.append(job.step4)
        queue.append((job, steps + [job.finish]))

    def pause(k):
        advance()

    for s in range(stages - 1, -1, -1):
        l = s // 2
        keep = rmask[...]
        if s == last:
            cross, total = first_cross, first_total
        else:
            cross, total = exchange_finish(stages + s, 2)
        if s % 2 == 0:
            small_row("att", l, 25, local_cross, slice(0, width))
            small_row("att", l, 25, local_sum, slice(width, 2 * width))
        else:
            small_row("mb", l, 11, local_cross, slice(0, width))
            small_row("mb", l, 16 + 11, local_sum, slice(0, width))
        grad_branch = (stats[s : s + 1, :] * gains[s : s + 1]) * (gnow[...] - total - normed[s] * cross)
        grad_branch = jnp.concatenate(
            [grad_branch[:, lanes(j)] * keep for j in range(wide)], axis=1
        ).astype(BF)
        grad_t[...] = mm(rowperm[...], grad_branch, NT).astype(BF)
        back = attention_backward if s % 2 == 0 else expand_backward
        grad_hidden, gradients = back(l, s, grad_branch, pause)
        after = (gnow[...] + grad_hidden).astype(BF).astype(F32)
        gnow[...] = after
        if s > 0:
            local_cross, local_sum = column_sum(after * normed[s - 1]), column_sum(after)
            exchange_start(stages + s - 1, [local_cross, local_sum])
        gradients()
        advance()
        for name in ("att", "proj", "qkv") if s % 2 == 0 else ("mb", "point", "inv"):
            enter(jobs[name, l])
        if s == last:
            at["out_x"][...] = mm(spread, hid[stages], TN).astype(BF)

    at["out_g"][...] = mm(spread, gnow[...].astype(BF), TN).astype(BF)
    while any(steps for _, steps in queue):
        advance()
    for job, _ in queue:
        job.drain()
    for e in range(2 * stages - 1):
        rows = slot_rows(4 if e == last else 2)
        wait_bytes(exbuf.at[e, 0 : n_dp - 1, 0:rows], send_sem.at[e])


def unsplit(value, wide):
    lane = iota((1, LANE), 1) >> 5
    columns = []
    for c in range(wide):
        parts = [value[:, lanes(part * wide + c)] for part in range(3)]
        for k in range(3):
            column = None
            for slot in range(4):
                index = 4 * k + slot
                moved = pltpu.roll(parts[index % 3], (slot - index // 3) % 4 * 32, 1)
                column = moved if column is None else jnp.where(lane == slot, moved, column)
            columns.append(column)
    return columns


def arrange(layers, wide, shares, x_in, g_in, qkv_in, proj_in, inv_in, point_in, att_in, mb_in,
            x_out, g_out, qkv_out, proj_out, inv_out, point_out, dw_out, group_out, ibias_out, mdw_out, mbias_out,
            gain_out, shift_out):
    width = wide * LANE
    share_qkv, share_proj, share_inv, share_point = shares
    x_out[...] = x_in[...]
    g_out[...] = g_in[...]
    taps, mtaps = dw_out.shape[0], mdw_out.shape[0]
    for l in range(layers):
        qkv_out[l] = jnp.transpose(jnp.concatenate([qkv_in[l], jnp.zeros((32, qkv_in.shape[2]), F32)], axis=0))[
            0:share_qkv, 0 : qkv_in.shape[1]
        ]
        proj_out[l] = jnp.transpose(jnp.concatenate([proj_in[l], jnp.zeros((32, proj_in.shape[2]), F32)], axis=0))[
            0:share_proj, 0 : proj_in.shape[1]
        ]
        inv_out[l] = inv_in[l, :, 0:share_inv]
        point_out[l] = jnp.transpose(jnp.concatenate([point_in[l], jnp.zeros((32, point_in.shape[2]), F32)], axis=0))[
            0:share_point, 0 : point_in.shape[1]
        ]
        natural = unsplit(att_in[l], wide)
        for j, column in enumerate(natural):
            for t in range(taps):
                dw_out[t, l : l + 1, lanes(j)] = column[t : t + 1]
            group_out[l, :, lanes(j)] = column[32:64]
        for block in range(4):
            cut = slice(block * width, (block + 1) * width)
            rows = mb_in[l, 16 * block : 16 * block + 16]
            for t in range(mtaps):
                mdw_out[t, l : l + 1, cut] = rows[t : t + 1]
            mbias_out[l : l + 1, cut] = rows[9:10]
            ibias_out[l : l + 1, cut] = rows[10:11]
        gain_out[2 * l : 2 * l + 1, :] = att_in[l, 25:26, 0:width]
        shift_out[2 * l : 2 * l + 1, :] = att_in[l, 25:26, width : 2 * width]
        gain_out[2 * l + 1 : 2 * l + 2, :] = mb_in[l, 11:12, :]
        shift_out[2 * l + 1 : 2 * l + 2, :] = mb_in[l, 27:28, :]


def padded(columns):
    return -(-columns // LANE) * LANE


def body(
    activations, cotangent, att_qkv, att_dw, att_group, att_proj, mb_inv, mb_inv_bias, mb_dw, mb_dw_bias, mb_point,
    bn_gain, bn_bias,
):
    n_dp, n_pipe = lax.axis_size("dp"), lax.axis_size("pipe")
    layers, width, joined_width = att_qkv.shape
    mixed_width = att_proj.shape[1]
    expanded = mb_inv.shape[2]
    tokens = activations.shape[2]
    stages = 2 * layers
    rows = width // 2 // n_pipe
    vmem = pl.BlockSpec(memory_space=pltpu.VMEM)
    hbm = pl.BlockSpec(memory_space=pl.ANY)
    columns = {"qkv": joined_width, "proj": mixed_width, "inv": expanded, "point": expanded}
    small_columns = {"att": joined_width, "mb": width}
    outs = {
        "out_x": jax.ShapeDtypeStruct((tokens, width), BF),
        "out_g": jax.ShapeDtypeStruct((tokens, width), BF),
    }
    scratch = {
        "proj": pltpu.VMEM(att_proj.shape, BF),
        "inv": pltpu.VMEM(mb_inv.shape, BF),
        "point": pltpu.VMEM(mb_point.shape, BF),
        "perm": pltpu.VMEM((width, width), BF),
        "rowperm": pltpu.VMEM((width, width), BF),
        "wp": pltpu.VMEM((layers, width, joined_width), BF),
        "blocks_bd": pltpu.VMEM((layers, joined_width // LANE, LANE, LANE), BF),
        "dwp": pltpu.VMEM((layers, 32, joined_width), F32),
        "mdwp": pltpu.VMEM((layers, 16, expanded), F32),
        "rmask": pltpu.VMEM((ROWS, LANE), F32),
        "smask": pltpu.VMEM((48, 192), F32),
        "hid": pltpu.VMEM((stages + 1, ROWS, width), BF),
        "hid_t": pltpu.VMEM((stages, width, ROWS), BF),
        "grad_t": pltpu.VMEM((width, ROWS), BF),
        "normed": pltpu.VMEM((stages, ROWS, width), F32),
        "mixo": pltpu.VMEM((layers, ROWS, mixed_width), F32),
        "rden": pltpu.VMEM((layers, ROWS, mixed_width), F32),
        "tvals": pltpu.VMEM((layers, ROWS, 3 * mixed_width), F32),
        "joined": pltpu.VMEM((layers, ROWS, joined_width), F32),
        "s0": pltpu.VMEM((layers, ROWS, joined_width), BF),
        "dvals": pltpu.VMEM((ROWS, 3 * mixed_width), F32),
        "gmix": pltpu.VMEM((ROWS, mixed_width), F32),
        "pre_u": pltpu.VMEM((layers, ROWS, expanded), F32),
        "pre_d": pltpu.VMEM((layers, ROWS, expanded), BF),
        "act": pltpu.VMEM((layers, ROWS, expanded), BF),
        "act_d": pltpu.VMEM((layers, ROWS, expanded), BF),
        "mid": pltpu.VMEM((ROWS, expanded), BF),
        "branch": pltpu.VMEM((ROWS, width), F32),
        "gnow": pltpu.VMEM((ROWS, width), F32),
        "stats": pltpu.VMEM((8, width), F32),
        "exbuf": pltpu.VMEM((2 * stages - 1, n_dp, 2 * SUB, LANE), F32),
        "whole": pltpu.VMEM((rows, expanded), F32),
        "send_sem": pltpu.SemaphoreType.DMA((2 * stages - 1,)),
        "recv_sem": pltpu.SemaphoreType.DMA((2 * stages - 1,)),
        "load_sem": pltpu.SemaphoreType.DMA((4, layers)),
        "red_send": pltpu.SemaphoreType.DMA((KINDS * 6 * layers,)),
        "red_recv": pltpu.SemaphoreType.DMA((KINDS * 6 * layers,)),
    }
    for name in MATRICES:
        n = columns[name]
        share = padded(n // n_dp)
        outs[f"out_{name}"] = jax.ShapeDtypeStruct((layers, 2 * rows, share), F32)
        scratch[f"{name}_own"] = pltpu.VMEM((layers, 2, n_pipe, rows, n), BF)
        scratch[f"{name}_pair"] = pltpu.VMEM((layers, n_pipe, rows, n), BF)
        scratch[f"{name}_first"] = pltpu.VMEM((layers, 2, rows, n), BF)
        scratch[f"{name}_second"] = pltpu.VMEM((layers, rows, n), BF)
        scratch[f"{name}_outgoing"] = pltpu.VMEM((n_dp, rows, share), BF)
        scratch[f"{name}_landed"] = pltpu.VMEM((layers, n_dp, rows, share), BF)
    for name in SMALLS:
        n = small_columns[name]
        outs[f"out_{name}"] = jax.ShapeDtypeStruct((layers, 8 * SUB, n), F32)
        scratch[f"{name}_own"] = pltpu.VMEM((layers, 2, n_pipe, SUB, n), F32)
        scratch[f"{name}_pair"] = pltpu.VMEM((layers, n_pipe, SUB, n), F32)
        scratch[f"{name}_first"] = pltpu.VMEM((layers, 2, SUB, n), F32)
        scratch[f"{name}_second"] = pltpu.VMEM((layers, SUB, n), F32)
        scratch[f"{name}_along"] = pltpu.VMEM((layers, n_dp // 2, SUB, n), F32)
        scratch[f"{name}_everywhere"] = pltpu.VMEM((layers, 2 * n_pipe, SUB, n), F32)
    results = pl.pallas_call(
        functools.partial(kernel, n_dp, n_pipe, 13, tuple(outs) + tuple(scratch)),
        out_shape=tuple(outs.values()),
        in_specs=[vmem, vmem, hbm, vmem, vmem, hbm, hbm, vmem, vmem, vmem, hbm, vmem, vmem],
        out_specs=(vmem,) * len(outs),
        scratch_shapes=list(scratch.values()),
        compiler_params=pltpu.CompilerParams(
            collective_id=0, has_side_effects=True, vmem_limit_bytes=63 * 1024 * 1024
        ),
    )(
        activations.reshape(tokens, width),
        cotangent.reshape(tokens, width),
        att_qkv,
        att_dw.transpose(1, 0, 2),
        att_group,
        att_proj,
        mb_inv,
        mb_inv_bias,
        mb_dw.transpose(1, 0, 2),
        mb_dw_bias,
        mb_point,
        bn_gain,
        bn_bias,
    )
    shares = tuple(columns[name] // n_dp for name in MATRICES)
    taps, mtaps = att_dw.shape[1], mb_dw.shape[1]
    arranged = pl.pallas_call(
        functools.partial(arrange, layers, width // LANE, shares),
        out_shape=(
            jax.ShapeDtypeStruct((tokens, width), BF),
            jax.ShapeDtypeStruct((tokens, width), BF),
            jax.ShapeDtypeStruct((layers, shares[0], 2 * rows), F32),
            jax.ShapeDtypeStruct((layers, shares[1], 2 * rows), F32),
            jax.ShapeDtypeStruct((layers, 2 * rows, shares[2]), F32),
            jax.ShapeDtypeStruct((layers, shares[3], 2 * rows), F32),
            jax.ShapeDtypeStruct((taps, layers, joined_width), F32),
            jax.ShapeDtypeStruct((layers, 32, joined_width), F32),
            jax.ShapeDtypeStruct((layers, expanded), F32),
            jax.ShapeDtypeStruct((mtaps, layers, expanded), F32),
            jax.ShapeDtypeStruct((layers, expanded), F32),
            jax.ShapeDtypeStruct((stages, width), F32),
            jax.ShapeDtypeStruct((stages, width), F32),
        ),
        in_specs=[vmem] * 8,
        out_specs=(vmem,) * 13,
    )(*results)
    x_out, g_out, qkv, proj, inv, point, dw, group, ibias, mdw, mbias, gain, shift = arranged
    groups, size = att_group.shape[1], att_group.shape[2]
    return (
        x_out.reshape(activations.shape),
        g_out.reshape(activations.shape),
        qkv.transpose(0, 2, 1),
        dw.transpose(1, 0, 2),
        group.reshape(layers, size, groups, size).transpose(0, 2, 1, 3),
        proj,
        inv,
        ibias,
        mdw.transpose(1, 0, 2),
        mbias,
        point,
        gain,
        shift,
    )


def solution(mesh):
    placed = (P("pipe", "dp", None, None), P("pipe", "dp", None, None)) + (P(),) * 11
    return jax.shard_map(
        body,
        mesh=mesh,
        in_specs=placed,
        out_specs=(
            P("pipe", "dp", None, None),
            P("pipe", "dp", None, None),
            P(None, "pipe", "dp"),
            P(),
            P(),
            P(None, "dp", "pipe"),
            P(None, "pipe", "dp"),
            P(),
            P(),
            P(),
            P(None, "dp", "pipe"),
            P(),
            P(),
        ),
        check_vma=False,
    )
```

```python
import functools

import jax
import jax.numpy as jnp
from jax import lax
from jax.experimental import pallas as pl
from jax.experimental.pallas import tpu as pltpu
from jax.sharding import PartitionSpec as P

F32 = jnp.float32
BF = jnp.bfloat16
EPS = 1e-05
LANE = 128
SUB = 8
ROWS = 160
SMALL = 112
BLOCKS = ((0, 56), (56, 56), (112, 48))
HEADS = 4
UNITS = 6
UNIT_STEP = 6
EXPAND_STEP = 1
NN = (((1,), (0,)), ((), ()))
NT = (((1,), (1,)), ((), ()))
TN = (((0,), (0,)), ((), ()))


def mm(a, b, dims=NN):
    return lax.dot_general(a, b, dims, preferred_element_type=F32)


def iota(shape, dim):
    return lax.broadcasted_iota(jnp.int32, shape, dim)


def lanes(j):
    if isinstance(j, int):
        return slice(j * LANE, (j + 1) * LANE)
    return pl.ds(pl.multiple_of(j * LANE, LANE), LANE)


def spread_matrix(tokens):
    row, col = iota((ROWS, tokens), 0), iota((ROWS, tokens), 1)
    crop = (row >= 56).astype(jnp.int32)
    inner = row - 56 * crop
    big = crop * 49 + (inner >> 3) * 7 + (inner & 7)
    small_row = row - SMALL
    pair = (small_row >= 24).astype(jnp.int32)
    inner = small_row - 24 * pair
    small = 98 + (pair * 2 + ((inner & 7) >> 2)) * 9 + (inner >> 3) * 3 + (inner & 3)
    is_big = row < SMALL
    valid = jnp.where(is_big, row & 7, (row & 3) + 4) < 7
    hit = (jnp.where(is_big, big, small) == col) & valid
    return jnp.where(hit, 1.0, 0.0).astype(BF)


def split_matrix(width):
    row, col = iota((width, width), 0), iota((width, width), 1)
    head = (row >= 96).astype(jnp.int32) + (row >= 192).astype(jnp.int32) + (row >= 288).astype(jnp.int32)
    rest = row - 96 * head
    part = (rest >= 32).astype(jnp.int32) + (rest >= 64).astype(jnp.int32)
    target = part * 128 + head * 32 + (rest - 32 * part)
    return jnp.where(target == col, 1.0, 0.0).astype(BF)


def row_mask(width=LANE):
    row = iota((ROWS, width), 0)
    valid = jnp.where(row < SMALL, row & 7, (row & 3) + 4) < 7
    return jnp.where(valid, 1.0, 0.0)


def crop_mask(rows, columns):
    row, col = iota((rows, columns), 0), iota((rows, columns), 1)
    for step in (3, 2, 1):
        col = jnp.where(col >= rows * step, col - rows * step, col)
    row_crop = (row >= 24).astype(jnp.int32) * 2 + ((row & 7) >> 2)
    col_crop = (col >= 24).astype(jnp.int32) * 2 + ((col & 7) >> 2)
    return jnp.where(row_crop == col_crop, 1.0, 0.0)


def head_masks():
    lane = iota((1, LANE), 1)
    return [jnp.where((lane >= 32 * h) & (lane < 32 * h + 32), 1.0, 0.0) for h in range(HEADS)]


def stacked(value):
    return jnp.concatenate([value * mask for mask in head_masks()], axis=0).astype(BF)


def joint(*values):
    return jnp.concatenate(values, axis=1).astype(BF)


def shifted(tokens, step):
    if step == 0:
        return tokens
    moved = pltpu.roll(tokens, (-step) % SUB, 1)
    if abs(step) == 1:
        return moved
    at = iota((1, SUB, LANE), 1)
    if tokens.shape[0] > 6:
        wrong = (at == 0) if step < 0 else (at == 6)
    else:
        wrong = ((at & 3) == 0) if step < 0 else ((at & 3) == 2)
    return jnp.where(wrong, 0.0, moved)


def tap_pairs(side, step):
    return range(max(0, -step), min(side, side - step))


def crops(tokens):
    return ((tokens[:14], 7), (tokens[14:], 3))


def depthwise(tokens, taps, reach, flip=False):
    margin = reach // 2
    parts = []
    for cells, side in crops(tokens):
        sums = [None] * side
        for dj in range(-margin, margin + 1):
            moved = shifted(cells, dj).reshape(2, side, SUB, LANE)
            for di in range(-margin, margin + 1):
                tap = (margin - di) * reach + margin - dj if flip else (margin + di) * reach + margin + dj
                weight = taps[tap : tap + 1, :].reshape(1, 1, LANE)
                for a in tap_pairs(side, di):
                    term = moved[:, a + di] * weight
                    sums[a] = term if sums[a] is None else sums[a] + term
        parts.append(jnp.stack(sums, axis=1).reshape(2 * side, SUB, LANE))
    return jnp.concatenate(parts, axis=0)


def depthwise_taps(tokens, grads, reach):
    margin = reach // 2
    totals = {}
    for (cells, side), (grad_cells, _) in zip(crops(tokens), crops(grads)):
        grad_cells = grad_cells.reshape(2, side, SUB, LANE)
        for dj in range(-margin, margin + 1):
            moved = shifted(cells, dj).reshape(2, side, SUB, LANE)
            for di in range(-margin, margin + 1):
                tap = (margin + di) * reach + margin + dj
                total = totals.get(tap)
                for a in tap_pairs(side, di):
                    term = moved[:, a + di] * grad_cells[:, a]
                    total = term if total is None else total + term
                if total is not None:
                    totals[tap] = total
    return [jnp.sum(jnp.sum(totals[tap], axis=0), axis=0, keepdims=True) for tap in range(reach * reach)]


def softplus(x):
    small = jnp.exp(-jnp.abs(x))
    return jnp.maximum(x, 0.0) + jnp.where(small < 1e-3, small * (1.0 - 0.5 * small), jnp.log(1.0 + small))


def silu_parts(x):
    gate = 0.5 * jnp.tanh(0.5 * x) + 0.5
    value = x * gate
    return value, gate + value * (1.0 - gate)


def loop(count, step, body):
    def several(i, carry):
        for k in range(step):
            body(i * step + k)
        return carry

    if step == count:
        several(0, 0)
    else:
        lax.fori_loop(0, count // step, several, 0)


def groups(count, step, body, unroll=False):
    if step == count or unroll:
        for first in range(0, count, step):
            body(first)
    else:
        lax.fori_loop(0, count // step, lambda i, carry: (body(i * step), carry)[1], 0)


def column_sum(value):
    return jnp.sum(value, axis=0, keepdims=True)


def wait_bytes(ref, sem):
    pltpu.make_async_copy(ref, ref, sem).wait()


class Reduction:
    def __init__(self, place, own, pair, first, second, send_sem, recv_sem, base):
        self.place, self.own, self.pair, self.first, self.second = place, own, pair, first, second
        self.send_sem, self.recv_sem, self.base = send_sem, recv_sem, base

    def copy(self, source, target, kind, pipe, dp):
        return pltpu.make_async_remote_copy(
            src_ref=source,
            dst_ref=target,
            send_sem=self.send_sem.at[self.base + kind],
            recv_sem=self.recv_sem.at[self.base + kind],
            device_id={"pipe": pipe, "dp": dp},
        )

    def to_pair(self):
        at = self.place
        return self.copy(self.own.at[1 - at.core], self.pair, 0, at.pipe, at.dp + 1 - 2 * at.core)

    def to_first(self, bit):
        at = self.place
        peer = at.pipe + (1 + at.core) * (1 - 2 * at.bit1)
        return self.copy(self.own.at[at.core, at.slab(1 - at.bit1, bit)], self.first.at[bit], 1 + bit, peer, at.dp)

    def to_second(self):
        at = self.place
        peer = at.pipe + (2 - at.core) * (1 - 2 * at.bit2)
        return self.copy(self.own.at[at.core, at.slab(at.bit1, 1 - at.bit2)], self.second, 3, peer, at.dp)

    def start(self):
        self.to_pair().start()

    def step1(self):
        at = self.place
        self.to_pair().wait_recv()
        for bit in range(2):
            slab = at.slab(1 - at.bit1, bit)
            self.own[at.core, slab] = self.own[at.core, slab] + self.pair[slab]
            self.to_first(bit).start()

    def step2(self):
        at = self.place
        for bit in range(2):
            self.to_first(bit).wait_recv()
        bit = 1 - at.bit2
        slab = at.slab(at.bit1, bit)
        total = self.own[at.core, slab].astype(F32) + self.pair[slab].astype(F32) + self.first[bit].astype(F32)
        self.own[at.core, slab] = total.astype(self.own.dtype)
        self.to_second().start()

    def part(self):
        at = self.place
        self.to_second().wait_recv()
        slab = at.pipe
        total = self.own[at.core, slab].astype(F32) + self.pair[slab].astype(F32)
        return total + self.first[at.bit2].astype(F32) + self.second[...].astype(F32)

    def drain(self):
        for made in (self.to_pair(), self.to_first(0), self.to_first(1), self.to_second()):
            made.wait_send()


class Place:
    def __init__(self):
        self.pipe, self.dp = lax.axis_index("pipe"), lax.axis_index("dp")
        self.core = lax.rem(self.dp, 2)
        low, high = lax.rem(self.pipe, 2), self.pipe // 2
        self.bit1 = low * (1 - self.core) + high * self.core
        self.bit2 = high * (1 - self.core) + low * self.core

    def slab(self, bit1, bit2):
        return bit1 * (1 + self.core) + bit2 * (2 - self.core)


class Columns:
    def __init__(self, place, matrices, shares, send_sem, recv_sem, base, outgoing, landed, whole, result):
        self.place, self.matrices, self.shares = place, matrices, shares
        self.send_sem, self.recv_sem = send_sem.at[base], recv_sem.at[base]
        self.outgoing, self.landed, self.whole, self.result = outgoing, landed, whole, result

    def send(self):
        at = self.place
        n_dp, rows, width = self.outgoing.shape
        spans, start = [], 0
        for pieces in self.matrices:
            first = start
            for piece in pieces:
                size = piece.own.shape[3]
                self.whole[:, start : start + size] = piece.part()
                start += size
            spans.append((first, start - first))
        lane = iota((1, width), 1)

        def cut(d, carry):
            result, target = None, 0
            for (first, columns), share in zip(spans, self.shares):
                cover = min(max(padded(share) + LANE, width), columns)
                offset = d * share
                base = jnp.minimum(offset // LANE, (columns - cover) // LANE) * LANE
                piece = self.whole[:, pl.ds(pl.multiple_of(first + base, LANE), cover)]
                piece = pltpu.roll(piece, lax.rem(cover + target - (offset - base), cover), 1)[:, 0:width]
                result = piece if result is None else jnp.where(lane < target, result, piece)
                target += share
            self.outgoing[d] = result.astype(BF)
            return carry

        lax.fori_loop(0, n_dp, cut, 0)

        def push(k, carry):
            peer = lax.rem(at.dp + k, n_dp)
            pltpu.make_async_remote_copy(
                src_ref=self.outgoing.at[peer],
                dst_ref=self.landed.at[at.dp],
                send_sem=self.send_sem,
                recv_sem=self.recv_sem,
                device_id={"dp": peer},
            ).start()
            return carry

        lax.fori_loop(1, n_dp, push, 0)
        self.landed[at.dp] = self.outgoing[at.dp]

    def finish(self):
        n_dp, rows, _ = self.outgoing.shape
        wait_bytes(self.landed.at[0 : n_dp - 1], self.recv_sem)
        for core in range(2):
            total = self.landed[core].astype(F32)
            for d in range(core + 2, n_dp, 2):
                total = total + self.landed[d].astype(F32)
            self.result[core * rows : (core + 1) * rows, :] = total
        wait_bytes(self.outgoing.at[0 : n_dp - 1], self.send_sem)


class Small(Reduction):
    def __init__(self, *args):
        *rest, self.stage, self.along, self.everywhere, self.result = args
        super().__init__(*rest)

    def start(self):
        slabs, _, columns = self.stage.shape
        half = self.own.shape[3]
        for q in range(slabs):
            if half == columns:
                self.own[q // self.own.shape[1], q % self.own.shape[1]] = self.stage[q]
                continue
            low, high = self.stage[q, :, 0:half], self.stage[q, :, half:columns]
            if columns < 2 * half:
                high = jnp.concatenate([high, jnp.zeros((SUB, 2 * half - columns), F32)], axis=1)
            self.own[q // self.own.shape[1], q % self.own.shape[1]] = jnp.concatenate([low, high], axis=0).astype(BF)
        super().start()

    def step3(self):
        at = self.place
        pairs = self.along.shape[0]
        mine = at.dp // 2
        self.along[mine] = self.part().astype(self.along.dtype)

        def send(k, carry):
            peer = lax.rem(mine + k, pairs)
            pltpu.make_async_remote_copy(
                src_ref=self.along.at[mine],
                dst_ref=self.along.at[mine],
                send_sem=self.send_sem.at[self.base + 4],
                recv_sem=self.recv_sem.at[self.base + 4],
                device_id={"dp": peer * 2 + at.core},
            ).start()
            return carry

        lax.fori_loop(1, pairs, send, 0)

    def step4(self):
        at = self.place
        pairs = self.along.shape[0]
        wait_bytes(self.along.at[0 : pairs - 1], self.recv_sem.at[self.base + 4])
        total = self.along[0].astype(F32)
        for d in range(1, pairs):
            total = total + self.along[d].astype(F32)
        parts = self.everywhere.shape[0]
        segments = parts // 2
        mine = at.core * segments + at.pipe
        self.everywhere[mine] = total.astype(self.everywhere.dtype)

        def send(k, carry):
            peer = lax.rem(mine + k, parts)
            pltpu.make_async_remote_copy(
                src_ref=self.everywhere.at[mine],
                dst_ref=self.everywhere.at[mine],
                send_sem=self.send_sem.at[self.base + 5],
                recv_sem=self.recv_sem.at[self.base + 5],
                device_id={"pipe": lax.rem(peer, segments), "dp": at.dp - at.core + peer // segments},
            ).start()
            return carry

        lax.fori_loop(1, parts, send, 0)

    def finish(self):
        parts = self.everywhere.shape[0]
        wait_bytes(self.everywhere.at[0 : parts - 1], self.recv_sem.at[self.base + 5])
        for q in range(parts):
            value = self.everywhere[q].astype(F32)
            half = value.shape[1]
            self.result[q * SUB : (q + 1) * SUB, 0:half] = value[0:SUB]
            if half < self.result.shape[1]:
                self.result[q * SUB : (q + 1) * SUB, half:] = value[SUB:, 0 : self.result.shape[1] - half]

    def drain(self):
        super().drain()
        pairs, parts = self.along.shape[0], self.everywhere.shape[0]
        wait_bytes(self.along.at[0 : pairs - 1], self.send_sem.at[self.base + 4])
        wait_bytes(self.everywhere.at[0 : parts - 1], self.send_sem.at[self.base + 5])


PLAN = {
    ("m2", 1): ("point.1.step1",),
    ("done", 3): ("mb.1.step1",),
    ("begin", 2): ("inv.1.step1",),
    ("t0", 1): ("point.1.step2", "mb.1.step2",),
    ("t2", 1): ("proj.1.step1",),
    ("c0", 1): (),
    ("c1", 1): (),
    ("c2", 1): ("inv.1.step2", "qkv0.1.step1",),
    ("sent", 2): ("mb.1.step3", "qkv1.1.step1",),
    ("done", 2): ("qkv2.1.step1", "proj.1.step2", "att.1.step1",),
    ("begin", 1): ("mbcols.1.send", "qkv0.1.step2",),
    ("m0", 0): ("qkv1.1.step2", "qkv2.1.step2", "att.1.step2",),
    ("m2", 0): ("point.0.step1", "mb.1.step4",),
    ("sent", 1): ("att.1.step3", "attcols.1.send",),
    ("done", 1): ("mb.0.step1", "mb.1.finish",),
    ("begin", 0): ("inv.0.step1", "mbcols.1.finish",),
    ("t0", 0): ("point.0.step2", "mb.0.step2", "att.1.step4",),
    ("t2", 0): ("proj.0.step1",),
    ("c0", 0): ("mb.0.step3",),
    ("c1", 0): ("qkv0.0.step1", "inv.0.step2",),
    ("c2", 0): ("qkv1.0.step1", "attcols.1.finish", "att.1.finish",),
    ("sent", 0): ("qkv2.0.step1", "att.0.step1", "proj.0.step2", "mb.0.step4", "qkv0.0.step2", "mbcols.0.send",),
    ("done", 0): ("att.0.step2", "qkv1.0.step2", "qkv2.0.step2", "att.0.step3", "attcols.0.send", "att.0.step4", "mb.0.finish", "mbcols.0.finish", "attcols.0.finish", "att.0.finish",),
}
KINDS = 6
MATRICES = ("qkv0", "qkv1", "qkv2", "proj", "inv", "point")
SMALLS = ("att", "mb")
JOBS = len(MATRICES) + len(SMALLS)


def kernel(n_dp, n_pipe, count_in, names, *refs):
    (
        x_ref, ct_ref, qkv_hbm, dw_ref, group_ref, proj_hbm, inv_hbm, ibias_ref, mdw_ref, mbias_ref, point_hbm,
        gain_ref, shift_ref,
    ) = refs[:count_in]
    at = dict(zip(names, refs[count_in:]))
    (
        inv_own, proj_ref, inv_ref, point_ref, perm, rowperm, wp, blocks_bd, dwp, mdwp, rmask, smask, diag, diag_t, hid, hid_t,
        grad_t, normed, mixo, rden, tvals, joined, s0, dvals, gmix, pre_u, pre_d, act, act_d, mid, gact, branch,
        gnow, stats, exbuf, send_sem, recv_sem, load_sem, red_send, red_recv, whole,
    ) = (at[name] for name in (
        "inv_own", "proj", "inv", "point", "perm", "rowperm", "wp", "blocks_bd", "dwp", "mdwp", "rmask", "smask", "diag", "diag_t", "hid",
        "hid_t", "grad_t", "normed", "mixo", "rden", "tvals", "joined", "s0", "dvals", "gmix", "pre_u", "pre_d",
        "act", "act_d", "mid", "dvals", "branch", "gnow", "stats", "exbuf", "send_sem", "recv_sem", "load_sem",
        "red_send", "red_recv", "whole",
    ))
    place = Place()
    me = place.dp
    layers = proj_ref.shape[0]
    width = x_ref.shape[1]
    expanded = inv_ref.shape[2]
    total_rows = float(x_ref.shape[0] * n_dp)
    wide = width // LANE
    stages = 2 * layers

    loads = {}
    for i, (source, target) in enumerate(
        ((proj_hbm, proj_ref), (inv_hbm, inv_ref), (point_hbm, point_ref)), 1
    ):
        for l in range(layers):
            loads[i, l] = pltpu.make_async_copy(source.at[l], target.at[l], load_sem.at[i, l])
    piece_rows = width // 2 // n_pipe
    for l in range(layers):
        for q in range(2 * n_pipe):
            pltpu.make_async_copy(
                qkv_hbm.at[l, q * piece_rows : (q + 1) * piece_rows],
                inv_own.at[l, q // n_pipe, q % n_pipe, :, 0 : 3 * width],
                load_sem.at[0, l],
            ).start()
        for i in range(1, 4):
            loads[i, l].start()

    barrier = pltpu.get_barrier_semaphore()

    def greet(k, carry):
        pl.semaphore_signal(barrier, inc=1, device_id={"dp": lax.rem(me + k, n_dp)})
        return carry

    lax.fori_loop(1, n_dp, greet, 0)

    def greet_segment(k, carry):
        there = lax.rem(place.pipe + k, n_pipe)
        for other in (me, me + 1 - 2 * place.core):
            pl.semaphore_signal(barrier, inc=1, device_id={"pipe": there, "dp": other})
        return carry

    lax.fori_loop(1, n_pipe, greet_segment, 0)

    jobs = {}
    for l in range(layers):
        for i, name in enumerate(MATRICES + SMALLS):
            refs_of = [at[f"{name}_{kind}"].at[l] for kind in ("own", "pair", "first", "second")]
            base = KINDS * (JOBS * l + i)
            if name in SMALLS:
                rest = [at[f"{name}_stage"]] + [at[f"{name}_{kind}"].at[l] for kind in ("along", "everywhere")]
                jobs[name, l] = Small(place, *refs_of, red_send, red_recv, base, *rest, at[f"out_{name}"].at[l])
            else:
                jobs[name, l] = Reduction(place, *refs_of, red_send, red_recv, base)
        for i, (name, members, sizes) in enumerate((
            ("attcols", (("qkv0", "qkv1", "qkv2"), ("proj",)), (3 * width, proj_ref.shape[1])),
            ("mbcols", (("inv",), ("point",)), (expanded, expanded)),
        )):
            jobs[name, l] = Columns(
                place, [[jobs[piece, l] for piece in pieces] for pieces in members], [n // n_dp for n in sizes],
                red_send, red_recv, KINDS * JOBS * layers + 2 * l + i, at[f"{name}_outgoing"], at[f"{name}_landed"].at[l],
                whole, at[f"out_{name}"].at[l],
            )

    perm[...] = split_matrix(width)
    row, col = iota((width, width), 0), iota((width, width), 1)
    half = width // 2
    core_of = (row >= half).astype(jnp.int32)
    inner = row - half * core_of
    for q in range(1, n_pipe):
        inner = jnp.where(row - half * core_of >= q * piece_rows, inner + piece_rows, inner)
    rowperm[...] = jnp.where(inner + core_of * piece_rows == col, 1.0, 0.0).astype(BF)
    rmask[...] = row_mask()
    smask[...] = crop_mask(48, 192)

    block_lane, block_row = iota((LANE, LANE), 1), iota((LANE, LANE), 0)
    on_diag = (block_lane >> 5) == (block_row >> 5)
    ones_on_diag = jnp.where(on_diag, 1.0, 0.0)
    diag[...] = jnp.concatenate([ones_on_diag, ones_on_diag], axis=1)
    diag_t[...] = jnp.concatenate([ones_on_diag, ones_on_diag], axis=0)
    tile = jnp.where((iota((32, LANE), 1) & 31) == iota((32, LANE), 0), 1.0, 0.0).astype(BF)

    for t in range(dw_ref.shape[0]):
        taps = dw_ref[t].astype(F32)
        for l in range(layers):
            dwp[l, t : t + 1, :] = taps[l : l + 1]
    for t in range(mdw_ref.shape[0]):
        taps = mdw_ref[t].astype(F32)
        for l in range(layers):
            mdwp[l, t : t + 1, :] = taps[l : l + 1]

    def prepare(l):
        wait_bytes(inv_own.at[l, :, :, :, 0 : 3 * width], load_sem.at[0, l])
        for c in range(wide):
            cut = slice(c * width, (c + 1) * width)
            w_split = mm(inv_own[l, :, :, :, cut].reshape(width, width), perm[...]).astype(BF)
            for part in range(3):
                wp[l, :, lanes(part * wide + c)] = w_split[:, lanes(part)]
        taps = [mm(dwp[l, :, c * width : (c + 1) * width].astype(BF), perm[...]) for c in range(wide)]
        for c in range(wide):
            for part in range(3):
                dwp[l, :, lanes(part * wide + c)] = taps[c][:, lanes(part)]
                rows = jnp.concatenate([group_ref[l, 3 * (4 * c + i) + part] for i in range(HEADS)], axis=0)
                full = jnp.where(on_diag, mm(rows, tile), 0.0)
                blocks_bd[l, part * wide + c] = full.astype(BF)

    spread = spread_matrix(x_ref.shape[0])
    hid[0] = mm(spread, x_ref[...]).astype(BF)
    gnow[...] = mm(spread, ct_ref[...])
    prepare(0)
    pl.semaphore_wait(barrier, n_dp - 1 + 2 * (n_pipe - 1))

    def slot_rows(count):
        return -(-count * wide // SUB) * SUB

    def exchange_start(e, vectors):
        rows = slot_rows(len(vectors))
        for i, vector in enumerate(vectors):
            for j in range(wide):
                row = i * wide + j
                exbuf[e, me, row : row + 1, :] = vector[:, lanes(j)]

        def send(k, carry):
            pltpu.make_async_remote_copy(
                src_ref=exbuf.at[e, me, 0:rows],
                dst_ref=exbuf.at[e, me, 0:rows],
                send_sem=send_sem.at[e],
                recv_sem=recv_sem.at[e],
                device_id={"dp": lax.rem(me + k, n_dp)},
            ).start()
            return carry

        lax.fori_loop(1, n_dp, send, 0)

    def exchange_finish(e, count):
        rows = slot_rows(count)
        wait_bytes(exbuf.at[e, 0 : n_dp - 1, 0:rows], recv_sem.at[e])
        total = exbuf[e, 0, 0:rows]
        for d in range(1, n_dp):
            total = total + exbuf[e, d, 0:rows]
        total = total * (1.0 / total_rows)
        return [
            jnp.concatenate([total[i * wide + j : i * wide + j + 1] for j in range(wide)], axis=1)
            for i in range(count)
        ]

    def attention_forward(l, s):
        joined[l] = mm(hid[s], wp[l]).astype(BF).astype(F32)

        def chunks(c):
            keep = rmask[...]
            columns = [lanes(part * wide + c) for part in range(3)]
            cells = [joined[l, :, at] for at in columns]
            convs = []
            for at, value in zip(columns, cells):
                conv = depthwise(value.reshape(20, SUB, LANE), dwp[l, :, at], 5)
                convs.append((conv.reshape(ROWS, LANE) * keep).astype(BF))
            linears = [mm(conv, blocks_bd[l, part * wide + c]) for part, conv in enumerate(convs)]
            results = []
            for query, key, value in (cells, linears):
                results.append((softplus(query), softplus(key) * keep, value))
            for part in range(3):
                s0[l, :, columns[part]] = convs[part]
                for source in range(2):
                    tvals[l, :, lanes(part * UNITS + source * wide + c)] = results[source][part]

        groups(wide, 1, chunks, True)

        def units(first):
            places = [(first + k, start, size) for k in range(UNIT_STEP) for start, size in BLOCKS]
            inputs = [
                [tvals[l, start : start + size, lanes(u + part * UNITS)] for part in range(3)]
                for u, start, size in places
            ]
            weights = []
            for (_, start, size), (query, key, value) in zip(places, inputs):
                ones = jnp.ones_like(value)
                if start == SMALL:
                    scores = mm(query.astype(BF), stacked(key), NT) * smask[...]
                    weights.append((scores, jnp.concatenate([stacked(value), stacked(ones)], axis=1)))
                else:
                    state = mm(key.astype(BF), joint(value, ones), TN) * diag[...]
                    weights.append((query, state.astype(BF)))
            sums = [mm(left.astype(BF), right) for left, right in weights]
            results = []
            for value in sums:
                inverse = 1.0 / value[:, LANE:]
                results.append((inverse, value[:, :LANE] * inverse))
            for (u, start, size), (inverse, mixed) in zip(places, results):
                rden[l, start : start + size, lanes(u)] = inverse
                mixo[l, start : start + size, lanes(u)] = mixed

        groups(UNITS, UNIT_STEP, units)
        loads[1, l].wait()
        branch[...] = mm(mixo[l].astype(BF), proj_ref[l])

    def expand_forward(l, s):
        loads[2, l].wait()
        pre_u[l] = mm(hid[s], inv_ref[l])

        def chunk(j):
            at = lanes(j)
            pre = pre_u[l, :, at] + ibias_ref[:, at].astype(F32)[l : l + 1]
            value, slope = silu_parts(pre)
            value = value * rmask[...]
            pre_u[l, :, at] = value
            pre_d[l, :, at] = (slope * rmask[...]).astype(BF)
            conv = depthwise(value.reshape(20, SUB, LANE), mdwp[l, :, at], 3).reshape(ROWS, LANE)
            out, out_slope = silu_parts(conv + mbias_ref[:, at].astype(F32)[l : l + 1])
            act[l, :, at] = (out * rmask[...]).astype(BF)
            act_d[l, :, at] = out_slope.astype(BF)

        loop(expanded // LANE, EXPAND_STEP, chunk)
        loads[3, l].wait()
        branch[...] = mm(act[l], point_ref[l])

    gains = gain_ref[...].astype(F32)
    shifts = shift_ref[...].astype(F32)
    last = stages - 1
    for s in range(stages):
        l = s // 2
        if s % 2 == 0:
            attention_forward(l, s)
        else:
            expand_forward(l, s)
        keep = rmask[...]
        for j in range(wide):
            branch[:, lanes(j)] = branch[:, lanes(j)] * keep
        value = branch[...]
        vectors = [column_sum(value), column_sum(value * value)]
        if s == last:
            upstream = gnow[...]
            vectors += [column_sum(upstream * value), column_sum(upstream)]
        exchange_start(s, vectors)
        if s == 0:
            for l in range(1, layers):
                prepare(l)
        hid_t[s] = mm(rowperm[...], hid[s], NT).astype(BF)
        mean, square, *backward = exchange_finish(s, len(vectors))
        scale = lax.rsqrt(square - mean * mean + EPS)
        stats[s : s + 1, :] = scale
        norm = (branch[...] - mean) * scale
        after = hid[s].astype(F32) + gains[s : s + 1] * norm + shifts[s : s + 1]
        for j in range(wide):
            normed[s, :, lanes(j)] = norm[:, lanes(j)] * keep
            hid[s + 1, :, lanes(j)] = (after[:, lanes(j)] * keep).astype(BF)
        if s == last:
            first_cross = scale * (backward[0] - mean * backward[1])
            first_total = backward[1]
            local_cross = scale * (vectors[2] - mean * vectors[3])
            local_sum = vectors[3]

    def small_row(name, l, row, value, at):
        jobs[name, l].stage[row // SUB, row % SUB : row % SUB + 1, at] = value

    def expand_row(l, j, tap, value):
        jobs["mb", l].stage[j // wide * 2 + tap // SUB, tap % SUB : tap % SUB + 1, lanes(j % wide)] = value

    def matrix(name, l, left, right, columns):
        own = jobs[name, l].own
        step = width
        for c in range(columns // step):
            cut = slice(c * step, (c + 1) * step)
            own[:, :, :, cut] = mm(left, right(cut)).astype(BF).reshape(2, n_pipe, piece_rows, step)
        jobs[name, l].start()

    def attention_backward(l, s, grad_branch, pause):
        gmix[...] = mm(grad_branch, proj_ref[l], NT).astype(BF).astype(F32)
        matrix("proj", l, grad_t[...], lambda cut: mixo[l, :, cut].astype(BF), mixo.shape[2])
        pause("t0", l)

        def units(first):
            places = [(first + k, start, size) for k in range(UNIT_STEP) for start, size in BLOCKS]
            inputs = []
            for u, start, size in places:
                rows = slice(start, start + size)
                down = gmix[rows, lanes(u)] * rden[l, rows, lanes(u)]
                inputs.append(
                    [tvals[l, rows, lanes(u + part * UNITS)] for part in range(3)]
                    + [down, -down * mixo[l, rows, lanes(u)]]
                )
            products = []
            for (_, start, size), (query, key, value, down, level) in zip(places, inputs):
                ones = jnp.ones_like(value)
                if start == SMALL:
                    inside = smask[...]
                    query_stack, down_stack = stacked(query), stacked(down)
                    grad_scores = mm(
                        joint(down, level), jnp.concatenate([stacked(value), stacked(ones)], axis=1), NT
                    )
                    grad_scores_t = mm(
                        joint(value, ones), jnp.concatenate([down_stack, stacked(level)], axis=1), NT
                    )
                    scores_t = mm(key.astype(BF), query_stack, NT)
                    products.append((
                        (grad_scores * inside, stacked(key)),
                        (grad_scores_t * inside, query_stack),
                        (scores_t * inside, down_stack),
                    ))
                else:
                    both, slopes = joint(value, ones), joint(down, level)
                    state_t = mm(both, key.astype(BF), TN) * diag_t[...]
                    grad_state_t = mm(slopes, query.astype(BF), TN) * diag_t[...]
                    grad_state = mm(query.astype(BF), down.astype(BF), TN) * diag[:, 0:LANE]
                    products.append((
                        (slopes, state_t.astype(BF)), (both, grad_state_t.astype(BF)), (key, grad_state.astype(BF))
                    ))
            results = []
            for (query, key, *_), pairs in zip(inputs, products):
                grad_query, grad_key, grad_value = (mm(left.astype(BF), right) for left, right in pairs)
                results.append(
                    (grad_query * (1.0 - jnp.exp(-query)), grad_key * (1.0 - jnp.exp(-key)), grad_value)
                )
            for (u, start, size), grads in zip(places, results):
                for part, grad in enumerate(grads):
                    dvals[start : start + size, lanes(u + part * UNITS)] = grad

        groups(UNITS, UNIT_STEP, units)
        pause("t2", l)

        def chunks(c):
            keep = rmask[...]
            columns = [lanes(part * wide + c) for part in range(3)]
            slots = [part * UNITS + c for part in range(3)]
            grads = [dvals[:, lanes(slot + wide)].astype(BF) for slot in slots]
            direct = [dvals[:, lanes(slot)] for slot in slots]
            cells = [joined[l, :, at].reshape(20, SUB, LANE) for at in columns]
            convs = [
                mm(grad, blocks_bd[l, part * wide + c], NT).reshape(20, SUB, LANE) for part, grad in enumerate(grads)
            ]
            blocks = [mm(s0[l, :, at], grad, TN) * diag[:, 0:LANE] for at, grad in zip(columns, grads)]
            taps_of, grads_of = [], []
            for part, conv in enumerate(convs):
                back = depthwise(conv, dwp[l, :, columns[part]], 5, flip=True).reshape(ROWS, LANE)
                taps_of.append(depthwise_taps(cells[part], conv, 5))
                grads_of.append((direct[part] + back * keep).astype(BF))
            for at, block, taps, joined_grad in zip(columns, blocks, taps_of, grads_of):
                block = block[0:32] + block[32:64] + block[64:96] + block[96:128]
                jobs["att", l].stage[4:8, :, at] = block.reshape(4, SUB, LANE)
                for tap, row in enumerate(taps):
                    small_row("att", l, tap, row, at)
                mid[:, at] = joined_grad
            natural = mm(jnp.concatenate(grads_of, axis=1), perm[...], NT).astype(BF)
            matrix(f"qkv{c}", l, hid_t[s], lambda cut: natural, width)
            pause(f"c{c}", l)

        groups(wide, 1, chunks, True)
        jobs["att", l].start()
        pause("t5", l)
        grad_hidden = mm(mid[:, : 3 * width], wp[l], NT)

        def gradients():
            pass

        return grad_hidden, gradients

    def expand_backward(l, s, grad_branch, pause):
        gact[:, 0:expanded] = mm(grad_branch, point_ref[l], NT).astype(BF).astype(F32)
        matrix("point", l, grad_t[...], lambda cut: act[l, :, cut], expanded)
        pause("m0", l)

        def chunk(j):
            at = lanes(j)
            grad_conv = gact[:, at] * act_d[l, :, at].astype(F32)
            expand_row(l, j, 9, column_sum(grad_conv))
            cells = pre_u[l, :, at].reshape(20, SUB, LANE)
            grad_conv = grad_conv.reshape(20, SUB, LANE)
            for tap, row in enumerate(depthwise_taps(cells, grad_conv, 3)):
                expand_row(l, j, tap, row)
            back = depthwise(grad_conv, mdwp[l, :, at], 3, flip=True).reshape(ROWS, LANE)
            grad_pre = (back * pre_d[l, :, at].astype(F32)).astype(BF)
            mid[:, at] = grad_pre
            expand_row(l, j, 10, column_sum(grad_pre.astype(F32)))

        loop(expanded // LANE, EXPAND_STEP, chunk)
        jobs["mb", l].start()
        pause("m2", l)
        grad_hidden = mm(mid[...], inv_ref[l], NT)

        def gradients():
            matrix("inv", l, hid_t[s], lambda cut: mid[:, cut], expanded)

        return grad_hidden, gradients

    def pause(moment, l):
        for step in PLAN.get((moment, l), ()):
            name, number, method = step.split(".")
            getattr(jobs[name, int(number)], method)()

    for s in range(stages - 1, -1, -1):
        l = s // 2
        keep = rmask[...]
        if s == last:
            cross, total = first_cross, first_total
        else:
            cross, total = exchange_finish(stages + s, 2)
        pause("begin", s)
        if s % 2 == 0:
            small_row("att", l, 25, local_cross, slice(0, width))
            small_row("att", l, 25, local_sum, slice(width, 2 * width))
        else:
            small_row("mb", l, 11, local_cross, slice(0, width))
            small_row("mb", l, 16 + 11, local_sum, slice(0, width))
        grad_branch = (stats[s : s + 1, :] * gains[s : s + 1]) * (gnow[...] - total - normed[s] * cross)
        grad_branch = jnp.concatenate(
            [grad_branch[:, lanes(j)] * keep for j in range(wide)], axis=1
        ).astype(BF)
        grad_t[...] = mm(rowperm[...], grad_branch, NT).astype(BF)
        back = attention_backward if s % 2 == 0 else expand_backward
        grad_hidden, gradients = back(l, s, grad_branch, pause)
        after = (gnow[...] + grad_hidden).astype(BF).astype(F32)
        gnow[...] = after
        if s > 0:
            local_cross, local_sum = column_sum(after * normed[s - 1]), column_sum(after)
            exchange_start(stages + s - 1, [local_cross, local_sum])
        pause("sent", s)
        gradients()
        pause("done", s)
        if s == last:
            at["out_x"][...] = mm(spread, hid[stages], TN).astype(BF)

    at["out_g"][...] = mm(spread, gnow[...].astype(BF), TN).astype(BF)
    for job in jobs.values():
        if isinstance(job, Reduction):
            job.drain()
    for e in range(2 * stages - 1):
        rows = slot_rows(4 if e == last else 2)
        wait_bytes(exbuf.at[e, 0 : n_dp - 1, 0:rows], send_sem.at[e])


def unsplit(value, wide):
    lane = iota((1, LANE), 1) >> 5
    columns = []
    for c in range(wide):
        parts = [value[:, lanes(part * wide + c)] for part in range(3)]
        for k in range(3):
            column = None
            for slot in range(4):
                index = 4 * k + slot
                moved = pltpu.roll(parts[index % 3], (slot - index // 3) % 4 * 32, 1)
                column = moved if column is None else jnp.where(lane == slot, moved, column)
            columns.append(column)
    return columns


def arrange(layers, wide, shares, x_in, g_in, attcols_in, mbcols_in, att_in, mb_in,
            x_out, g_out, qkv_out, proj_out, inv_out, point_out, dw_out, group_out, ibias_out, mdw_out, mbias_out,
            gain_out, shift_out):
    width = wide * LANE
    share_qkv, share_proj, share_inv, share_point = shares
    x_out[...] = x_in[...]
    g_out[...] = g_in[...]
    taps, mtaps = dw_out.shape[0], mdw_out.shape[0]
    for l in range(layers):
        rows = attcols_in.shape[1]
        values = []
        for value, share in ((attcols_in[l], share_qkv), (mbcols_in[l], share_inv)):
            value = jnp.concatenate([value, jnp.zeros((padded(rows) - rows, value.shape[1]), F32)], axis=0)
            values += [value, pltpu.roll(value, value.shape[1] - share, 1)]
        qkv_out[l] = jnp.transpose(values[0])[0:share_qkv, 0:rows]
        proj_out[l] = jnp.transpose(values[1])[0:share_proj, 0:rows]
        inv_out[l] = values[2][0:rows, 0:share_inv]
        point_out[l] = jnp.transpose(values[3])[0:share_point, 0:rows]
        natural = unsplit(att_in[l], wide)
        for j, column in enumerate(natural):
            for t in range(taps):
                dw_out[t, l : l + 1, lanes(j)] = column[t : t + 1]
            group_out[l, :, lanes(j)] = column[32:64]
        for block in range(4):
            cut = slice(block * width, (block + 1) * width)
            rows = mb_in[l, 16 * block : 16 * block + 16]
            for t in range(mtaps):
                mdw_out[t, l : l + 1, cut] = rows[t : t + 1]
            mbias_out[l : l + 1, cut] = rows[9:10]
            ibias_out[l : l + 1, cut] = rows[10:11]
        gain_out[2 * l : 2 * l + 1, :] = att_in[l, 25:26, 0:width]
        shift_out[2 * l : 2 * l + 1, :] = att_in[l, 25:26, width : 2 * width]
        gain_out[2 * l + 1 : 2 * l + 2, :] = mb_in[l, 11:12, :]
        shift_out[2 * l + 1 : 2 * l + 2, :] = mb_in[l, 27:28, :]


def padded(columns):
    return -(-columns // LANE) * LANE


def body(
    activations, cotangent, att_qkv, att_dw, att_group, att_proj, mb_inv, mb_inv_bias, mb_dw, mb_dw_bias, mb_point,
    bn_gain, bn_bias,
):
    n_dp, n_pipe = lax.axis_size("dp"), lax.axis_size("pipe")
    layers, width, joined_width = att_qkv.shape
    mixed_width = att_proj.shape[1]
    expanded = mb_inv.shape[2]
    tokens = activations.shape[2]
    stages = 2 * layers
    rows = width // 2 // n_pipe
    vmem = pl.BlockSpec(memory_space=pltpu.VMEM)
    hbm = pl.BlockSpec(memory_space=pl.ANY)
    columns = {"qkv0": width, "qkv1": width, "qkv2": width, "proj": mixed_width, "inv": expanded, "point": expanded}
    small_columns = {"att": joined_width, "mb": width}
    outs = {
        "out_x": jax.ShapeDtypeStruct((tokens, width), BF),
        "out_g": jax.ShapeDtypeStruct((tokens, width), BF),
    }
    scratch = {
        "proj": pltpu.VMEM(att_proj.shape, BF),
        "inv": pltpu.VMEM(mb_inv.shape, BF),
        "point": pltpu.VMEM(mb_point.shape, BF),
        "perm": pltpu.VMEM((width, width), BF),
        "rowperm": pltpu.VMEM((width, width), BF),
        "wp": pltpu.VMEM((layers, width, joined_width), BF),
        "blocks_bd": pltpu.VMEM((layers, joined_width // LANE, LANE, LANE), BF),
        "dwp": pltpu.VMEM((layers, 32, joined_width), F32),
        "mdwp": pltpu.VMEM((layers, 16, expanded), F32),
        "rmask": pltpu.VMEM((ROWS, LANE), F32),
        "smask": pltpu.VMEM((48, 192), F32),
        "diag": pltpu.VMEM((LANE, 2 * LANE), F32),
        "diag_t": pltpu.VMEM((2 * LANE, LANE), F32),
        "hid": pltpu.VMEM((stages + 1, ROWS, width), BF),
        "hid_t": pltpu.VMEM((stages, width, ROWS), BF),
        "grad_t": pltpu.VMEM((width, ROWS), BF),
        "normed": pltpu.VMEM((stages, ROWS, width), F32),
        "mixo": pltpu.VMEM((layers, ROWS, mixed_width), F32),
        "rden": pltpu.VMEM((layers, ROWS, mixed_width), F32),
        "tvals": pltpu.VMEM((layers, ROWS, 3 * mixed_width), F32),
        "joined": pltpu.VMEM((layers, ROWS, joined_width), F32),
        "s0": pltpu.VMEM((layers, ROWS, joined_width), BF),
        "dvals": pltpu.VMEM((ROWS, 3 * mixed_width), F32),
        "gmix": pltpu.VMEM((ROWS, mixed_width), F32),
        "pre_u": pltpu.VMEM((layers, ROWS, expanded), F32),
        "pre_d": pltpu.VMEM((layers, ROWS, expanded), BF),
        "act": pltpu.VMEM((layers, ROWS, expanded), BF),
        "act_d": pltpu.VMEM((layers, ROWS, expanded), BF),
        "mid": pltpu.VMEM((ROWS, expanded), BF),
        "branch": pltpu.VMEM((ROWS, width), F32),
        "gnow": pltpu.VMEM((ROWS, width), F32),
        "stats": pltpu.VMEM((8, width), F32),
        "exbuf": pltpu.VMEM((2 * stages - 1, n_dp, 2 * SUB, LANE), F32),
        "whole": pltpu.VMEM((rows, 2 * expanded), F32),
        "send_sem": pltpu.SemaphoreType.DMA((2 * stages - 1,)),
        "recv_sem": pltpu.SemaphoreType.DMA((2 * stages - 1,)),
        "load_sem": pltpu.SemaphoreType.DMA((4, layers)),
        "red_send": pltpu.SemaphoreType.DMA((KINDS * JOBS * layers + 2 * layers,)),
        "red_recv": pltpu.SemaphoreType.DMA((KINDS * JOBS * layers + 2 * layers,)),
    }
    for name in MATRICES:
        n = columns[name]
        scratch[f"{name}_own"] = pltpu.VMEM((layers, 2, n_pipe, rows, n), BF)
        scratch[f"{name}_pair"] = pltpu.VMEM((layers, n_pipe, rows, n), BF)
        scratch[f"{name}_first"] = pltpu.VMEM((layers, 2, rows, n), BF)
        scratch[f"{name}_second"] = pltpu.VMEM((layers, rows, n), BF)
    shares = tuple(n // n_dp for n in (joined_width, mixed_width, expanded, expanded))
    for name, share in (("attcols", padded(shares[0] + shares[1])), ("mbcols", padded(shares[2] + shares[3]))):
        outs[f"out_{name}"] = jax.ShapeDtypeStruct((layers, 2 * rows, share), F32)
        scratch[f"{name}_outgoing"] = pltpu.VMEM((n_dp, rows, share), BF)
        scratch[f"{name}_landed"] = pltpu.VMEM((layers, n_dp, rows, share), BF)
    for name in SMALLS:
        n = small_columns[name]
        outs[f"out_{name}"] = jax.ShapeDtypeStruct((layers, 8 * SUB, n), F32)
        half, rows_in, kind = (padded(n // 2), 2 * SUB, BF) if name == "att" else (n, SUB, F32)
        scratch[f"{name}_stage"] = pltpu.VMEM((8, SUB, n), F32)
        scratch[f"{name}_own"] = pltpu.VMEM((layers, 2, n_pipe, rows_in, half), kind)
        scratch[f"{name}_pair"] = pltpu.VMEM((layers, n_pipe, rows_in, half), kind)
        scratch[f"{name}_first"] = pltpu.VMEM((layers, 2, rows_in, half), kind)
        scratch[f"{name}_second"] = pltpu.VMEM((layers, rows_in, half), kind)
        scratch[f"{name}_along"] = pltpu.VMEM((layers, n_dp // 2, rows_in, half), kind)
        scratch[f"{name}_everywhere"] = pltpu.VMEM((layers, 2 * n_pipe, rows_in, half), kind)
    results = pl.pallas_call(
        functools.partial(kernel, n_dp, n_pipe, 13, tuple(outs) + tuple(scratch)),
        out_shape=tuple(outs.values()),
        in_specs=[vmem, vmem, hbm, vmem, vmem, hbm, hbm, vmem, vmem, vmem, hbm, vmem, vmem],
        out_specs=(vmem,) * len(outs),
        scratch_shapes=list(scratch.values()),
        compiler_params=pltpu.CompilerParams(
            collective_id=0, has_side_effects=True, vmem_limit_bytes=63 * 1024 * 1024
        ),
    )(
        activations.reshape(tokens, width),
        cotangent.reshape(tokens, width),
        att_qkv,
        att_dw.transpose(1, 0, 2),
        att_group,
        att_proj,
        mb_inv,
        mb_inv_bias,
        mb_dw.transpose(1, 0, 2),
        mb_dw_bias,
        mb_point,
        bn_gain,
        bn_bias,
    )
    taps, mtaps = att_dw.shape[1], mb_dw.shape[1]
    arranged = pl.pallas_call(
        functools.partial(arrange, layers, width // LANE, shares),
        out_shape=(
            jax.ShapeDtypeStruct((tokens, width), BF),
            jax.ShapeDtypeStruct((tokens, width), BF),
            jax.ShapeDtypeStruct((layers, shares[0], 2 * rows), F32),
            jax.ShapeDtypeStruct((layers, shares[1], 2 * rows), F32),
            jax.ShapeDtypeStruct((layers, 2 * rows, shares[2]), F32),
            jax.ShapeDtypeStruct((layers, shares[3], 2 * rows), F32),
            jax.ShapeDtypeStruct((taps, layers, joined_width), F32),
            jax.ShapeDtypeStruct((layers, 32, joined_width), F32),
            jax.ShapeDtypeStruct((layers, expanded), F32),
            jax.ShapeDtypeStruct((mtaps, layers, expanded), F32),
            jax.ShapeDtypeStruct((layers, expanded), F32),
            jax.ShapeDtypeStruct((stages, width), F32),
            jax.ShapeDtypeStruct((stages, width), F32),
        ),
        in_specs=[vmem] * 6,
        out_specs=(vmem,) * 13,
    )(*results)
    x_out, g_out, qkv, proj, inv, point, dw, group, ibias, mdw, mbias, gain, shift = arranged
    groups, size = att_group.shape[1], att_group.shape[2]
    return (
        x_out.reshape(activations.shape),
        g_out.reshape(activations.shape),
        qkv.transpose(0, 2, 1),
        dw.transpose(1, 0, 2),
        group.reshape(layers, size, groups, size).transpose(0, 2, 1, 3),
        proj,
        inv,
        ibias,
        mdw.transpose(1, 0, 2),
        mbias,
        point,
        gain,
        shift,
    )


def solution(mesh):
    placed = (P("pipe", "dp", None, None), P("pipe", "dp", None, None)) + (P(),) * 11
    return jax.shard_map(
        body,
        mesh=mesh,
        in_specs=placed,
        out_specs=(
            P("pipe", "dp", None, None),
            P("pipe", "dp", None, None),
            P(None, "pipe", "dp"),
            P(),
            P(),
            P(None, "dp", "pipe"),
            P(None, "pipe", "dp"),
            P(),
            P(),
            P(),
            P(None, "dp", "pipe"),
            P(),
            P(),
        ),
        check_vma=False,
    )
```

```python
import functools
from types import SimpleNamespace

import jax
import jax.numpy as jnp
from jax import lax
from jax.experimental import pallas as pl
from jax.experimental.pallas import tpu as pltpu
from jax.sharding import PartitionSpec as P

F32 = jnp.float32
BF = jnp.bfloat16
EPS = 1e-05
LANE = 128
SUB = 8
ROWS = 160
SMALL = 112
BLOCKS = ((0, 56), (56, 56), (112, 48))
HEADS = 4
UNITS = 6
UNIT_STEP = 6
EXPAND_STEP = 1
NN = (((1,), (0,)), ((), ()))
NT = (((1,), (1,)), ((), ()))
TN = (((0,), (0,)), ((), ()))


def mm(a, b, dims=NN):
    return lax.dot_general(a, b, dims, preferred_element_type=F32)


def iota(shape, dim):
    return lax.broadcasted_iota(jnp.int32, shape, dim)


def lanes(j):
    if isinstance(j, int):
        return slice(j * LANE, (j + 1) * LANE)
    return pl.ds(pl.multiple_of(j * LANE, LANE), LANE)


def spread_matrix(tokens):
    row, col = iota((ROWS, tokens), 0), iota((ROWS, tokens), 1)
    crop = (row >= 56).astype(jnp.int32)
    inner = row - 56 * crop
    big = crop * 49 + (inner >> 3) * 7 + (inner & 7)
    small_row = row - SMALL
    pair = (small_row >= 24).astype(jnp.int32)
    inner = small_row - 24 * pair
    small = 98 + (pair * 2 + ((inner & 7) >> 2)) * 9 + (inner >> 3) * 3 + (inner & 3)
    is_big = row < SMALL
    valid = jnp.where(is_big, row & 7, (row & 3) + 4) < 7
    hit = (jnp.where(is_big, big, small) == col) & valid
    return jnp.where(hit, 1.0, 0.0).astype(BF)


def split_matrix(width):
    row, col = iota((width, width), 0), iota((width, width), 1)
    head = (row >= 96).astype(jnp.int32) + (row >= 192).astype(jnp.int32) + (row >= 288).astype(jnp.int32)
    rest = row - 96 * head
    part = (rest >= 32).astype(jnp.int32) + (rest >= 64).astype(jnp.int32)
    target = part * 128 + head * 32 + (rest - 32 * part)
    return jnp.where(target == col, 1.0, 0.0).astype(BF)


def row_mask(width=LANE):
    row = iota((ROWS, width), 0)
    valid = jnp.where(row < SMALL, row & 7, (row & 3) + 4) < 7
    return jnp.where(valid, 1.0, 0.0)


def crop_mask(rows, columns):
    row, col = iota((rows, columns), 0), iota((rows, columns), 1)
    for step in (3, 2, 1):
        col = jnp.where(col >= rows * step, col - rows * step, col)
    row_crop = (row >= 24).astype(jnp.int32) * 2 + ((row & 7) >> 2)
    col_crop = (col >= 24).astype(jnp.int32) * 2 + ((col & 7) >> 2)
    return jnp.where(row_crop == col_crop, 1.0, 0.0)


def head_masks():
    lane = iota((1, LANE), 1)
    return [jnp.where((lane >= 32 * h) & (lane < 32 * h + 32), 1.0, 0.0) for h in range(HEADS)]


def stacked(value):
    return jnp.concatenate([value * mask for mask in head_masks()], axis=0).astype(BF)


def joint(*values):
    return jnp.concatenate(values, axis=1).astype(BF)


def shifted(tokens, step):
    if step == 0:
        return tokens
    moved = pltpu.roll(tokens, (-step) % SUB, 1)
    if abs(step) == 1:
        return moved
    at = iota((1, SUB, LANE), 1)
    if tokens.shape[0] > 6:
        wrong = (at == 0) if step < 0 else (at == 6)
    else:
        wrong = ((at & 3) == 0) if step < 0 else ((at & 3) == 2)
    return jnp.where(wrong, 0.0, moved)


def tap_pairs(side, step):
    return range(max(0, -step), min(side, side - step))


def crops(tokens):
    return ((tokens[:14], 7), (tokens[14:], 3))


def depthwise(tokens, taps, reach, flip=False):
    margin = reach // 2
    parts = []
    for cells, side in crops(tokens):
        sums = [None] * side
        for dj in range(-margin, margin + 1):
            moved = shifted(cells, dj).reshape(2, side, SUB, LANE)
            for di in range(-margin, margin + 1):
                tap = (margin - di) * reach + margin - dj if flip else (margin + di) * reach + margin + dj
                weight = taps[tap : tap + 1, :].reshape(1, 1, LANE)
                for a in tap_pairs(side, di):
                    term = moved[:, a + di] * weight
                    sums[a] = term if sums[a] is None else sums[a] + term
        parts.append(jnp.stack(sums, axis=1).reshape(2 * side, SUB, LANE))
    return jnp.concatenate(parts, axis=0)


def depthwise_taps(tokens, grads, reach):
    margin = reach // 2
    totals = {}
    for (cells, side), (grad_cells, _) in zip(crops(tokens), crops(grads)):
        grad_cells = grad_cells.reshape(2, side, SUB, LANE)
        for dj in range(-margin, margin + 1):
            moved = shifted(cells, dj).reshape(2, side, SUB, LANE)
            for di in range(-margin, margin + 1):
                tap = (margin + di) * reach + margin + dj
                total = totals.get(tap)
                for a in tap_pairs(side, di):
                    term = moved[:, a + di] * grad_cells[:, a]
                    total = term if total is None else total + term
                if total is not None:
                    totals[tap] = total
    return [jnp.sum(jnp.sum(totals[tap], axis=0), axis=0, keepdims=True) for tap in range(reach * reach)]


def softplus(x):
    small = jnp.exp(-jnp.abs(x))
    return jnp.maximum(x, 0.0) + jnp.where(small < 1e-3, small * (1.0 - 0.5 * small), jnp.log(1.0 + small))


def silu_parts(x):
    gate = 0.5 * jnp.tanh(0.5 * x) + 0.5
    value = x * gate
    return value, gate + value * (1.0 - gate)


def loop(count, step, body):
    def several(i, carry):
        for k in range(step):
            body(i * step + k)
        return carry

    if step == count:
        several(0, 0)
    else:
        lax.fori_loop(0, count // step, several, 0)


def groups(count, step, body, unroll=False):
    if step == count or unroll:
        for first in range(0, count, step):
            body(first)
    else:
        lax.fori_loop(0, count // step, lambda i, carry: (body(i * step), carry)[1], 0)


def column_sum(value):
    return jnp.sum(value, axis=0, keepdims=True)


def wait_bytes(ref, sem):
    pltpu.make_async_copy(ref, ref, sem).wait()


class Reduction:
    def __init__(self, direct, place, own, pair, first, second, send_sem, recv_sem, base):
        self.direct = direct
        self.place, self.own, self.pair, self.first, self.second = place, own, pair, first, second
        self.send_sem, self.recv_sem, self.base = send_sem, recv_sem, base

    def copy(self, source, target, kind, pipe, dp):
        return pltpu.make_async_remote_copy(
            src_ref=source,
            dst_ref=target,
            send_sem=self.send_sem.at[self.base + kind],
            recv_sem=self.recv_sem.at[self.base + kind],
            device_id={"pipe": pipe, "dp": dp},
        )

    def to_pair(self):
        at = self.place
        return self.copy(self.own.at[1 - at.core], self.pair, 0, at.pipe, at.dp + 1 - 2 * at.core)

    def to_first(self, bit):
        at = self.place
        peer = at.pipe + (1 + at.core) * (1 - 2 * at.bit1)
        return self.copy(self.own.at[at.core, at.slab(1 - at.bit1, bit)], self.first.at[bit], 1 + bit, peer, at.dp)

    def to_second(self):
        at = self.place
        peer = at.pipe + (2 - at.core) * (1 - 2 * at.bit2)
        return self.copy(self.own.at[at.core, at.slab(at.bit1, 1 - at.bit2)], self.second, 3, peer, at.dp)

    def to_segment(self, k):
        at = self.place
        peer = lax.rem(at.pipe + k, self.pair.shape[0])
        target = self.second if k == 3 else self.first.at[k - 1]
        return self.copy(self.own.at[at.core, peer], target, k, peer, at.dp)

    def start(self):
        self.to_pair().start()

    def step1(self):
        at = self.place
        self.to_pair().wait_recv()
        if self.direct:
            for k in (2, 1, 3):
                slab = lax.rem(at.pipe + k, self.pair.shape[0])
                self.own[at.core, slab] = self.own[at.core, slab] + self.pair[slab]
                self.to_segment(k).start()
            return
        for bit in range(2):
            slab = at.slab(1 - at.bit1, bit)
            self.own[at.core, slab] = self.own[at.core, slab] + self.pair[slab]
            self.to_first(bit).start()

    def step2(self):
        if self.direct:
            return
        at = self.place
        for bit in range(2):
            self.to_first(bit).wait_recv()
        bit = 1 - at.bit2
        slab = at.slab(at.bit1, bit)
        total = self.own[at.core, slab].astype(F32) + self.pair[slab].astype(F32) + self.first[bit].astype(F32)
        self.own[at.core, slab] = total.astype(self.own.dtype)
        self.to_second().start()

    def part(self):
        at = self.place
        slab = at.pipe
        if self.direct:
            total = self.own[at.core, slab].astype(F32) + self.pair[slab].astype(F32)
            for k in (1, 2, 3):
                self.to_segment(k).wait_recv()
                total = total + (self.second[...] if k == 3 else self.first[k - 1]).astype(F32)
            return total
        self.to_second().wait_recv()
        total = self.own[at.core, slab].astype(F32) + self.pair[slab].astype(F32)
        return total + self.first[at.bit2].astype(F32) + self.second[...].astype(F32)

    def do(self, step):
        (None, self.step1, self.step2, self.step3, self.step4, self.finish)[step]()

    step3 = step4 = finish = None

    def drain(self):
        self.to_pair().wait_send()
        if self.direct:
            rest = [self.to_segment(k) for k in (1, 2, 3)]
        else:
            rest = [self.to_first(0), self.to_first(1), self.to_second()]
        for made in rest:
            made.wait_send()


class Place:
    def __init__(self):
        self.pipe, self.dp = lax.axis_index("pipe"), lax.axis_index("dp")
        self.core = lax.rem(self.dp, 2)
        low, high = lax.rem(self.pipe, 2), self.pipe // 2
        self.bit1 = low * (1 - self.core) + high * self.core
        self.bit2 = high * (1 - self.core) + low * self.core

    def slab(self, bit1, bit2):
        return bit1 * (1 + self.core) + bit2 * (2 - self.core)


class Columns:
    def __init__(self, place, matrices, shares, send_sem, recv_sem, base, outgoing, landed, whole, result):
        self.place, self.matrices, self.shares = place, matrices, shares
        self.send_sem, self.recv_sem = send_sem.at[base], recv_sem.at[base]
        self.outgoing, self.landed, self.whole, self.result = outgoing, landed, whole, result

    def do(self, step):
        if step == SEND:
            self.send()
        else:
            self.finish()

    def send(self):
        at = self.place
        n_dp, rows, width = self.outgoing.shape
        spans, start = [], 0
        for pieces in self.matrices:
            first = start
            for piece in pieces:
                size = piece.own.shape[3]
                self.whole[:, start : start + size] = piece.part()
                start += size
            spans.append((first, start - first))
        lane = iota((1, width), 1)

        def cut(d, carry):
            result, target = None, 0
            for (first, columns), share in zip(spans, self.shares):
                cover = min(max(padded(share) + LANE, width), columns)
                offset = d * share
                base = jnp.minimum(offset // LANE, (columns - cover) // LANE) * LANE
                piece = self.whole[:, pl.ds(pl.multiple_of(first + base, LANE), cover)]
                piece = pltpu.roll(piece, lax.rem(cover + target - (offset - base), cover), 1)[:, 0:width]
                result = piece if result is None else jnp.where(lane < target, result, piece)
                target += share
            self.outgoing[d] = result.astype(BF)
            return carry

        lax.fori_loop(0, n_dp, cut, 0)

        def push(k, carry):
            peer = lax.rem(at.dp + k, n_dp)
            pltpu.make_async_remote_copy(
                src_ref=self.outgoing.at[peer],
                dst_ref=self.landed.at[at.dp],
                send_sem=self.send_sem,
                recv_sem=self.recv_sem,
                device_id={"dp": peer},
            ).start()
            return carry

        lax.fori_loop(1, n_dp, push, 0)
        self.landed[at.dp] = self.outgoing[at.dp]

    def finish(self):
        n_dp, rows, _ = self.outgoing.shape
        wait_bytes(self.landed.at[0 : n_dp - 1], self.recv_sem)
        for core in range(2):
            total = self.landed[core].astype(F32)
            for d in range(core + 2, n_dp, 2):
                total = total + self.landed[d].astype(F32)
            self.result[core * rows : (core + 1) * rows, :] = total
        wait_bytes(self.outgoing.at[0 : n_dp - 1], self.send_sem)


class Small(Reduction):
    def __init__(self, *args):
        *rest, self.stage, self.along, self.everywhere, self.result = args
        super().__init__(*rest)

    def start(self):
        slabs, _, columns = self.stage.shape
        half = self.own.shape[3]
        for q in range(slabs):
            if half == columns:
                self.own[q // self.own.shape[1], q % self.own.shape[1]] = self.stage[q]
                continue
            low, high = self.stage[q, :, 0:half], self.stage[q, :, half:columns]
            if columns < 2 * half:
                high = jnp.concatenate([high, jnp.zeros((SUB, 2 * half - columns), F32)], axis=1)
            self.own[q // self.own.shape[1], q % self.own.shape[1]] = jnp.concatenate([low, high], axis=0).astype(BF)
        super().start()

    def step3(self):
        at = self.place
        pairs = self.along.shape[0]
        mine = at.dp // 2
        self.along[mine] = self.part().astype(self.along.dtype)

        def send(k, carry):
            peer = lax.rem(mine + k, pairs)
            pltpu.make_async_remote_copy(
                src_ref=self.along.at[mine],
                dst_ref=self.along.at[mine],
                send_sem=self.send_sem.at[self.base + 4],
                recv_sem=self.recv_sem.at[self.base + 4],
                device_id={"dp": peer * 2 + at.core},
            ).start()
            return carry

        lax.fori_loop(1, pairs, send, 0)

    def step4(self):
        at = self.place
        pairs = self.along.shape[0]
        wait_bytes(self.along.at[0 : pairs - 1], self.recv_sem.at[self.base + 4])
        total = self.along[0].astype(F32)
        for d in range(1, pairs):
            total = total + self.along[d].astype(F32)
        parts = self.everywhere.shape[0]
        segments = parts // 2
        mine = at.core * segments + at.pipe
        self.everywhere[mine] = total.astype(self.everywhere.dtype)

        def send(k, carry):
            peer = lax.rem(mine + k, parts)
            pltpu.make_async_remote_copy(
                src_ref=self.everywhere.at[mine],
                dst_ref=self.everywhere.at[mine],
                send_sem=self.send_sem.at[self.base + 5],
                recv_sem=self.recv_sem.at[self.base + 5],
                device_id={"pipe": lax.rem(peer, segments), "dp": at.dp - at.core + peer // segments},
            ).start()
            return carry

        lax.fori_loop(1, parts, send, 0)

    def finish(self):
        parts = self.everywhere.shape[0]
        wait_bytes(self.everywhere.at[0 : parts - 1], self.recv_sem.at[self.base + 5])
        for q in range(parts):
            value = self.everywhere[q].astype(F32)
            half = value.shape[1]
            self.result[q * SUB : (q + 1) * SUB, 0:half] = value[0:SUB]
            if half < self.result.shape[1]:
                self.result[q * SUB : (q + 1) * SUB, half:] = value[SUB:, 0 : self.result.shape[1] - half]

    def drain(self):
        super().drain()
        pairs, parts = self.along.shape[0], self.everywhere.shape[0]
        wait_bytes(self.along.at[0 : pairs - 1], self.send_sem.at[self.base + 4])
        wait_bytes(self.everywhere.at[0 : parts - 1], self.send_sem.at[self.base + 5])


QKV, PROJ, INV, POINT, ATT, MB, ATT_COLUMNS, MB_COLUMNS = 0, 3, 4, 5, 6, 7, 8, 9
MATRICES, SMALLS = 6, 2
JOBS = MATRICES + SMALLS
DIRECT = ()
SEND, FINISH = 0, 5
BEGIN, M_START, M_CHUNKS, T_START, T_UNITS, T_CHUNKS, SENT, DONE = 0, 1, 2, 3, 4, 5, 8, 9
PLAN = {
    (M_CHUNKS, 3): ((POINT, 1, 1),),
    (DONE, 3): ((MB, 1, 1), (INV, 1, 1),),
    (BEGIN, 2): (),
    (T_START, 2): ((POINT, 1, 2), (MB, 1, 2),),
    (T_UNITS, 2): ((PROJ, 1, 1),),
    (T_CHUNKS, 2): (),
    (T_CHUNKS + 1, 2): (),
    (T_CHUNKS + 2, 2): ((INV, 1, 2), (QKV, 1, 1),),
    (SENT, 2): ((MB, 1, 3), (QKV + 1, 1, 1),),
    (DONE, 2): ((QKV + 2, 1, 1), (PROJ, 1, 2), (ATT, 1, 1),),
    (BEGIN, 1): ((MB_COLUMNS, 1, SEND), (QKV, 1, 2),),
    (M_START, 1): ((QKV + 1, 1, 2), (QKV + 2, 1, 2), (ATT, 1, 2),),
    (M_CHUNKS, 1): ((POINT, 0, 1), (MB, 1, 4),),
    (SENT, 1): ((ATT, 1, 3), (ATT_COLUMNS, 1, SEND),),
    (DONE, 1): ((MB, 0, 1), (INV, 0, 1), (MB, 1, FINISH),),
    (BEGIN, 0): ((MB_COLUMNS, 1, FINISH),),
    (T_START, 0): ((POINT, 0, 2), (MB, 0, 2), (ATT, 1, 4),),
    (T_UNITS, 0): ((PROJ, 0, 1),),
    (T_CHUNKS, 0): ((MB, 0, 3),),
    (T_CHUNKS + 1, 0): ((INV, 0, 2), (QKV, 0, 1),),
    (T_CHUNKS + 2, 0): ((QKV + 1, 0, 1), (ATT_COLUMNS, 1, FINISH), (ATT, 1, FINISH),),
    (SENT, 0): (
        (QKV + 2, 0, 1), (ATT, 0, 1), (PROJ, 0, 2), (MB, 0, 4), (QKV, 0, 2), (MB_COLUMNS, 0, SEND),
    ),
    (DONE, 0): (
        (ATT, 0, 2), (QKV + 1, 0, 2), (QKV + 2, 0, 2), (ATT, 0, 3), (ATT_COLUMNS, 0, SEND), (ATT, 0, 4),
        (MB, 0, FINISH), (MB_COLUMNS, 0, FINISH),
        (ATT_COLUMNS, 0, FINISH), (ATT, 0, FINISH),
    ),
}
KINDS = 6


def kernel(n_dp, n_pipe, count_in, names, *refs):
    (
        x_ref, ct_ref, qkv_hbm, dw_ref, group_ref, proj_hbm, inv_hbm, ibias_ref, mdw_ref, mbias_ref, point_hbm,
        gain_ref, shift_ref,
    ) = refs[:count_in]
    refs_of = dict(zip(names, refs[count_in:]))
    at = SimpleNamespace(**{name: ref for name, ref in refs_of.items() if isinstance(name, str)})
    (
        inv_own, proj_ref, inv_ref, point_ref, perm, rowperm, wp, blocks_bd, dwp, mdwp, rmask, smask, diag, diag_t,
        hid, hid_t, grad_t, normed, mixo, rden, tvals, joined, s0, dvals, gmix, pre_u, pre_d, act, act_d, mid,
        gact, branch, gnow, stats, exbuf, send_sem, recv_sem, load_sem, red_send, red_recv, whole,
    ) = (
        refs_of[INV, 0], at.proj, at.inv, at.point, at.perm, at.rowperm, at.wp, at.blocks_bd, at.dwp, at.mdwp, at.rmask,
        at.smask, at.diag, at.diag_t, at.hid, at.hid_t, at.grad_t, at.normed, at.mixo, at.rden, at.tvals,
        at.joined, at.s0, at.dvals, at.gmix, at.pre_u, at.pre_d, at.act, at.act_d, at.mid, at.dvals, at.branch,
        at.gnow, at.stats, at.exbuf, at.send_sem, at.recv_sem, at.load_sem, at.red_send, at.red_recv, at.whole,
    )
    place = Place()
    me = place.dp
    layers = proj_ref.shape[0]
    width = x_ref.shape[1]
    expanded = inv_ref.shape[2]
    total_rows = float(x_ref.shape[0] * n_dp)
    wide = width // LANE
    stages = 2 * layers

    loads = {}
    for i, (source, target) in enumerate(
        ((proj_hbm, proj_ref), (inv_hbm, inv_ref), (point_hbm, point_ref)), 1
    ):
        for l in range(layers):
            loads[i, l] = pltpu.make_async_copy(source.at[l], target.at[l], load_sem.at[i, l])
    piece_rows = width // 2 // n_pipe
    for l in range(layers):
        for q in range(2 * n_pipe):
            pltpu.make_async_copy(
                qkv_hbm.at[l, q * piece_rows : (q + 1) * piece_rows],
                inv_own.at[l, q // n_pipe, q % n_pipe, :, 0 : 3 * width],
                load_sem.at[0, l],
            ).start()
        for i in range(1, 4):
            loads[i, l].start()

    barrier = pltpu.get_barrier_semaphore()

    def greet(k, carry):
        pl.semaphore_signal(barrier, inc=1, device_id={"dp": lax.rem(me + k, n_dp)})
        return carry

    lax.fori_loop(1, n_dp, greet, 0)

    def greet_segment(k, carry):
        there = lax.rem(place.pipe + k, n_pipe)
        for other in (me, me + 1 - 2 * place.core):
            pl.semaphore_signal(barrier, inc=1, device_id={"pipe": there, "dp": other})
        return carry

    lax.fori_loop(1, n_pipe, greet_segment, 0)

    jobs = {}
    for l in range(layers):
        for job in range(JOBS):
            base = KINDS * (JOBS * l + job)
            buffers = [refs_of[job, kind].at[l] for kind in range(4)]
            given = ((job, l) in DIRECT, place, *buffers, red_send, red_recv, base)
            if job < MATRICES:
                jobs[job, l] = Reduction(*given)
            else:
                rest = (refs_of[job, 6], refs_of[job, 4].at[l], refs_of[job, 5].at[l])
                jobs[job, l] = Small(*given, *rest, (at.out_att, at.out_mb)[job - ATT].at[l])
        for job, members, sizes, result in (
            (ATT_COLUMNS, ((QKV, QKV + 1, QKV + 2), (PROJ,)), (3 * width, proj_ref.shape[1]), at.out_attcols),
            (MB_COLUMNS, ((INV,), (POINT,)), (expanded, expanded), at.out_mbcols),
        ):
            jobs[job, l] = Columns(
                place, [[jobs[piece, l] for piece in pieces] for pieces in members], [n // n_dp for n in sizes],
                red_send, red_recv, KINDS * JOBS * layers + 2 * l + job - ATT_COLUMNS, refs_of[job, 0],
                refs_of[job, 1].at[l], whole, result.at[l],
            )

    perm[...] = split_matrix(width)
    row, col = iota((width, width), 0), iota((width, width), 1)
    half = width // 2
    core_of = (row >= half).astype(jnp.int32)
    inner = row - half * core_of
    for q in range(1, n_pipe):
        inner = jnp.where(row - half * core_of >= q * piece_rows, inner + piece_rows, inner)
    rowperm[...] = jnp.where(inner + core_of * piece_rows == col, 1.0, 0.0).astype(BF)
    rmask[...] = row_mask()
    smask[...] = crop_mask(48, 192)

    block_lane, block_row = iota((LANE, LANE), 1), iota((LANE, LANE), 0)
    on_diag = (block_lane >> 5) == (block_row >> 5)
    ones_on_diag = jnp.where(on_diag, 1.0, 0.0)
    diag[...] = jnp.concatenate([ones_on_diag, ones_on_diag], axis=1)
    diag_t[...] = jnp.concatenate([ones_on_diag, ones_on_diag], axis=0)
    tile = jnp.where((iota((32, LANE), 1) & 31) == iota((32, LANE), 0), 1.0, 0.0).astype(BF)

    for t in range(dw_ref.shape[0]):
        taps = dw_ref[t].astype(F32)
        for l in range(layers):
            dwp[l, t : t + 1, :] = taps[l : l + 1]
    for t in range(mdw_ref.shape[0]):
        taps = mdw_ref[t].astype(F32)
        for l in range(layers):
            mdwp[l, t : t + 1, :] = taps[l : l + 1]

    def prepare(l):
        wait_bytes(inv_own.at[l, :, :, :, 0 : 3 * width], load_sem.at[0, l])
        for c in range(wide):
            cut = slice(c * width, (c + 1) * width)
            w_split = mm(inv_own[l, :, :, :, cut].reshape(width, width), perm[...]).astype(BF)
            for part in range(3):
                wp[l, :, lanes(part * wide + c)] = w_split[:, lanes(part)]
        taps = [mm(dwp[l, :, c * width : (c + 1) * width].astype(BF), perm[...]) for c in range(wide)]
        for c in range(wide):
            for part in range(3):
                dwp[l, :, lanes(part * wide + c)] = taps[c][:, lanes(part)]
                rows = jnp.concatenate([group_ref[l, 3 * (4 * c + i) + part] for i in range(HEADS)], axis=0)
                full = jnp.where(on_diag, mm(rows, tile), 0.0)
                blocks_bd[l, part * wide + c] = full.astype(BF)

    spread = spread_matrix(x_ref.shape[0])
    hid[0] = mm(spread, x_ref[...]).astype(BF)
    gnow[...] = mm(spread, ct_ref[...])
    prepare(0)
    pl.semaphore_wait(barrier, n_dp - 1 + 2 * (n_pipe - 1))

    def slot_rows(count):
        return -(-count * wide // SUB) * SUB

    def exchange_start(e, vectors):
        rows = slot_rows(len(vectors))
        for i, vector in enumerate(vectors):
            for j in range(wide):
                row = i * wide + j
                exbuf[e, me, row : row + 1, :] = vector[:, lanes(j)]

        def send(k, carry):
            pltpu.make_async_remote_copy(
                src_ref=exbuf.at[e, me, 0:rows],
                dst_ref=exbuf.at[e, me, 0:rows],
                send_sem=send_sem.at[e],
                recv_sem=recv_sem.at[e],
                device_id={"dp": lax.rem(me + k, n_dp)},
            ).start()
            return carry

        lax.fori_loop(1, n_dp, send, 0)

    def exchange_finish(e, count):
        rows = slot_rows(count)
        wait_bytes(exbuf.at[e, 0 : n_dp - 1, 0:rows], recv_sem.at[e])
        total = exbuf[e, 0, 0:rows]
        for d in range(1, n_dp):
            total = total + exbuf[e, d, 0:rows]
        total = total * (1.0 / total_rows)
        return [
            jnp.concatenate([total[i * wide + j : i * wide + j + 1] for j in range(wide)], axis=1)
            for i in range(count)
        ]

    def attention_forward(l, s):
        joined[l] = mm(hid[s], wp[l]).astype(BF).astype(F32)

        def chunks(c):
            keep = rmask[...]
            columns = [lanes(part * wide + c) for part in range(3)]
            cells = [joined[l, :, at] for at in columns]
            convs = []
            for at, value in zip(columns, cells):
                conv = depthwise(value.reshape(20, SUB, LANE), dwp[l, :, at], 5)
                convs.append((conv.reshape(ROWS, LANE) * keep).astype(BF))
            linears = [mm(conv, blocks_bd[l, part * wide + c]) for part, conv in enumerate(convs)]
            results = []
            for query, key, value in (cells, linears):
                results.append((softplus(query), softplus(key) * keep, value))
            for part in range(3):
                s0[l, :, columns[part]] = convs[part]
                for source in range(2):
                    tvals[l, :, lanes(part * UNITS + source * wide + c)] = results[source][part]

        groups(wide, 1, chunks, True)

        def units(first):
            places = [(first + k, start, size) for k in range(UNIT_STEP) for start, size in BLOCKS]
            inputs = [
                [tvals[l, start : start + size, lanes(u + part * UNITS)] for part in range(3)]
                for u, start, size in places
            ]
            weights = []
            for (_, start, size), (query, key, value) in zip(places, inputs):
                ones = jnp.ones_like(value)
                if start == SMALL:
                    scores = mm(query.astype(BF), stacked(key), NT) * smask[...]
                    weights.append((scores, jnp.concatenate([stacked(value), stacked(ones)], axis=1)))
                else:
                    state = mm(key.astype(BF), joint(value, ones), TN) * diag[...]
                    weights.append((query, state.astype(BF)))
            sums = [mm(left.astype(BF), right) for left, right in weights]
            results = []
            for value in sums:
                inverse = 1.0 / value[:, LANE:]
                results.append((inverse, value[:, :LANE] * inverse))
            for (u, start, size), (inverse, mixed) in zip(places, results):
                rden[l, start : start + size, lanes(u)] = inverse
                mixo[l, start : start + size, lanes(u)] = mixed

        groups(UNITS, UNIT_STEP, units)
        loads[1, l].wait()
        branch[...] = mm(mixo[l].astype(BF), proj_ref[l])

    def expand_forward(l, s):
        loads[2, l].wait()
        pre_u[l] = mm(hid[s], inv_ref[l])

        def chunk(j):
            at = lanes(j)
            pre = pre_u[l, :, at] + ibias_ref[:, at].astype(F32)[l : l + 1]
            value, slope = silu_parts(pre)
            value = value * rmask[...]
            pre_u[l, :, at] = value
            pre_d[l, :, at] = (slope * rmask[...]).astype(BF)
            conv = depthwise(value.reshape(20, SUB, LANE), mdwp[l, :, at], 3).reshape(ROWS, LANE)
            out, out_slope = silu_parts(conv + mbias_ref[:, at].astype(F32)[l : l + 1])
            act[l, :, at] = (out * rmask[...]).astype(BF)
            act_d[l, :, at] = out_slope.astype(BF)

        loop(expanded // LANE, EXPAND_STEP, chunk)
        loads[3, l].wait()
        branch[...] = mm(act[l], point_ref[l])

    gains = gain_ref[...].astype(F32)
    shifts = shift_ref[...].astype(F32)
    last = stages - 1
    for s in range(stages):
        l = s // 2
        if s % 2 == 0:
            attention_forward(l, s)
        else:
            expand_forward(l, s)
        keep = rmask[...]
        for j in range(wide):
            branch[:, lanes(j)] = branch[:, lanes(j)] * keep
        value = branch[...]
        vectors = [column_sum(value), column_sum(value * value)]
        if s == last:
            upstream = gnow[...]
            vectors += [column_sum(upstream * value), column_sum(upstream)]
        exchange_start(s, vectors)
        if s == 0:
            for l in range(1, layers):
                prepare(l)
        hid_t[s] = mm(rowperm[...], hid[s], NT).astype(BF)
        mean, square, *backward = exchange_finish(s, len(vectors))
        scale = lax.rsqrt(square - mean * mean + EPS)
        stats[s : s + 1, :] = scale
        norm = (branch[...] - mean) * scale
        after = hid[s].astype(F32) + gains[s : s + 1] * norm + shifts[s : s + 1]
        for j in range(wide):
            normed[s, :, lanes(j)] = norm[:, lanes(j)] * keep
            hid[s + 1, :, lanes(j)] = (after[:, lanes(j)] * keep).astype(BF)
        if s == last:
            first_cross = scale * (backward[0] - mean * backward[1])
            first_total = backward[1]
            local_cross = scale * (vectors[2] - mean * vectors[3])
            local_sum = vectors[3]

    def small_row(name, l, row, value, at):
        jobs[name, l].stage[row // SUB, row % SUB : row % SUB + 1, at] = value

    def expand_row(l, j, tap, value):
        jobs[MB, l].stage[j // wide * 2 + tap // SUB, tap % SUB : tap % SUB + 1, lanes(j % wide)] = value

    def matrix(name, l, left, right, columns):
        own = jobs[name, l].own
        step = width
        for c in range(columns // step):
            cut = slice(c * step, (c + 1) * step)
            own[:, :, :, cut] = mm(left, right(cut)).astype(BF).reshape(2, n_pipe, piece_rows, step)
        jobs[name, l].start()

    def attention_backward(l, s, grad_branch, pause):
        gmix[...] = mm(grad_branch, proj_ref[l], NT).astype(BF).astype(F32)
        matrix(PROJ, l, grad_t[...], lambda cut: mixo[l, :, cut].astype(BF), mixo.shape[2])
        pause(T_START, s)

        def units(first):
            places = [(first + k, start, size) for k in range(UNIT_STEP) for start, size in BLOCKS]
            inputs = []
            for u, start, size in places:
                rows = slice(start, start + size)
                down = gmix[rows, lanes(u)] * rden[l, rows, lanes(u)]
                inputs.append(
                    [tvals[l, rows, lanes(u + part * UNITS)] for part in range(3)]
                    + [down, -down * mixo[l, rows, lanes(u)]]
                )
            products = []
            for (_, start, size), (query, key, value, down, level) in zip(places, inputs):
                ones = jnp.ones_like(value)
                if start == SMALL:
                    inside = smask[...]
                    query_stack, down_stack = stacked(query), stacked(down)
                    grad_scores = mm(
                        joint(down, level), jnp.concatenate([stacked(value), stacked(ones)], axis=1), NT
                    )
                    grad_scores_t = mm(
                        joint(value, ones), jnp.concatenate([down_stack, stacked(level)], axis=1), NT
                    )
                    scores_t = mm(key.astype(BF), query_stack, NT)
                    products.append((
                        (grad_scores * inside, stacked(key)),
                        (grad_scores_t * inside, query_stack),
                        (scores_t * inside, down_stack),
                    ))
                else:
                    both, slopes = joint(value, ones), joint(down, level)
                    state_t = mm(both, key.astype(BF), TN) * diag_t[...]
                    grad_state_t = mm(slopes, query.astype(BF), TN) * diag_t[...]
                    grad_state = mm(query.astype(BF), down.astype(BF), TN) * diag[:, 0:LANE]
                    products.append((
                        (slopes, state_t.astype(BF)), (both, grad_state_t.astype(BF)), (key, grad_state.astype(BF))
                    ))
            results = []
            for (query, key, *_), pairs in zip(inputs, products):
                grad_query, grad_key, grad_value = (mm(left.astype(BF), right) for left, right in pairs)
                results.append(
                    (grad_query * (1.0 - jnp.exp(-query)), grad_key * (1.0 - jnp.exp(-key)), grad_value)
                )
            for (u, start, size), grads in zip(places, results):
                for part, grad in enumerate(grads):
                    dvals[start : start + size, lanes(u + part * UNITS)] = grad

        groups(UNITS, UNIT_STEP, units)
        pause(T_UNITS, s)

        def chunks(c):
            keep = rmask[...]
            columns = [lanes(part * wide + c) for part in range(3)]
            slots = [part * UNITS + c for part in range(3)]
            grads = [dvals[:, lanes(slot + wide)].astype(BF) for slot in slots]
            direct = [dvals[:, lanes(slot)] for slot in slots]
            cells = [joined[l, :, at].reshape(20, SUB, LANE) for at in columns]
            convs = [
                mm(grad, blocks_bd[l, part * wide + c], NT).reshape(20, SUB, LANE) for part, grad in enumerate(grads)
            ]
            blocks = [mm(s0[l, :, at], grad, TN) * diag[:, 0:LANE] for at, grad in zip(columns, grads)]
            taps_of, grads_of = [], []
            for part, conv in enumerate(convs):
                back = depthwise(conv, dwp[l, :, columns[part]], 5, flip=True).reshape(ROWS, LANE)
                taps_of.append(depthwise_taps(cells[part], conv, 5))
                grads_of.append((direct[part] + back * keep).astype(BF))
            for at, block, taps, joined_grad in zip(columns, blocks, taps_of, grads_of):
                block = block[0:32] + block[32:64] + block[64:96] + block[96:128]
                jobs[ATT, l].stage[4:8, :, at] = block.reshape(4, SUB, LANE)
                for tap, row in enumerate(taps):
                    small_row(ATT, l, tap, row, at)
                mid[:, at] = joined_grad
            natural = mm(jnp.concatenate(grads_of, axis=1), perm[...], NT).astype(BF)
            matrix(QKV + c, l, hid_t[s], lambda cut: natural, width)
            pause(T_CHUNKS + c, s)

        groups(wide, 1, chunks, True)
        jobs[ATT, l].start()
        grad_hidden = mm(mid[:, : 3 * width], wp[l], NT)

        return grad_hidden

    def expand_backward(l, s, grad_branch, pause):
        gact[:, 0:expanded] = mm(grad_branch, point_ref[l], NT).astype(BF).astype(F32)
        matrix(POINT, l, grad_t[...], lambda cut: act[l, :, cut], expanded)
        pause(M_START, s)

        def chunk(j):
            at = lanes(j)
            grad_conv = gact[:, at] * act_d[l, :, at].astype(F32)
            expand_row(l, j, 9, column_sum(grad_conv))
            cells = pre_u[l, :, at].reshape(20, SUB, LANE)
            grad_conv = grad_conv.reshape(20, SUB, LANE)
            for tap, row in enumerate(depthwise_taps(cells, grad_conv, 3)):
                expand_row(l, j, tap, row)
            back = depthwise(grad_conv, mdwp[l, :, at], 3, flip=True).reshape(ROWS, LANE)
            grad_pre = (back * pre_d[l, :, at].astype(F32)).astype(BF)
            mid[:, at] = grad_pre
            expand_row(l, j, 10, column_sum(grad_pre.astype(F32)))

        loop(expanded // LANE, EXPAND_STEP, chunk)
        matrix(INV, l, hid_t[s], lambda cut: mid[:, cut], expanded)
        jobs[MB, l].start()
        pause(M_CHUNKS, s)
        return mm(mid[...], inv_ref[l], NT)

    def pause(moment, s):
        for job, l, step in PLAN.get((moment, s), ()):
            jobs[job, l].do(step)

    for s in range(stages - 1, -1, -1):
        l = s // 2
        keep = rmask[...]
        if s == last:
            cross, total = first_cross, first_total
        else:
            cross, total = exchange_finish(stages + s, 2)
        pause(BEGIN, s)
        if s % 2 == 0:
            small_row(ATT, l, 25, local_cross, slice(0, width))
            small_row(ATT, l, 25, local_sum, slice(width, 2 * width))
        else:
            small_row(MB, l, 11, local_cross, slice(0, width))
            small_row(MB, l, 16 + 11, local_sum, slice(0, width))
        grad_branch = (stats[s : s + 1, :] * gains[s : s + 1]) * (gnow[...] - total - normed[s] * cross)
        grad_branch = jnp.concatenate(
            [grad_branch[:, lanes(j)] * keep for j in range(wide)], axis=1
        ).astype(BF)
        grad_t[...] = mm(rowperm[...], grad_branch, NT).astype(BF)
        back = attention_backward if s % 2 == 0 else expand_backward
        grad_hidden = back(l, s, grad_branch, pause)
        after = (gnow[...] + grad_hidden).astype(BF).astype(F32)
        gnow[...] = after
        if s > 0:
            local_cross, local_sum = column_sum(after * normed[s - 1]), column_sum(after)
            exchange_start(stages + s - 1, [local_cross, local_sum])
        pause(SENT, s)
        pause(DONE, s)
        if s == last:
            at.out_x[...] = mm(spread, hid[stages], TN).astype(BF)

    at.out_g[...] = mm(spread, gnow[...].astype(BF), TN).astype(BF)
    for job in jobs.values():
        if isinstance(job, Reduction):
            job.drain()
    for e in range(2 * stages - 1):
        rows = slot_rows(4 if e == last else 2)
        wait_bytes(exbuf.at[e, 0 : n_dp - 1, 0:rows], send_sem.at[e])


def unsplit(value, wide):
    lane = iota((1, LANE), 1) >> 5
    columns = []
    for c in range(wide):
        parts = [value[:, lanes(part * wide + c)] for part in range(3)]
        for k in range(3):
            column = None
            for slot in range(4):
                index = 4 * k + slot
                moved = pltpu.roll(parts[index % 3], (slot - index // 3) % 4 * 32, 1)
                column = moved if column is None else jnp.where(lane == slot, moved, column)
            columns.append(column)
    return columns


def arrange(layers, wide, shares, x_in, g_in, attcols_in, mbcols_in, att_in, mb_in,
            x_out, g_out, qkv_out, proj_out, inv_out, point_out, dw_out, group_out, ibias_out, mdw_out, mbias_out,
            gain_out, shift_out):
    width = wide * LANE
    share_qkv, share_proj, share_inv, share_point = shares
    x_out[...] = x_in[...]
    g_out[...] = g_in[...]
    taps, mtaps = dw_out.shape[0], mdw_out.shape[0]
    for l in range(layers):
        rows = attcols_in.shape[1]
        values = []
        for value, share in ((attcols_in[l], share_qkv), (mbcols_in[l], share_inv)):
            value = jnp.concatenate([value, jnp.zeros((padded(rows) - rows, value.shape[1]), F32)], axis=0)
            values += [value, pltpu.roll(value, value.shape[1] - share, 1)]
        qkv_out[l] = jnp.transpose(values[0])[0:share_qkv, 0:rows]
        proj_out[l] = jnp.transpose(values[1])[0:share_proj, 0:rows]
        inv_out[l] = values[2][0:rows, 0:share_inv]
        point_out[l] = jnp.transpose(values[3])[0:share_point, 0:rows]
        natural = unsplit(att_in[l], wide)
        for j, column in enumerate(natural):
            for t in range(taps):
                dw_out[t, l : l + 1, lanes(j)] = column[t : t + 1]
            group_out[l, :, lanes(j)] = column[32:64]
        for block in range(4):
            cut = slice(block * width, (block + 1) * width)
            rows = mb_in[l, 16 * block : 16 * block + 16]
            for t in range(mtaps):
                mdw_out[t, l : l + 1, cut] = rows[t : t + 1]
            mbias_out[l : l + 1, cut] = rows[9:10]
            ibias_out[l : l + 1, cut] = rows[10:11]
        gain_out[2 * l : 2 * l + 1, :] = att_in[l, 25:26, 0:width]
        shift_out[2 * l : 2 * l + 1, :] = att_in[l, 25:26, width : 2 * width]
        gain_out[2 * l + 1 : 2 * l + 2, :] = mb_in[l, 11:12, :]
        shift_out[2 * l + 1 : 2 * l + 2, :] = mb_in[l, 27:28, :]


def padded(columns):
    return -(-columns // LANE) * LANE


def body(
    activations, cotangent, att_qkv, att_dw, att_group, att_proj, mb_inv, mb_inv_bias, mb_dw, mb_dw_bias, mb_point,
    bn_gain, bn_bias,
):
    n_dp, n_pipe = lax.axis_size("dp"), lax.axis_size("pipe")
    layers, width, joined_width = att_qkv.shape
    mixed_width = att_proj.shape[1]
    expanded = mb_inv.shape[2]
    tokens = activations.shape[2]
    stages = 2 * layers
    rows = width // 2 // n_pipe
    vmem = pl.BlockSpec(memory_space=pltpu.VMEM)
    hbm = pl.BlockSpec(memory_space=pl.ANY)
    columns = (width, width, width, mixed_width, expanded, expanded, joined_width, width)
    shares = tuple(n // n_dp for n in (joined_width, mixed_width, expanded, expanded))
    share_att, share_mb = padded(shares[0] + shares[1]), padded(shares[2] + shares[3])
    outs = dict(
        out_x=jax.ShapeDtypeStruct((tokens, width), BF),
        out_g=jax.ShapeDtypeStruct((tokens, width), BF),
        out_attcols=jax.ShapeDtypeStruct((layers, 2 * rows, share_att), F32),
        out_mbcols=jax.ShapeDtypeStruct((layers, 2 * rows, share_mb), F32),
        out_att=jax.ShapeDtypeStruct((layers, 8 * SUB, joined_width), F32),
        out_mb=jax.ShapeDtypeStruct((layers, 8 * SUB, width), F32),
    )
    scratch = dict(
        proj=pltpu.VMEM(att_proj.shape, BF),
        inv=pltpu.VMEM(mb_inv.shape, BF),
        point=pltpu.VMEM(mb_point.shape, BF),
        perm=pltpu.VMEM((width, width), BF),
        rowperm=pltpu.VMEM((width, width), BF),
        wp=pltpu.VMEM((layers, width, joined_width), BF),
        blocks_bd=pltpu.VMEM((layers, joined_width // LANE, LANE, LANE), BF),
        dwp=pltpu.VMEM((layers, 32, joined_width), F32),
        mdwp=pltpu.VMEM((layers, 16, expanded), F32),
        rmask=pltpu.VMEM((ROWS, LANE), F32),
        smask=pltpu.VMEM((48, 192), F32),
        diag=pltpu.VMEM((LANE, 2 * LANE), F32),
        diag_t=pltpu.VMEM((2 * LANE, LANE), F32),
        hid=pltpu.VMEM((stages + 1, ROWS, width), BF),
        hid_t=pltpu.VMEM((stages, width, ROWS), BF),
        grad_t=pltpu.VMEM((width, ROWS), BF),
        normed=pltpu.VMEM((stages, ROWS, width), F32),
        mixo=pltpu.VMEM((layers, ROWS, mixed_width), F32),
        rden=pltpu.VMEM((layers, ROWS, mixed_width), F32),
        tvals=pltpu.VMEM((layers, ROWS, 3 * mixed_width), F32),
        joined=pltpu.VMEM((layers, ROWS, joined_width), F32),
        s0=pltpu.VMEM((layers, ROWS, joined_width), BF),
        dvals=pltpu.VMEM((ROWS, 3 * mixed_width), F32),
        gmix=pltpu.VMEM((ROWS, mixed_width), F32),
        pre_u=pltpu.VMEM((layers, ROWS, expanded), F32),
        pre_d=pltpu.VMEM((layers, ROWS, expanded), BF),
        act=pltpu.VMEM((layers, ROWS, expanded), BF),
        act_d=pltpu.VMEM((layers, ROWS, expanded), BF),
        mid=pltpu.VMEM((ROWS, expanded), BF),
        branch=pltpu.VMEM((ROWS, width), F32),
        gnow=pltpu.VMEM((ROWS, width), F32),
        stats=pltpu.VMEM((8, width), F32),
        exbuf=pltpu.VMEM((2 * stages - 1, n_dp, 2 * SUB, LANE), F32),
        whole=pltpu.VMEM((rows, 2 * expanded), F32),
        send_sem=pltpu.SemaphoreType.DMA((2 * stages - 1,)),
        recv_sem=pltpu.SemaphoreType.DMA((2 * stages - 1,)),
        load_sem=pltpu.SemaphoreType.DMA((4, layers)),
        red_send=pltpu.SemaphoreType.DMA((KINDS * JOBS * layers + 2 * layers,)),
        red_recv=pltpu.SemaphoreType.DMA((KINDS * JOBS * layers + 2 * layers,)),
    )
    for job, n in enumerate(columns):
        high, kind = rows, BF
        if job == ATT:
            n, high = padded(n // 2), 2 * SUB
        elif job == MB:
            high, kind = SUB, F32
        shapes = [(2, n_pipe), (n_pipe,), (2,), ()]
        if job >= MATRICES:
            shapes += [(n_dp // 2,), (2 * n_pipe,)]
            scratch[job, 6] = pltpu.VMEM((8, SUB, columns[job]), F32)
        for i, shape in enumerate(shapes):
            scratch[job, i] = pltpu.VMEM((layers, *shape, high, n), kind)
    for job, share in ((ATT_COLUMNS, share_att), (MB_COLUMNS, share_mb)):
        scratch[job, 0] = pltpu.VMEM((n_dp, rows, share), BF)
        scratch[job, 1] = pltpu.VMEM((layers, n_dp, rows, share), BF)
    results = pl.pallas_call(
        functools.partial(kernel, n_dp, n_pipe, 13, tuple(outs) + tuple(scratch)),
        out_shape=tuple(outs.values()),
        in_specs=[vmem, vmem, hbm, vmem, vmem, hbm, hbm, vmem, vmem, vmem, hbm, vmem, vmem],
        out_specs=(vmem,) * len(outs),
        scratch_shapes=list(scratch.values()),
        compiler_params=pltpu.CompilerParams(
            collective_id=0, has_side_effects=True, vmem_limit_bytes=63 * 1024 * 1024
        ),
    )(
        activations.reshape(tokens, width),
        cotangent.reshape(tokens, width),
        att_qkv,
        att_dw.transpose(1, 0, 2),
        att_group,
        att_proj,
        mb_inv,
        mb_inv_bias,
        mb_dw.transpose(1, 0, 2),
        mb_dw_bias,
        mb_point,
        bn_gain,
        bn_bias,
    )
    taps, mtaps = att_dw.shape[1], mb_dw.shape[1]
    arranged = pl.pallas_call(
        functools.partial(arrange, layers, width // LANE, shares),
        out_shape=(
            jax.ShapeDtypeStruct((tokens, width), BF),
            jax.ShapeDtypeStruct((tokens, width), BF),
            jax.ShapeDtypeStruct((layers, shares[0], 2 * rows), F32),
            jax.ShapeDtypeStruct((layers, shares[1], 2 * rows), F32),
            jax.ShapeDtypeStruct((layers, 2 * rows, shares[2]), F32),
            jax.ShapeDtypeStruct((layers, shares[3], 2 * rows), F32),
            jax.ShapeDtypeStruct((taps, layers, joined_width), F32),
            jax.ShapeDtypeStruct((layers, 32, joined_width), F32),
            jax.ShapeDtypeStruct((layers, expanded), F32),
            jax.ShapeDtypeStruct((mtaps, layers, expanded), F32),
            jax.ShapeDtypeStruct((layers, expanded), F32),
            jax.ShapeDtypeStruct((stages, width), F32),
            jax.ShapeDtypeStruct((stages, width), F32),
        ),
        in_specs=[vmem] * 6,
        out_specs=(vmem,) * 13,
    )(*results)
    x_out, g_out, qkv, proj, inv, point, dw, group, ibias, mdw, mbias, gain, shift = arranged
    groups, size = att_group.shape[1], att_group.shape[2]
    return (
        x_out.reshape(activations.shape),
        g_out.reshape(activations.shape),
        qkv.transpose(0, 2, 1),
        dw.transpose(1, 0, 2),
        group.reshape(layers, size, groups, size).transpose(0, 2, 1, 3),
        proj,
        inv,
        ibias,
        mdw.transpose(1, 0, 2),
        mbias,
        point,
        gain,
        shift,
    )


def solution(mesh):
    placed = (P("pipe", "dp", None, None), P("pipe", "dp", None, None)) + (P(),) * 11
    return jax.shard_map(
        body,
        mesh=mesh,
        in_specs=placed,
        out_specs=(
            P("pipe", "dp", None, None),
            P("pipe", "dp", None, None),
            P(None, "pipe", "dp"),
            P(),
            P(),
            P(None, "dp", "pipe"),
            P(None, "pipe", "dp"),
            P(),
            P(),
            P(),
            P(None, "dp", "pipe"),
            P(),
            P(),
        ),
        check_vma=False,
    )
```

```python
import functools
from types import SimpleNamespace

import jax
import jax.numpy as jnp
from jax import lax
from jax.experimental import pallas as pl
from jax.experimental.pallas import tpu as pltpu
from jax.sharding import PartitionSpec as P

F32 = jnp.float32
BF = jnp.bfloat16
EPS = 1e-05
LANE = 128
SUB = 8
ROWS = 160
SMALL = 112
BLOCKS = ((0, 56), (56, 56), (112, 48))
HEADS = 4
UNITS = 6
UNIT_STEP = 6
EXPAND_STEP = 1
NN = (((1,), (0,)), ((), ()))
NT = (((1,), (1,)), ((), ()))
TN = (((0,), (0,)), ((), ()))


def mm(a, b, dims=NN):
    return lax.dot_general(a, b, dims, preferred_element_type=F32)


def iota(shape, dim):
    return lax.broadcasted_iota(jnp.int32, shape, dim)


def lanes(j):
    if isinstance(j, int):
        return slice(j * LANE, (j + 1) * LANE)
    return pl.ds(pl.multiple_of(j * LANE, LANE), LANE)


def spread_matrix(tokens):
    row, col = iota((ROWS, tokens), 0), iota((ROWS, tokens), 1)
    crop = (row >= 56).astype(jnp.int32)
    inner = row - 56 * crop
    big = crop * 49 + (inner >> 3) * 7 + (inner & 7)
    small_row = row - SMALL
    pair = (small_row >= 24).astype(jnp.int32)
    inner = small_row - 24 * pair
    small = 98 + (pair * 2 + ((inner & 7) >> 2)) * 9 + (inner >> 3) * 3 + (inner & 3)
    is_big = row < SMALL
    valid = jnp.where(is_big, row & 7, (row & 3) + 4) < 7
    hit = (jnp.where(is_big, big, small) == col) & valid
    return jnp.where(hit, 1.0, 0.0).astype(BF)


def split_matrix(width):
    row, col = iota((width, width), 0), iota((width, width), 1)
    head = (row >= 96).astype(jnp.int32) + (row >= 192).astype(jnp.int32) + (row >= 288).astype(jnp.int32)
    rest = row - 96 * head
    part = (rest >= 32).astype(jnp.int32) + (rest >= 64).astype(jnp.int32)
    target = part * 128 + head * 32 + (rest - 32 * part)
    return jnp.where(target == col, 1.0, 0.0).astype(BF)


def row_mask(width=LANE):
    row = iota((ROWS, width), 0)
    valid = jnp.where(row < SMALL, row & 7, (row & 3) + 4) < 7
    return jnp.where(valid, 1.0, 0.0)


def crop_mask(rows, columns):
    row, col = iota((rows, columns), 0), iota((rows, columns), 1)
    for step in (3, 2, 1):
        col = jnp.where(col >= rows * step, col - rows * step, col)
    row_crop = (row >= 24).astype(jnp.int32) * 2 + ((row & 7) >> 2)
    col_crop = (col >= 24).astype(jnp.int32) * 2 + ((col & 7) >> 2)
    return jnp.where(row_crop == col_crop, 1.0, 0.0)


def head_masks():
    lane = iota((1, LANE), 1)
    return [jnp.where((lane >= 32 * h) & (lane < 32 * h + 32), 1.0, 0.0) for h in range(HEADS)]


def stacked(value):
    return jnp.concatenate([value * mask for mask in head_masks()], axis=0).astype(BF)


def joint(*values):
    return jnp.concatenate(values, axis=1).astype(BF)


def shifted(tokens, step):
    if step == 0:
        return tokens
    moved = pltpu.roll(tokens, (-step) % SUB, 1)
    if abs(step) == 1:
        return moved
    at = iota((1, SUB, LANE), 1)
    if tokens.shape[0] > 6:
        wrong = (at == 0) if step < 0 else (at == 6)
    else:
        wrong = ((at & 3) == 0) if step < 0 else ((at & 3) == 2)
    return jnp.where(wrong, 0.0, moved)


def tap_pairs(side, step):
    return range(max(0, -step), min(side, side - step))


def crops(tokens):
    return ((tokens[:14], 7), (tokens[14:], 3))


def depthwise(tokens, taps, reach, flip=False):
    margin = reach // 2
    parts = []
    for cells, side in crops(tokens):
        sums = [None] * side
        for dj in range(-margin, margin + 1):
            moved = shifted(cells, dj).reshape(2, side, SUB, LANE)
            for di in range(-margin, margin + 1):
                tap = (margin - di) * reach + margin - dj if flip else (margin + di) * reach + margin + dj
                weight = taps[tap : tap + 1, :].reshape(1, 1, LANE)
                for a in tap_pairs(side, di):
                    term = moved[:, a + di] * weight
                    sums[a] = term if sums[a] is None else sums[a] + term
        parts.append(jnp.stack(sums, axis=1).reshape(2 * side, SUB, LANE))
    return jnp.concatenate(parts, axis=0)


def depthwise_taps(tokens, grads, reach):
    margin = reach // 2
    totals = {}
    for (cells, side), (grad_cells, _) in zip(crops(tokens), crops(grads)):
        grad_cells = grad_cells.reshape(2, side, SUB, LANE)
        for dj in range(-margin, margin + 1):
            moved = shifted(cells, dj).reshape(2, side, SUB, LANE)
            for di in range(-margin, margin + 1):
                tap = (margin + di) * reach + margin + dj
                total = totals.get(tap)
                for a in tap_pairs(side, di):
                    term = moved[:, a + di] * grad_cells[:, a]
                    total = term if total is None else total + term
                if total is not None:
                    totals[tap] = total
    return [jnp.sum(jnp.sum(totals[tap], axis=0), axis=0, keepdims=True) for tap in range(reach * reach)]


def softplus(x):
    small = jnp.exp(-jnp.abs(x))
    return jnp.maximum(x, 0.0) + jnp.where(small < 1e-3, small * (1.0 - 0.5 * small), jnp.log(1.0 + small))


def silu_parts(x):
    gate = 0.5 * jnp.tanh(0.5 * x) + 0.5
    value = x * gate
    return value, gate + value * (1.0 - gate)


def loop(count, step, body):
    def several(i, carry):
        for k in range(step):
            body(i * step + k)
        return carry

    if step == count:
        several(0, 0)
    else:
        lax.fori_loop(0, count // step, several, 0)


def groups(count, step, body, unroll=False):
    if step == count or unroll:
        for first in range(0, count, step):
            body(first)
    else:
        lax.fori_loop(0, count // step, lambda i, carry: (body(i * step), carry)[1], 0)


def column_sum(value):
    return jnp.sum(value, axis=0, keepdims=True)


def wait_bytes(ref, sem):
    pltpu.make_async_copy(ref, ref, sem).wait()


class Reduction:
    def __init__(self, direct, place, own, pair, first, second, send_sem, recv_sem, base):
        self.direct = direct
        self.place, self.own, self.pair, self.first, self.second = place, own, pair, first, second
        self.send_sem, self.recv_sem, self.base = send_sem, recv_sem, base

    def copy(self, source, target, kind, pipe, dp):
        return pltpu.make_async_remote_copy(
            src_ref=source,
            dst_ref=target,
            send_sem=self.send_sem.at[self.base + kind],
            recv_sem=self.recv_sem.at[self.base + kind],
            device_id={"pipe": pipe, "dp": dp},
        )

    def to_pair(self):
        at = self.place
        return self.copy(self.own.at[1 - at.core], self.pair, 0, at.pipe, at.dp + 1 - 2 * at.core)

    def to_first(self, bit):
        at = self.place
        peer = at.pipe + (1 + at.core) * (1 - 2 * at.bit1)
        return self.copy(self.own.at[at.core, at.slab(1 - at.bit1, bit)], self.first.at[bit], 1 + bit, peer, at.dp)

    def to_second(self):
        at = self.place
        peer = at.pipe + (2 - at.core) * (1 - 2 * at.bit2)
        return self.copy(self.own.at[at.core, at.slab(at.bit1, 1 - at.bit2)], self.second, 3, peer, at.dp)

    def to_segment(self, k):
        at = self.place
        peer = lax.rem(at.pipe + k, self.pair.shape[0])
        target = self.second if k == 3 else self.first.at[k - 1]
        return self.copy(self.own.at[at.core, peer], target, k, peer, at.dp)

    def start(self):
        self.to_pair().start()

    def step1(self):
        at = self.place
        self.to_pair().wait_recv()
        if self.direct:
            for k in (2, 1, 3):
                slab = lax.rem(at.pipe + k, self.pair.shape[0])
                self.own[at.core, slab] = self.own[at.core, slab] + self.pair[slab]
                self.to_segment(k).start()
            return
        for bit in range(2):
            slab = at.slab(1 - at.bit1, bit)
            self.own[at.core, slab] = self.own[at.core, slab] + self.pair[slab]
            self.to_first(bit).start()

    def step2(self):
        if self.direct:
            return
        at = self.place
        for bit in range(2):
            self.to_first(bit).wait_recv()
        bit = 1 - at.bit2
        slab = at.slab(at.bit1, bit)
        total = self.own[at.core, slab].astype(F32) + self.pair[slab].astype(F32) + self.first[bit].astype(F32)
        self.own[at.core, slab] = total.astype(self.own.dtype)
        self.to_second().start()

    def part(self):
        at = self.place
        slab = at.pipe
        if self.direct:
            total = self.own[at.core, slab].astype(F32) + self.pair[slab].astype(F32)
            for k in (1, 2, 3):
                self.to_segment(k).wait_recv()
                total = total + (self.second[...] if k == 3 else self.first[k - 1]).astype(F32)
            return total
        self.to_second().wait_recv()
        total = self.own[at.core, slab].astype(F32) + self.pair[slab].astype(F32)
        return total + self.first[at.bit2].astype(F32) + self.second[...].astype(F32)

    def do(self, step):
        (None, self.step1, self.step2, self.step3, self.step4, self.finish)[step]()

    step3 = step4 = finish = None

    def drain(self):
        self.to_pair().wait_send()
        if self.direct:
            rest = [self.to_segment(k) for k in (1, 2, 3)]
        else:
            rest = [self.to_first(0), self.to_first(1), self.to_second()]
        for made in rest:
            made.wait_send()


class Place:
    def __init__(self):
        self.pipe, self.dp = lax.axis_index("pipe"), lax.axis_index("dp")
        self.core = lax.rem(self.dp, 2)
        low, high = lax.rem(self.pipe, 2), self.pipe // 2
        self.bit1 = low * (1 - self.core) + high * self.core
        self.bit2 = high * (1 - self.core) + low * self.core

    def slab(self, bit1, bit2):
        return bit1 * (1 + self.core) + bit2 * (2 - self.core)


class Columns:
    def __init__(self, place, matrices, shares, send_sem, recv_sem, base, outgoing, landed, whole, result):
        self.place, self.matrices, self.shares = place, matrices, shares
        self.send_sem, self.recv_sem = send_sem.at[base], recv_sem.at[base]
        self.outgoing, self.landed, self.whole, self.result = outgoing, landed, whole, result

    def do(self, step):
        if step == SEND:
            self.send()
        else:
            self.finish()

    def send(self):
        at = self.place
        n_dp, rows, width = self.outgoing.shape
        spans, start = [], 0
        for pieces in self.matrices:
            first = start
            for piece in pieces:
                size = piece.own.shape[3]
                self.whole[:, start : start + size] = piece.part()
                start += size
            spans.append((first, start - first))
        lane = iota((1, width), 1)

        def cut(d, carry):
            result, target = None, 0
            for (first, columns), share in zip(spans, self.shares):
                cover = min(max(padded(share) + LANE, width), columns)
                offset = d * share
                base = jnp.minimum(offset // LANE, (columns - cover) // LANE) * LANE
                piece = self.whole[:, pl.ds(pl.multiple_of(first + base, LANE), cover)]
                piece = pltpu.roll(piece, lax.rem(cover + target - (offset - base), cover), 1)[:, 0:width]
                result = piece if result is None else jnp.where(lane < target, result, piece)
                target += share
            self.outgoing[d] = result.astype(BF)
            return carry

        lax.fori_loop(0, n_dp, cut, 0)

        def push(k, carry):
            peer = lax.rem(at.dp + k, n_dp)
            pltpu.make_async_remote_copy(
                src_ref=self.outgoing.at[peer],
                dst_ref=self.landed.at[at.dp],
                send_sem=self.send_sem,
                recv_sem=self.recv_sem,
                device_id={"dp": peer},
            ).start()
            return carry

        lax.fori_loop(1, n_dp, push, 0)
        self.landed[at.dp] = self.outgoing[at.dp]

    def finish(self):
        n_dp, rows, _ = self.outgoing.shape
        wait_bytes(self.landed.at[0 : n_dp - 1], self.recv_sem)
        for core in range(2):
            total = self.landed[core].astype(F32)
            for d in range(core + 2, n_dp, 2):
                total = total + self.landed[d].astype(F32)
            self.result[core * rows : (core + 1) * rows, :] = total
        wait_bytes(self.outgoing.at[0 : n_dp - 1], self.send_sem)


class Small(Reduction):
    def __init__(self, *args):
        *rest, self.stage, self.along, self.everywhere, self.result = args
        super().__init__(*rest)

    def start(self):
        slabs, _, columns = self.stage.shape
        half = self.own.shape[3]
        for q in range(slabs):
            if half == columns:
                self.own[q // self.own.shape[1], q % self.own.shape[1]] = self.stage[q]
                continue
            low, high = self.stage[q, :, 0:half], self.stage[q, :, half:columns]
            if columns < 2 * half:
                high = jnp.concatenate([high, jnp.zeros((SUB, 2 * half - columns), F32)], axis=1)
            self.own[q // self.own.shape[1], q % self.own.shape[1]] = jnp.concatenate([low, high], axis=0).astype(BF)
        super().start()

    def step3(self):
        at = self.place
        pairs = self.along.shape[0]
        mine = at.dp // 2
        self.along[mine] = self.part().astype(self.along.dtype)

        def send(k, carry):
            peer = lax.rem(mine + k, pairs)
            pltpu.make_async_remote_copy(
                src_ref=self.along.at[mine],
                dst_ref=self.along.at[mine],
                send_sem=self.send_sem.at[self.base + 4],
                recv_sem=self.recv_sem.at[self.base + 4],
                device_id={"dp": peer * 2 + at.core},
            ).start()
            return carry

        lax.fori_loop(1, pairs, send, 0)

    def step4(self):
        at = self.place
        pairs = self.along.shape[0]
        wait_bytes(self.along.at[0 : pairs - 1], self.recv_sem.at[self.base + 4])
        total = self.along[0].astype(F32)
        for d in range(1, pairs):
            total = total + self.along[d].astype(F32)
        parts = self.everywhere.shape[0]
        segments = parts // 2
        mine = at.core * segments + at.pipe
        self.everywhere[mine] = total.astype(self.everywhere.dtype)

        def send(k, carry):
            peer = lax.rem(mine + k, parts)
            pltpu.make_async_remote_copy(
                src_ref=self.everywhere.at[mine],
                dst_ref=self.everywhere.at[mine],
                send_sem=self.send_sem.at[self.base + 5],
                recv_sem=self.recv_sem.at[self.base + 5],
                device_id={"pipe": lax.rem(peer, segments), "dp": at.dp - at.core + peer // segments},
            ).start()
            return carry

        lax.fori_loop(1, parts, send, 0)

    def finish(self):
        parts = self.everywhere.shape[0]
        wait_bytes(self.everywhere.at[0 : parts - 1], self.recv_sem.at[self.base + 5])
        for q in range(parts):
            value = self.everywhere[q].astype(F32)
            half = value.shape[1]
            self.result[q * SUB : (q + 1) * SUB, 0:half] = value[0:SUB]
            if half < self.result.shape[1]:
                self.result[q * SUB : (q + 1) * SUB, half:] = value[SUB:, 0 : self.result.shape[1] - half]

    def drain(self):
        super().drain()
        pairs, parts = self.along.shape[0], self.everywhere.shape[0]
        wait_bytes(self.along.at[0 : pairs - 1], self.send_sem.at[self.base + 4])
        wait_bytes(self.everywhere.at[0 : parts - 1], self.send_sem.at[self.base + 5])


QKV, PROJ, INV, POINT, ATT, MB, ATT_COLUMNS, MB_COLUMNS = 0, 3, 4, 5, 6, 7, 8, 9
MATRICES, SMALLS = 6, 2
JOBS = MATRICES + SMALLS
DIRECT = ()
SEND, FINISH = 0, 5
BEGIN, M_START, M_CHUNKS, T_START, T_UNITS, T_CHUNKS, SENT, DONE = 0, 1, 2, 3, 4, 5, 8, 9
PLAN = {
    (M_CHUNKS, 3): ((POINT, 1, 1),),
    (DONE, 3): ((MB, 1, 1), (INV, 1, 1),),
    (BEGIN, 2): (),
    (T_START, 2): ((POINT, 1, 2), (MB, 1, 2),),
    (T_UNITS, 2): ((PROJ, 1, 1),),
    (T_CHUNKS, 2): (),
    (T_CHUNKS + 1, 2): (),
    (T_CHUNKS + 2, 2): ((INV, 1, 2), (QKV, 1, 1),),
    (SENT, 2): ((MB, 1, 3), (QKV + 1, 1, 1),),
    (DONE, 2): ((QKV + 2, 1, 1), (PROJ, 1, 2), (ATT, 1, 1),),
    (BEGIN, 1): ((MB_COLUMNS, 1, SEND), (QKV, 1, 2),),
    (M_START, 1): ((QKV + 1, 1, 2), (QKV + 2, 1, 2), (ATT, 1, 2),),
    (M_CHUNKS, 1): ((POINT, 0, 1), (MB, 1, 4),),
    (SENT, 1): ((ATT, 1, 3), (ATT_COLUMNS, 1, SEND),),
    (DONE, 1): ((MB, 0, 1), (INV, 0, 1),),
    (T_START, 0): ((POINT, 0, 2), (MB, 0, 2), (ATT, 1, 4),),
    (T_UNITS, 0): ((PROJ, 0, 1),),
    (T_CHUNKS, 0): ((MB, 0, 3),),
    (T_CHUNKS + 1, 0): ((INV, 0, 2), (QKV, 0, 1),),
    (T_CHUNKS + 2, 0): ((QKV + 1, 0, 1), (MB_COLUMNS, 1, FINISH),),
    (SENT, 0): (
        (QKV + 2, 0, 1), (ATT, 0, 1), (PROJ, 0, 2), (MB, 0, 4), (QKV, 0, 2), (MB_COLUMNS, 0, SEND),
    ),
    (DONE, 0): (
        (ATT, 0, 2), (QKV + 1, 0, 2), (QKV + 2, 0, 2), (ATT_COLUMNS, 1, FINISH), (MB, 1, FINISH), (ATT, 1, FINISH),
        (ATT, 0, 3), (ATT_COLUMNS, 0, SEND), (ATT, 0, 4),
        (MB, 0, FINISH), (MB_COLUMNS, 0, FINISH),
        (ATT_COLUMNS, 0, FINISH), (ATT, 0, FINISH),
    ),
}
KINDS = 6


def kernel(n_dp, n_pipe, count_in, names, *refs):
    (
        x_ref, ct_ref, qkv_hbm, dw_ref, group_ref, proj_hbm, inv_hbm, ibias_ref, mdw_ref, mbias_ref, point_hbm,
        gain_ref, shift_ref,
    ) = refs[:count_in]
    refs_of = dict(zip(names, refs[count_in:]))
    at = SimpleNamespace(**{name: ref for name, ref in refs_of.items() if isinstance(name, str)})
    (
        inv_own, proj_ref, inv_ref, point_ref, perm, rowperm, wp, blocks_bd, dwp, mdwp, rmask, smask, diag, diag_t,
        hid, hid_t, grad_t, normed, mixo, rden, tvals, joined, s0, dvals, gmix, pre_u, pre_d, act, act_d, mid,
        gact, branch, gnow, stats, exbuf, send_sem, recv_sem, load_sem, red_send, red_recv, whole,
    ) = (
        refs_of[INV, 0], at.proj, at.inv, at.point, at.perm, at.rowperm, at.wp, at.blocks_bd, at.dwp, at.mdwp, at.rmask,
        at.smask, at.diag, at.diag_t, at.hid, at.hid_t, at.grad_t, at.normed, at.mixo, at.rden, at.tvals,
        at.joined, at.s0, at.dvals, at.gmix, at.pre_u, at.pre_d, at.act, at.act_d, at.mid, at.dvals, at.branch,
        at.gnow, at.stats, at.exbuf, at.send_sem, at.recv_sem, at.load_sem, at.red_send, at.red_recv, at.whole,
    )
    place = Place()
    me = place.dp
    layers = proj_ref.shape[0]
    width = x_ref.shape[1]
    expanded = inv_ref.shape[2]
    total_rows = float(x_ref.shape[0] * n_dp)
    wide = width // LANE
    stages = 2 * layers

    loads = {}
    for i, (source, target) in enumerate(
        ((proj_hbm, proj_ref), (inv_hbm, inv_ref), (point_hbm, point_ref)), 1
    ):
        for l in range(layers):
            loads[i, l] = pltpu.make_async_copy(source.at[l], target.at[l], load_sem.at[i, l])
    piece_rows = width // 2 // n_pipe
    for l in range(layers):
        for q in range(2 * n_pipe):
            pltpu.make_async_copy(
                qkv_hbm.at[l, q * piece_rows : (q + 1) * piece_rows],
                inv_own.at[l, q // n_pipe, q % n_pipe, :, 0 : 3 * width],
                load_sem.at[0, l],
            ).start()
        for i in range(1, 4):
            loads[i, l].start()

    barrier = pltpu.get_barrier_semaphore()

    def greet(k, carry):
        pl.semaphore_signal(barrier, inc=1, device_id={"dp": lax.rem(me + k, n_dp)})
        return carry

    lax.fori_loop(1, n_dp, greet, 0)

    def greet_segment(k, carry):
        there = lax.rem(place.pipe + k, n_pipe)
        for other in (me, me + 1 - 2 * place.core):
            pl.semaphore_signal(barrier, inc=1, device_id={"pipe": there, "dp": other})
        return carry

    lax.fori_loop(1, n_pipe, greet_segment, 0)

    jobs = {}
    for l in range(layers):
        for job in range(JOBS):
            base = KINDS * (JOBS * l + job)
            buffers = [refs_of[job, kind].at[l] for kind in range(4)]
            given = ((job, l) in DIRECT, place, *buffers, red_send, red_recv, base)
            if job < MATRICES:
                jobs[job, l] = Reduction(*given)
            else:
                rest = (refs_of[job, 6], refs_of[job, 4].at[l], refs_of[job, 5].at[l])
                jobs[job, l] = Small(*given, *rest, (at.out_att, at.out_mb)[job - ATT].at[l])
        for job, members, sizes, result in (
            (ATT_COLUMNS, ((QKV, QKV + 1, QKV + 2), (PROJ,)), (3 * width, proj_ref.shape[1]), at.out_attcols),
            (MB_COLUMNS, ((INV,), (POINT,)), (expanded, expanded), at.out_mbcols),
        ):
            jobs[job, l] = Columns(
                place, [[jobs[piece, l] for piece in pieces] for pieces in members], [n // n_dp for n in sizes],
                red_send, red_recv, KINDS * JOBS * layers + 2 * l + job - ATT_COLUMNS, refs_of[job, 0],
                refs_of[job, 1].at[l], whole, result.at[l],
            )

    perm[...] = split_matrix(width)
    row, col = iota((width, width), 0), iota((width, width), 1)
    half = width // 2
    core_of = (row >= half).astype(jnp.int32)
    inner = row - half * core_of
    for q in range(1, n_pipe):
        inner = jnp.where(row - half * core_of >= q * piece_rows, inner + piece_rows, inner)
    rowperm[...] = jnp.where(inner + core_of * piece_rows == col, 1.0, 0.0).astype(BF)
    rmask[...] = row_mask()
    smask[...] = crop_mask(48, 192)

    block_lane, block_row = iota((LANE, LANE), 1), iota((LANE, LANE), 0)
    on_diag = (block_lane >> 5) == (block_row >> 5)
    ones_on_diag = jnp.where(on_diag, 1.0, 0.0)
    diag[...] = jnp.concatenate([ones_on_diag, ones_on_diag], axis=1)
    diag_t[...] = jnp.concatenate([ones_on_diag, ones_on_diag], axis=0)
    tile = jnp.where((iota((32, LANE), 1) & 31) == iota((32, LANE), 0), 1.0, 0.0).astype(BF)

    for t in range(dw_ref.shape[0]):
        taps = dw_ref[t].astype(F32)
        for l in range(layers):
            dwp[l, t : t + 1, :] = taps[l : l + 1]
    for t in range(mdw_ref.shape[0]):
        taps = mdw_ref[t].astype(F32)
        for l in range(layers):
            mdwp[l, t : t + 1, :] = taps[l : l + 1]

    def prepare(l):
        wait_bytes(inv_own.at[l, :, :, :, 0 : 3 * width], load_sem.at[0, l])
        for c in range(wide):
            cut = slice(c * width, (c + 1) * width)
            w_split = mm(inv_own[l, :, :, :, cut].reshape(width, width), perm[...]).astype(BF)
            for part in range(3):
                wp[l, :, lanes(part * wide + c)] = w_split[:, lanes(part)]
        taps = [mm(dwp[l, :, c * width : (c + 1) * width].astype(BF), perm[...]) for c in range(wide)]
        for c in range(wide):
            for part in range(3):
                dwp[l, :, lanes(part * wide + c)] = taps[c][:, lanes(part)]
                rows = jnp.concatenate([group_ref[l, 3 * (4 * c + i) + part] for i in range(HEADS)], axis=0)
                full = jnp.where(on_diag, mm(rows, tile), 0.0)
                blocks_bd[l, part * wide + c] = full.astype(BF)

    spread = spread_matrix(x_ref.shape[0])
    hid[0] = mm(spread, x_ref[...]).astype(BF)
    gnow[...] = mm(spread, ct_ref[...])
    prepare(0)
    pl.semaphore_wait(barrier, n_dp - 1 + 2 * (n_pipe - 1))

    def slot_rows(count):
        return -(-count * wide // SUB) * SUB

    def exchange_start(e, vectors):
        rows = slot_rows(len(vectors))
        for i, vector in enumerate(vectors):
            for j in range(wide):
                row = i * wide + j
                exbuf[e, me, row : row + 1, :] = vector[:, lanes(j)]

        def send(k, carry):
            pltpu.make_async_remote_copy(
                src_ref=exbuf.at[e, me, 0:rows],
                dst_ref=exbuf.at[e, me, 0:rows],
                send_sem=send_sem.at[e],
                recv_sem=recv_sem.at[e],
                device_id={"dp": lax.rem(me + k, n_dp)},
            ).start()
            return carry

        lax.fori_loop(1, n_dp, send, 0)

    def exchange_finish(e, count):
        rows = slot_rows(count)
        wait_bytes(exbuf.at[e, 0 : n_dp - 1, 0:rows], recv_sem.at[e])
        total = exbuf[e, 0, 0:rows]
        for d in range(1, n_dp):
            total = total + exbuf[e, d, 0:rows]
        total = total * (1.0 / total_rows)
        return [
            jnp.concatenate([total[i * wide + j : i * wide + j + 1] for j in range(wide)], axis=1)
            for i in range(count)
        ]

    def attention_forward(l, s):
        joined[l] = mm(hid[s], wp[l]).astype(BF).astype(F32)

        def chunks(c):
            keep = rmask[...]
            columns = [lanes(part * wide + c) for part in range(3)]
            cells = [joined[l, :, at] for at in columns]
            convs = []
            for at, value in zip(columns, cells):
                conv = depthwise(value.reshape(20, SUB, LANE), dwp[l, :, at], 5)
                convs.append((conv.reshape(ROWS, LANE) * keep).astype(BF))
            linears = [mm(conv, blocks_bd[l, part * wide + c]) for part, conv in enumerate(convs)]
            results = []
            for query, key, value in (cells, linears):
                results.append((softplus(query), softplus(key) * keep, value))
            for part in range(3):
                s0[l, :, columns[part]] = convs[part]
                for source in range(2):
                    tvals[l, :, lanes(part * UNITS + source * wide + c)] = results[source][part]

        groups(wide, 1, chunks, True)

        def units(first):
            places = [(first + k, start, size) for k in range(UNIT_STEP) for start, size in BLOCKS]
            inputs = [
                [tvals[l, start : start + size, lanes(u + part * UNITS)] for part in range(3)]
                for u, start, size in places
            ]
            weights = []
            for (_, start, size), (query, key, value) in zip(places, inputs):
                ones = jnp.ones_like(value)
                if start == SMALL:
                    scores = mm(query.astype(BF), stacked(key), NT) * smask[...]
                    weights.append((scores, jnp.concatenate([stacked(value), stacked(ones)], axis=1)))
                else:
                    state = mm(key.astype(BF), joint(value, ones), TN) * diag[...]
                    weights.append((query, state.astype(BF)))
            sums = [mm(left.astype(BF), right) for left, right in weights]
            results = []
            for value in sums:
                inverse = 1.0 / value[:, LANE:]
                results.append((inverse, value[:, :LANE] * inverse))
            for (u, start, size), (inverse, mixed) in zip(places, results):
                rden[l, start : start + size, lanes(u)] = inverse
                mixo[l, start : start + size, lanes(u)] = mixed

        groups(UNITS, UNIT_STEP, units)
        loads[1, l].wait()
        branch[...] = mm(mixo[l].astype(BF), proj_ref[l])

    def expand_forward(l, s):
        loads[2, l].wait()
        pre_u[l] = mm(hid[s], inv_ref[l])

        def chunk(j):
            at = lanes(j)
            pre = pre_u[l, :, at] + ibias_ref[:, at].astype(F32)[l : l + 1]
            value, slope = silu_parts(pre)
            value = value * rmask[...]
            pre_u[l, :, at] = value
            pre_d[l, :, at] = (slope * rmask[...]).astype(BF)
            conv = depthwise(value.reshape(20, SUB, LANE), mdwp[l, :, at], 3).reshape(ROWS, LANE)
            out, out_slope = silu_parts(conv + mbias_ref[:, at].astype(F32)[l : l + 1])
            act[l, :, at] = (out * rmask[...]).astype(BF)
            act_d[l, :, at] = out_slope.astype(BF)

        loop(expanded // LANE, EXPAND_STEP, chunk)
        loads[3, l].wait()
        branch[...] = mm(act[l], point_ref[l])

    gains = gain_ref[...].astype(F32)
    shifts = shift_ref[...].astype(F32)
    last = stages - 1
    for s in range(stages):
        l = s // 2
        if s % 2 == 0:
            attention_forward(l, s)
        else:
            expand_forward(l, s)
        keep = rmask[...]
        for j in range(wide):
            branch[:, lanes(j)] = branch[:, lanes(j)] * keep
        value = branch[...]
        vectors = [column_sum(value), column_sum(value * value)]
        if s == last:
            upstream = gnow[...]
            vectors += [column_sum(upstream * value), column_sum(upstream)]
        exchange_start(s, vectors)
        if s == 0:
            for l in range(1, layers):
                prepare(l)
        hid_t[s] = mm(rowperm[...], hid[s], NT).astype(BF)
        mean, square, *backward = exchange_finish(s, len(vectors))
        scale = lax.rsqrt(square - mean * mean + EPS)
        stats[s : s + 1, :] = scale
        norm = (branch[...] - mean) * scale
        after = hid[s].astype(F32) + gains[s : s + 1] * norm + shifts[s : s + 1]
        for j in range(wide):
            normed[s, :, lanes(j)] = norm[:, lanes(j)] * keep
            hid[s + 1, :, lanes(j)] = (after[:, lanes(j)] * keep).astype(BF)
        if s == last:
            first_cross = scale * (backward[0] - mean * backward[1])
            first_total = backward[1]
            local_cross = scale * (vectors[2] - mean * vectors[3])
            local_sum = vectors[3]

    def small_row(name, l, row, value, at):
        jobs[name, l].stage[row // SUB, row % SUB : row % SUB + 1, at] = value

    def expand_row(l, j, tap, value):
        jobs[MB, l].stage[j // wide * 2 + tap // SUB, tap % SUB : tap % SUB + 1, lanes(j % wide)] = value

    def matrix(name, l, left, right, columns):
        own = jobs[name, l].own
        step = width
        for c in range(columns // step):
            cut = slice(c * step, (c + 1) * step)
            own[:, :, :, cut] = mm(left, right(cut)).astype(BF).reshape(2, n_pipe, piece_rows, step)
        jobs[name, l].start()

    def attention_backward(l, s, grad_branch, pause):
        gmix[...] = mm(grad_branch, proj_ref[l], NT).astype(BF).astype(F32)
        matrix(PROJ, l, grad_t[...], lambda cut: mixo[l, :, cut].astype(BF), mixo.shape[2])
        pause(T_START, s)

        def units(first):
            places = [(first + k, start, size) for k in range(UNIT_STEP) for start, size in BLOCKS]
            inputs = []
            for u, start, size in places:
                rows = slice(start, start + size)
                down = gmix[rows, lanes(u)] * rden[l, rows, lanes(u)]
                inputs.append(
                    [tvals[l, rows, lanes(u + part * UNITS)] for part in range(3)]
                    + [down, -down * mixo[l, rows, lanes(u)]]
                )
            products = []
            for (_, start, size), (query, key, value, down, level) in zip(places, inputs):
                ones = jnp.ones_like(value)
                if start == SMALL:
                    inside = smask[...]
                    query_stack, down_stack = stacked(query), stacked(down)
                    grad_scores = mm(
                        joint(down, level), jnp.concatenate([stacked(value), stacked(ones)], axis=1), NT
                    )
                    grad_scores_t = mm(
                        joint(value, ones), jnp.concatenate([down_stack, stacked(level)], axis=1), NT
                    )
                    scores_t = mm(key.astype(BF), query_stack, NT)
                    products.append((
                        (grad_scores * inside, stacked(key)),
                        (grad_scores_t * inside, query_stack),
                        (scores_t * inside, down_stack),
                    ))
                else:
                    both, slopes = joint(value, ones), joint(down, level)
                    state_t = mm(both, key.astype(BF), TN) * diag_t[...]
                    grad_state_t = mm(slopes, query.astype(BF), TN) * diag_t[...]
                    grad_state = mm(query.astype(BF), down.astype(BF), TN) * diag[:, 0:LANE]
                    products.append((
                        (slopes, state_t.astype(BF)), (both, grad_state_t.astype(BF)), (key, grad_state.astype(BF))
                    ))
            results = []
            for (query, key, *_), pairs in zip(inputs, products):
                grad_query, grad_key, grad_value = (mm(left.astype(BF), right) for left, right in pairs)
                results.append(
                    (grad_query * (1.0 - jnp.exp(-query)), grad_key * (1.0 - jnp.exp(-key)), grad_value)
                )
            for (u, start, size), grads in zip(places, results):
                for part, grad in enumerate(grads):
                    dvals[start : start + size, lanes(u + part * UNITS)] = grad

        groups(UNITS, UNIT_STEP, units)
        pause(T_UNITS, s)

        def chunks(c):
            keep = rmask[...]
            columns = [lanes(part * wide + c) for part in range(3)]
            slots = [part * UNITS + c for part in range(3)]
            grads = [dvals[:, lanes(slot + wide)].astype(BF) for slot in slots]
            direct = [dvals[:, lanes(slot)] for slot in slots]
            cells = [joined[l, :, at].reshape(20, SUB, LANE) for at in columns]
            convs = [
                mm(grad, blocks_bd[l, part * wide + c], NT).reshape(20, SUB, LANE) for part, grad in enumerate(grads)
            ]
            blocks = [mm(s0[l, :, at], grad, TN) * diag[:, 0:LANE] for at, grad in zip(columns, grads)]
            taps_of, grads_of = [], []
            for part, conv in enumerate(convs):
                back = depthwise(conv, dwp[l, :, columns[part]], 5, flip=True).reshape(ROWS, LANE)
                taps_of.append(depthwise_taps(cells[part], conv, 5))
                grads_of.append((direct[part] + back * keep).astype(BF))
            for at, block, taps, joined_grad in zip(columns, blocks, taps_of, grads_of):
                block = block[0:32] + block[32:64] + block[64:96] + block[96:128]
                jobs[ATT, l].stage[4:8, :, at] = block.reshape(4, SUB, LANE)
                for tap, row in enumerate(taps):
                    small_row(ATT, l, tap, row, at)
                mid[:, at] = joined_grad
            natural = mm(jnp.concatenate(grads_of, axis=1), perm[...], NT).astype(BF)
            matrix(QKV + c, l, hid_t[s], lambda cut: natural, width)
            pause(T_CHUNKS + c, s)

        groups(wide, 1, chunks, True)
        jobs[ATT, l].start()
        grad_hidden = mm(mid[:, : 3 * width], wp[l], NT)

        return grad_hidden

    def expand_backward(l, s, grad_branch, pause):
        gact[:, 0:expanded] = mm(grad_branch, point_ref[l], NT).astype(BF).astype(F32)
        matrix(POINT, l, grad_t[...], lambda cut: act[l, :, cut], expanded)
        pause(M_START, s)

        def chunk(j):
            at = lanes(j)
            grad_conv = gact[:, at] * act_d[l, :, at].astype(F32)
            expand_row(l, j, 9, column_sum(grad_conv))
            cells = pre_u[l, :, at].reshape(20, SUB, LANE)
            grad_conv = grad_conv.reshape(20, SUB, LANE)
            for tap, row in enumerate(depthwise_taps(cells, grad_conv, 3)):
                expand_row(l, j, tap, row)
            back = depthwise(grad_conv, mdwp[l, :, at], 3, flip=True).reshape(ROWS, LANE)
            grad_pre = (back * pre_d[l, :, at].astype(F32)).astype(BF)
            mid[:, at] = grad_pre
            expand_row(l, j, 10, column_sum(grad_pre.astype(F32)))

        loop(expanded // LANE, EXPAND_STEP, chunk)
        matrix(INV, l, hid_t[s], lambda cut: mid[:, cut], expanded)
        jobs[MB, l].start()
        pause(M_CHUNKS, s)
        return mm(mid[...], inv_ref[l], NT)

    def pause(moment, s):
        for job, l, step in PLAN.get((moment, s), ()):
            jobs[job, l].do(step)

    for s in range(stages - 1, -1, -1):
        l = s // 2
        keep = rmask[...]
        if s == last:
            cross, total = first_cross, first_total
        else:
            cross, total = exchange_finish(stages + s, 2)
        pause(BEGIN, s)
        if s % 2 == 0:
            small_row(ATT, l, 25, local_cross, slice(0, width))
            small_row(ATT, l, 25, local_sum, slice(width, 2 * width))
        else:
            small_row(MB, l, 11, local_cross, slice(0, width))
            small_row(MB, l, 16 + 11, local_sum, slice(0, width))
        grad_branch = (stats[s : s + 1, :] * gains[s : s + 1]) * (gnow[...] - total - normed[s] * cross)
        grad_branch = jnp.concatenate(
            [grad_branch[:, lanes(j)] * keep for j in range(wide)], axis=1
        ).astype(BF)
        grad_t[...] = mm(rowperm[...], grad_branch, NT).astype(BF)
        back = attention_backward if s % 2 == 0 else expand_backward
        grad_hidden = back(l, s, grad_branch, pause)
        after = (gnow[...] + grad_hidden).astype(BF).astype(F32)
        gnow[...] = after
        if s > 0:
            local_cross, local_sum = column_sum(after * normed[s - 1]), column_sum(after)
            exchange_start(stages + s - 1, [local_cross, local_sum])
        pause(SENT, s)
        pause(DONE, s)
        if s == last:
            at.out_x[...] = mm(spread, hid[stages], TN).astype(BF)

    at.out_g[...] = mm(spread, gnow[...].astype(BF), TN).astype(BF)
    for job in jobs.values():
        if isinstance(job, Reduction):
            job.drain()
    for e in range(2 * stages - 1):
        rows = slot_rows(4 if e == last else 2)
        wait_bytes(exbuf.at[e, 0 : n_dp - 1, 0:rows], send_sem.at[e])


def unsplit(value, wide):
    lane = iota((1, LANE), 1) >> 5
    columns = []
    for c in range(wide):
        parts = [value[:, lanes(part * wide + c)] for part in range(3)]
        for k in range(3):
            column = None
            for slot in range(4):
                index = 4 * k + slot
                moved = pltpu.roll(parts[index % 3], (slot - index // 3) % 4 * 32, 1)
                column = moved if column is None else jnp.where(lane == slot, moved, column)
            columns.append(column)
    return columns


def arrange(layers, wide, shares, x_in, g_in, attcols_in, mbcols_in, att_in, mb_in,
            x_out, g_out, qkv_out, proj_out, inv_out, point_out, dw_out, group_out, ibias_out, mdw_out, mbias_out,
            gain_out, shift_out):
    width = wide * LANE
    share_qkv, share_proj, share_inv, share_point = shares
    x_out[...] = x_in[...]
    g_out[...] = g_in[...]
    taps, mtaps = dw_out.shape[0], mdw_out.shape[0]
    for l in range(layers):
        rows = attcols_in.shape[1]
        values = []
        for value, share in ((attcols_in[l], share_qkv), (mbcols_in[l], share_inv)):
            value = jnp.concatenate([value, jnp.zeros((padded(rows) - rows, value.shape[1]), F32)], axis=0)
            values += [value, pltpu.roll(value, value.shape[1] - share, 1)]
        qkv_out[l] = jnp.transpose(values[0])[0:share_qkv, 0:rows]
        proj_out[l] = jnp.transpose(values[1])[0:share_proj, 0:rows]
        inv_out[l] = values[2][0:rows, 0:share_inv]
        point_out[l] = jnp.transpose(values[3])[0:share_point, 0:rows]
        natural = unsplit(att_in[l], wide)
        for j, column in enumerate(natural):
            for t in range(taps):
                dw_out[t, l : l + 1, lanes(j)] = column[t : t + 1]
            group_out[l, :, lanes(j)] = column[32:64]
        for block in range(4):
            cut = slice(block * width, (block + 1) * width)
            rows = mb_in[l, 16 * block : 16 * block + 16]
            for t in range(mtaps):
                mdw_out[t, l : l + 1, cut] = rows[t : t + 1]
            mbias_out[l : l + 1, cut] = rows[9:10]
            ibias_out[l : l + 1, cut] = rows[10:11]
        gain_out[2 * l : 2 * l + 1, :] = att_in[l, 25:26, 0:width]
        shift_out[2 * l : 2 * l + 1, :] = att_in[l, 25:26, width : 2 * width]
        gain_out[2 * l + 1 : 2 * l + 2, :] = mb_in[l, 11:12, :]
        shift_out[2 * l + 1 : 2 * l + 2, :] = mb_in[l, 27:28, :]


def padded(columns):
    return -(-columns // LANE) * LANE


def body(
    activations, cotangent, att_qkv, att_dw, att_group, att_proj, mb_inv, mb_inv_bias, mb_dw, mb_dw_bias, mb_point,
    bn_gain, bn_bias,
):
    n_dp, n_pipe = lax.axis_size("dp"), lax.axis_size("pipe")
    layers, width, joined_width = att_qkv.shape
    mixed_width = att_proj.shape[1]
    expanded = mb_inv.shape[2]
    tokens = activations.shape[2]
    stages = 2 * layers
    rows = width // 2 // n_pipe
    vmem = pl.BlockSpec(memory_space=pltpu.VMEM)
    hbm = pl.BlockSpec(memory_space=pl.ANY)
    columns = (width, width, width, mixed_width, expanded, expanded, joined_width, width)
    shares = tuple(n // n_dp for n in (joined_width, mixed_width, expanded, expanded))
    share_att, share_mb = padded(shares[0] + shares[1]), padded(shares[2] + shares[3])
    outs = dict(
        out_x=jax.ShapeDtypeStruct((tokens, width), BF),
        out_g=jax.ShapeDtypeStruct((tokens, width), BF),
        out_attcols=jax.ShapeDtypeStruct((layers, 2 * rows, share_att), F32),
        out_mbcols=jax.ShapeDtypeStruct((layers, 2 * rows, share_mb), F32),
        out_att=jax.ShapeDtypeStruct((layers, 8 * SUB, joined_width), F32),
        out_mb=jax.ShapeDtypeStruct((layers, 8 * SUB, width), F32),
    )
    scratch = dict(
        proj=pltpu.VMEM(att_proj.shape, BF),
        inv=pltpu.VMEM(mb_inv.shape, BF),
        point=pltpu.VMEM(mb_point.shape, BF),
        perm=pltpu.VMEM((width, width), BF),
        rowperm=pltpu.VMEM((width, width), BF),
        wp=pltpu.VMEM((layers, width, joined_width), BF),
        blocks_bd=pltpu.VMEM((layers, joined_width // LANE, LANE, LANE), BF),
        dwp=pltpu.VMEM((layers, 32, joined_width), F32),
        mdwp=pltpu.VMEM((layers, 16, expanded), F32),
        rmask=pltpu.VMEM((ROWS, LANE), F32),
        smask=pltpu.VMEM((48, 192), F32),
        diag=pltpu.VMEM((LANE, 2 * LANE), F32),
        diag_t=pltpu.VMEM((2 * LANE, LANE), F32),
        hid=pltpu.VMEM((stages + 1, ROWS, width), BF),
        hid_t=pltpu.VMEM((stages, width, ROWS), BF),
        grad_t=pltpu.VMEM((width, ROWS), BF),
        normed=pltpu.VMEM((stages, ROWS, width), F32),
        mixo=pltpu.VMEM((layers, ROWS, mixed_width), F32),
        rden=pltpu.VMEM((layers, ROWS, mixed_width), F32),
        tvals=pltpu.VMEM((layers, ROWS, 3 * mixed_width), F32),
        joined=pltpu.VMEM((layers, ROWS, joined_width), F32),
        s0=pltpu.VMEM((layers, ROWS, joined_width), BF),
        dvals=pltpu.VMEM((ROWS, 3 * mixed_width), F32),
        gmix=pltpu.VMEM((ROWS, mixed_width), F32),
        pre_u=pltpu.VMEM((layers, ROWS, expanded), F32),
        pre_d=pltpu.VMEM((layers, ROWS, expanded), BF),
        act=pltpu.VMEM((layers, ROWS, expanded), BF),
        act_d=pltpu.VMEM((layers, ROWS, expanded), BF),
        mid=pltpu.VMEM((ROWS, expanded), BF),
        branch=pltpu.VMEM((ROWS, width), F32),
        gnow=pltpu.VMEM((ROWS, width), F32),
        stats=pltpu.VMEM((8, width), F32),
        exbuf=pltpu.VMEM((2 * stages - 1, n_dp, 2 * SUB, LANE), F32),
        whole=pltpu.VMEM((rows, 2 * expanded), F32),
        send_sem=pltpu.SemaphoreType.DMA((2 * stages - 1,)),
        recv_sem=pltpu.SemaphoreType.DMA((2 * stages - 1,)),
        load_sem=pltpu.SemaphoreType.DMA((4, layers)),
        red_send=pltpu.SemaphoreType.DMA((KINDS * JOBS * layers + 2 * layers,)),
        red_recv=pltpu.SemaphoreType.DMA((KINDS * JOBS * layers + 2 * layers,)),
    )
    for job, n in enumerate(columns):
        high, kind = rows, BF
        if job == ATT:
            n, high = padded(n // 2), 2 * SUB
        elif job == MB:
            high, kind = SUB, F32
        shapes = [(2, n_pipe), (n_pipe,), (2,), ()]
        if job >= MATRICES:
            shapes += [(n_dp // 2,), (2 * n_pipe,)]
            scratch[job, 6] = pltpu.VMEM((8, SUB, columns[job]), F32)
        for i, shape in enumerate(shapes):
            scratch[job, i] = pltpu.VMEM((layers, *shape, high, n), kind)
    for job, share in ((ATT_COLUMNS, share_att), (MB_COLUMNS, share_mb)):
        scratch[job, 0] = pltpu.VMEM((n_dp, rows, share), BF)
        scratch[job, 1] = pltpu.VMEM((layers, n_dp, rows, share), BF)
    results = pl.pallas_call(
        functools.partial(kernel, n_dp, n_pipe, 13, tuple(outs) + tuple(scratch)),
        out_shape=tuple(outs.values()),
        in_specs=[vmem, vmem, hbm, vmem, vmem, hbm, hbm, vmem, vmem, vmem, hbm, vmem, vmem],
        out_specs=(vmem,) * len(outs),
        scratch_shapes=list(scratch.values()),
        compiler_params=pltpu.CompilerParams(
            collective_id=0, has_side_effects=True, vmem_limit_bytes=63 * 1024 * 1024
        ),
    )(
        activations.reshape(tokens, width),
        cotangent.reshape(tokens, width),
        att_qkv,
        att_dw.transpose(1, 0, 2),
        att_group,
        att_proj,
        mb_inv,
        mb_inv_bias,
        mb_dw.transpose(1, 0, 2),
        mb_dw_bias,
        mb_point,
        bn_gain,
        bn_bias,
    )
    taps, mtaps = att_dw.shape[1], mb_dw.shape[1]
    arranged = pl.pallas_call(
        functools.partial(arrange, layers, width // LANE, shares),
        out_shape=(
            jax.ShapeDtypeStruct((tokens, width), BF),
            jax.ShapeDtypeStruct((tokens, width), BF),
            jax.ShapeDtypeStruct((layers, shares[0], 2 * rows), F32),
            jax.ShapeDtypeStruct((layers, shares[1], 2 * rows), F32),
            jax.ShapeDtypeStruct((layers, 2 * rows, shares[2]), F32),
            jax.ShapeDtypeStruct((layers, shares[3], 2 * rows), F32),
            jax.ShapeDtypeStruct((taps, layers, joined_width), F32),
            jax.ShapeDtypeStruct((layers, 32, joined_width), F32),
            jax.ShapeDtypeStruct((layers, expanded), F32),
            jax.ShapeDtypeStruct((mtaps, layers, expanded), F32),
            jax.ShapeDtypeStruct((layers, expanded), F32),
            jax.ShapeDtypeStruct((stages, width), F32),
            jax.ShapeDtypeStruct((stages, width), F32),
        ),
        in_specs=[vmem] * 6,
        out_specs=(vmem,) * 13,
    )(*results)
    x_out, g_out, qkv, proj, inv, point, dw, group, ibias, mdw, mbias, gain, shift = arranged
    groups, size = att_group.shape[1], att_group.shape[2]
    return (
        x_out.reshape(activations.shape),
        g_out.reshape(activations.shape),
        qkv.transpose(0, 2, 1),
        dw.transpose(1, 0, 2),
        group.reshape(layers, size, groups, size).transpose(0, 2, 1, 3),
        proj,
        inv,
        ibias,
        mdw.transpose(1, 0, 2),
        mbias,
        point,
        gain,
        shift,
    )


def solution(mesh):
    placed = (P("pipe", "dp", None, None), P("pipe", "dp", None, None)) + (P(),) * 11
    return jax.shard_map(
        body,
        mesh=mesh,
        in_specs=placed,
        out_specs=(
            P("pipe", "dp", None, None),
            P("pipe", "dp", None, None),
            P(None, "pipe", "dp"),
            P(),
            P(),
            P(None, "dp", "pipe"),
            P(None, "pipe", "dp"),
            P(),
            P(),
            P(),
            P(None, "dp", "pipe"),
            P(),
            P(),
        ),
        check_vma=False,
    )
```
